32 devices in a mesh: groups: 2 (over x), seq: 16 (over z, y, core).
Axes of the slice: x: 2, y: 2, z: 4, core: 2. Of those that a mesh axis runs over, the one named last changes fastest.
Arguments:
- x_rows: bfloat16 [4096, 4096], P(('groups', 'seq')), parts along dimension 0, may hold values from -6 to 6
- bc_rows: bfloat16 [4096, 256], P(('groups', 'seq')), parts along dimension 0, may hold values from -6 to 6
- step: bfloat16 [4096, 64], P(('groups', 'seq')), parts along dimension 0, may hold values from 1e-06 to 0.3, as said below
- route: int32 [4096, 1], P(('groups', 'seq')), parts along dimension 0, may hold values from 0 to 15; in each aligned block of 128 rows (0 to 127, 128 to 255, ...) at most 12 rows name the same one
- doc_lengths: int32 [16], P('groups'), parts along dimension 0, may hold values from 1 to 1024, 2048 in all
- conv_weight: float32 [4, 4352], replicated, may hold values from -3 to 3
- conv_bias: float32 [4352], replicated, may hold values from -1.2 to 1.2
- rate: float32 [64], replicated, may hold values from 0.5 to 2
- skip: float32 [64], replicated, may hold values from 0.5 to 1.5
- clip_level: float32 [64], replicated, may hold values from 0.3 to 2
Outputs:
- layer_out: bfloat16 [4096, 4096], P(('groups', 'seq')), parts along dimension 0
The draws below stay inside these ranges and needn't reach their ends.
There are 2 independent parts, one for each index of `groups`. The reference program is written for one: setup_inputs(seed, part) draws one part's arguments, and reference() takes and returns one part's arrays. A program takes and returns all parts, laid end to end along the dimension named above; an argument that names none is the same for every part. Nothing has to cross between parts.
Inputs may be any that keep to these rules, and one draw needn't show every extreme that they name: `step`: Positive. `route`: at most 12 of the rows of one device name the same shard; on some device some shard is named exactly 12 times; every shard is named by some row. `doc_lengths`: the lengths sum to 2048; the largest is exactly half of 2048.
All inputs are finite; a program needn't handle non-finite values.
Results may differ from the reference program's by a relative error of at most 0.0038.
Values may be sent and summed in bfloat16 or wider, within the bound.
A program may use at most 320 MiB of HBM per device.

```python
import math
import jax
import jax.numpy as jnp
import numpy as np
from jax import lax

HEADS = 64
HEAD_DIM = 64
STATE = 128
CONV = 4
DOCS = 8
TOK_DEV = 128
PACKED_TOKENS = 2048
PAIR = 12
SLOTS = 192
WIDE = 4352
N_SEQ = 16


def draw_step(key, part):
    random_key_variety, random_key_quick, random_key_gentle, random_key_row, random_key_device, random_key_cluster, random_key_extent = jax.random.split(jax.random.fold_in(key, 17), 7)
    fast_share = 0.5
    fast_heads = jax.random.uniform(random_key_variety, (HEADS,), jnp.float32) < fast_share
    fast_base = jnp.exp(jax.random.uniform(random_key_quick, (HEADS,), jnp.float32, jnp.log(0.003), jnp.log(0.03)))
    slow_lo = jnp.log(0.8 / PACKED_TOKENS)
    slow_hi = jnp.log(3.0 / PACKED_TOKENS)
    slow_base = jnp.exp(jax.random.uniform(random_key_gentle, (HEADS,), jnp.float32, slow_lo, slow_hi))
    base_step = jnp.where(fast_heads, fast_base, slow_base)
    row_factor = jnp.exp(jax.random.uniform(random_key_row, (PACKED_TOKENS, HEADS), jnp.float32, -0.69, 0.69))
    device_count = PACKED_TOKENS // TOK_DEV
    device_factor = jnp.exp(jax.random.uniform(random_key_device, (device_count, 1, 1), jnp.float32, -0.69, 0.69))
    drawn_rows = (base_step[None, :] * row_factor).reshape(device_count, TOK_DEV, HEADS) * device_factor
    drawn_rows = jnp.minimum(jnp.maximum(drawn_rows.reshape(PACKED_TOKENS, HEADS), 2e-06), 0.29)
    cluster_rows = jax.random.randint(random_key_cluster, (6,), 0, PACKED_TOKENS)
    row_numbers = jnp.arange(PACKED_TOKENS, dtype=jnp.int32)
    flag_cluster = jnp.any(row_numbers[:, None] == cluster_rows[None, :], axis=1)
    cluster_size = jax.random.uniform(random_key_extent, (PACKED_TOKENS, 1), jnp.float32, 0.2, 0.3)
    value_entries = jnp.where(flag_cluster[:, None], cluster_size, drawn_rows)
    return value_entries.astype(jnp.bfloat16)


def steps_of(rng, shape, shards, low, top_value):
    def one(axis_at, shards_of):
        steps = jax.random.uniform(jax.random.fold_in(jax.random.fold_in(rng, 6), axis_at), (shards_of,), jnp.float32, low / len(shards), top_value / len(shards))
        return jnp.repeat(jnp.exp(steps), shape[axis_at] // shards_of).reshape((-1,) + (1,) * (len(shape) - axis_at - 1))

    factor_of = one(*shards[0])
    for cut in shards[1:]:
        factor_of = factor_of * one(*cut)
    return factor_of


def profile(amount, total, limit, slope):
    weights = [(1 << 20) // math.isqrt(rank ** slope) + 1 for rank in range(2, amount + 1)]
    rest, holding = total - limit - (amount - 1), [1] * (amount - 1)
    while rest > 0:
        movable = [i for i in range(amount - 1) if holding[i] < limit]
        pool, left = sum([weights[i] for i in movable]), rest
        for i in movable:
            extra = min(limit - holding[i], max(1, left * weights[i] // pool), rest)
            holding[i] = holding[i] + extra
            rest = rest - extra
    return np.array([limit] + holding)


def ragged(stream_key, amount, total, limit, slope):
    if amount == 2:
        one = jax.random.randint(stream_key, (), max(1, total - limit), min(limit, total - 1) + 1)
        return jnp.stack([one, total - one])
    sizes = jnp.asarray(profile(amount, total, limit, slope), jnp.int32)
    couples = (amount - 1) // 2
    giver, sink = sizes[1:1 + 2 * couples:2], sizes[2:2 + 2 * couples:2]
    slack = jnp.minimum(giver - 1, limit - sink)
    moved = jax.random.randint(jax.random.fold_in(stream_key, 1), (couples,), 0, 1 << 20) % (slack + 1)
    sizes = sizes.at[1:1 + 2 * couples:2].set(giver - moved).at[2:2 + 2 * couples:2].set(sink + moved)
    return sizes[jax.random.permutation(jax.random.fold_in(stream_key, 2), amount)]


def routed_block(rng, own, number, rows, number_of, top, most, skew):
    sequence = jax.random.permutation(rng, number_of)
    crowded, ordinary = load_shares(number_of, rows * top, most, skew, True), load_shares(number_of, rows * top, most, skew, False)
    places = jnp.arange(number_of)

    def named(lengths, turn):
        used = int((lengths > 0).sum())
        fixed = max(1, used // 4)
        shifted = fixed + (places - fixed + turn * (used - fixed)) % max(1, number_of - fixed)
        return jnp.zeros((number_of,), jnp.int32).at[sequence[jnp.where(places < fixed, places, shifted)]].set(jnp.asarray(lengths, jnp.int32))

    lengths = jnp.where(number % 4 == 0, named(crowded, number // 4), named(ordinary, number - number // 4 - 1))
    mixed = jax.random.permutation(jax.random.fold_in(own, 3), number_of)
    donor, taker = mixed[0:number_of // 2 * 2:2], mixed[1:number_of // 2 * 2:2]
    margin = jnp.minimum(lengths[donor] - 1, most - lengths[taker]) // 2
    margin = jnp.where((donor == sequence[0]) | (taker == sequence[0]) | (lengths[taker] == 0), 0, jnp.maximum(margin, 0))
    shifted = jax.random.randint(jax.random.fold_in(own, 4), (number_of // 2,), 0, 1 << 20) % (margin + 1)
    lengths = lengths.at[donor].add(-shifted).at[taker].add(shifted)
    labels = jnp.searchsorted(jnp.cumsum(lengths), jnp.arange(rows * top), side="right").astype(jnp.int32)
    grid = labels.reshape(top, rows).T
    grid = grid[jax.random.permutation(jax.random.fold_in(own, 1), rows)]
    turn = jax.random.randint(jax.random.fold_in(own, 2), (rows, 1), 0, top)
    return jnp.take_along_axis(grid, (jnp.arange(top)[None, :] + turn) % top, axis=1)


def load_shares(number_of, total, bound, slope, full):
    portions = [(1 << 20) // math.isqrt(standing ** slope) + 1 for standing in range(1, number_of + 1)]
    largest = bound if full else min(bound, max(-(-total // number_of), total * portions[0] // sum(portions)))
    least = 1 if total - largest >= number_of - 1 else 0
    holding, rest = [largest] + [least] * (number_of - 1), total - largest - least * (number_of - 1)
    while rest > 0:
        movable = [i for i in range(1, number_of) if holding[i] < largest] or [i for i in range(1, number_of) if holding[i] < bound]
        mass, left = sum([portions[i] for i in movable]), rest
        for i in movable:
            more = min(bound - holding[i], max(1, left * portions[i] // mass), rest)
            holding[i] = holding[i] + more
            rest = rest - more
    return np.array(holding)


def normal_values(own_key, dims, width, reach, pieces=(), kind=jnp.bfloat16):
    array = width * jax.random.normal(own_key, dims, jnp.float32)
    if pieces:
        array = array * steps_of(own_key, dims, pieces, -0.22, 0.18)
    return jnp.clip(array, -reach, reach).astype(kind)


def setup_inputs(seed: int = 0, part: int = 0) -> dict:
    key_list = jax.random.split(jax.random.key(seed), 11)
    part_keys = jax.random.split(jax.random.fold_in(key_list[10], part), 11)
    x_rows = normal_values(part_keys[0], (PACKED_TOKENS, HEADS * HEAD_DIM), 1.0, 6.0, ((0, 16),))
    bc_rows = normal_values(part_keys[1], (PACKED_TOKENS, 2 * STATE), 1.0, 6.0, ((0, 16),))
    step = draw_step(jax.random.fold_in(jax.random.fold_in(key_list[10], part), 71), part)
    route_keys = jax.random.split(jax.random.fold_in(part_keys[3], 1), PACKED_TOKENS // TOK_DEV)
    route_turns = jax.random.permutation(jax.random.fold_in(part_keys[3], 3), PACKED_TOKENS // TOK_DEV)
    route = jax.vmap(lambda own, number: routed_block(jax.random.fold_in(part_keys[3], 2), own, number, TOK_DEV, N_SEQ, 1, PAIR, 2))(route_keys, route_turns).reshape((PACKED_TOKENS, 1))
    doc_lengths = ragged(part_keys[4], DOCS, PACKED_TOKENS, PACKED_TOKENS // 2, 2).astype(jnp.int32)
    conv_weight = normal_values(key_list[5], (CONV, WIDE), CONV ** -0.5, 3.0, (), jnp.float32)
    conv_bias = normal_values(key_list[6], (WIDE,), 0.3, 1.2, (), jnp.float32)
    rate = jnp.clip(jnp.exp(jax.random.uniform(key_list[7], (HEADS,), jnp.float32, math.log(0.5), math.log(2.0))), 0.5, 2.0)
    skip = jnp.clip(jax.random.uniform(key_list[8], (HEADS,), jnp.float32, 0.5, 1.5), 0.5, 1.5)
    clip_level = jnp.clip(jnp.exp(jax.random.uniform(key_list[9], (HEADS,), jnp.float32, math.log(0.3), math.log(2.0))), 0.3, 2.0)
    return dict(x_rows=x_rows, bc_rows=bc_rows, step=step, route=route, doc_lengths=doc_lengths, conv_weight=conv_weight, conv_bias=conv_bias, rate=rate, skip=skip, clip_level=clip_level)


def doc_index(starts, positions):
    return jnp.sum((starts[None, :] <= positions[:, None]).astype(jnp.int32), axis=1) - 1


def rounded(value_entries):
    return lax.optimization_barrier(value_entries.astype(jnp.bfloat16)).astype(jnp.float32)


def reference(x_rows, bc_rows, step, route, doc_lengths, conv_weight, conv_bias, rate, skip, clip_level):
    hp_width = HEADS * HEAD_DIM
    targets = route[:, 0].astype(jnp.int32)
    seq_order = jnp.argsort(targets, stable=True).astype(jnp.int32)
    shard_ids = jnp.arange(N_SEQ, dtype=jnp.int32)
    block_rows = jnp.sum((targets[:, None] == shard_ids[None, :]).astype(jnp.int32), axis=0)
    offsets = (jnp.cumsum(block_rows) - block_rows).astype(jnp.int32)
    starts = (jnp.cumsum(doc_lengths) - doc_lengths).astype(jnp.int32)
    conv_in = jnp.concatenate([x_rows, bc_rows], axis=1)[seq_order]
    dt_seq = step[seq_order].astype(jnp.float32)
    positions = jnp.arange(PACKED_TOKENS, dtype=jnp.int32)
    doc_here = doc_index(starts, positions)
    mixed_sum = conv_bias[None, :] + conv_weight[0][None, :] * conv_in.astype(jnp.float32)
    for lag_steps in range(1, CONV):
        earlier_rows = jnp.concatenate([jnp.zeros((lag_steps, WIDE), conv_in.dtype), conv_in[:-lag_steps]], axis=0)
        same_doc = (doc_index(starts, positions - lag_steps) == doc_here).astype(jnp.float32)
        mixed_sum = mixed_sum + conv_weight[lag_steps][None, :] * earlier_rows.astype(jnp.float32) * same_doc[:, None]
    activated = jax.nn.silu(mixed_sum).astype(jnp.bfloat16)
    act_pad = jnp.concatenate([activated, jnp.zeros((SLOTS, WIDE), jnp.bfloat16)], axis=0)
    dt_pad = jnp.concatenate([dt_seq, jnp.zeros((SLOTS, HEADS), dt_seq.dtype)], axis=0)
    local_ids = jnp.arange(SLOTS, dtype=jnp.int32)
    causal = local_ids[:, None] >= local_ids[None, :]

    def block_step(state, inputs):
        block_first, block_count = inputs
        valid_rows = local_ids < block_count
        rows_here = lax.dynamic_slice_in_dim(act_pad, block_first, SLOTS, 0)
        rows_here = jnp.where(valid_rows[:, None], rows_here, jnp.zeros_like(rows_here))
        dt_here = lax.dynamic_slice_in_dim(dt_pad, block_first, SLOTS, 0)
        dt_here = jnp.where(valid_rows[:, None], dt_here, jnp.zeros_like(dt_here))
        last_pos = block_first + block_count - 1
        slot_pos = block_first + local_ids
        doc_slot = doc_index(starts, jnp.minimum(slot_pos, last_pos))
        doc_before = doc_index(starts, jnp.reshape(block_first - 1, (1,)))[0]
        doc_last = doc_index(starts, jnp.reshape(last_pos, (1,)))[0]
        head_in = rows_here[:, :hp_width].reshape(SLOTS, HEADS, HEAD_DIM).astype(jnp.float32)
        b_mat = rows_here[:, hp_width:hp_width + STATE]
        c_mat = rows_here[:, hp_width + STATE:]
        cums = jnp.cumsum(-dt_here * rate[None, :], axis=0)
        scores = jnp.dot(c_mat, b_mat.T, preferred_element_type=jnp.float32)
        keep_pair = causal & (doc_slot[:, None] == doc_slot[None, :])
        gaps = cums[:, None, :] - cums[None, :, :]
        decays = jnp.where(keep_pair[:, :, None], jnp.exp(jnp.where(keep_pair[:, :, None], gaps, 0.0)), 0.0)
        weights = rounded(scores[:, :, None] * decays * dt_here[None, :, :])
        y_intra = jnp.einsum('tsh,shp->thp', weights, head_in)
        tail_decay = jnp.exp(cums[-1][None, :] - cums) * (doc_slot == doc_last).astype(jnp.float32)[:, None] * dt_here
        b_weighted = rounded(b_mat.astype(jnp.float32)[:, None, :] * tail_decay[:, :, None])
        state_local = jnp.einsum('shn,shp->hnp', b_weighted, head_in)
        carry_here = jnp.exp(cums[-1]) * (doc_before == doc_last).astype(jnp.float32)
        head_decay = jnp.exp(cums) * (doc_slot == doc_before).astype(jnp.float32)[:, None]
        c_weighted = rounded(c_mat.astype(jnp.float32)[:, None, :] * head_decay[:, :, None])
        y_inter = jnp.einsum('thn,hnp->thp', c_weighted, rounded(state))
        total = y_intra + y_inter + skip[None, :, None] * head_in
        limits = clip_level[None, :, None]
        clipped = jnp.clip(total, -limits, limits).astype(jnp.bfloat16).reshape(SLOTS, hp_width)
        new_state = carry_here[:, None, None] * state + state_local
        return new_state, clipped

    start_state = jnp.zeros((HEADS, STATE, HEAD_DIM), jnp.float32)
    _, blocks = lax.scan(block_step, start_state, (offsets, block_rows))
    block_of = jnp.sum((offsets[None, :] <= positions[:, None]).astype(jnp.int32), axis=1) - 1
    flat_ids = block_of * SLOTS + positions - offsets[block_of]
    seq_out = blocks.reshape(N_SEQ * SLOTS, hp_width)[flat_ids]
    return jnp.zeros((PACKED_TOKENS, hp_width), jnp.bfloat16).at[seq_order].set(seq_out)
```

```python
import functools

import jax
import jax.numpy as jnp
from jax import lax
from jax.experimental import pallas as pl
from jax.experimental.pallas import tpu as pltpu
from jax.sharding import PartitionSpec as P

F32 = jnp.float32
BF16 = jnp.bfloat16
CHUNK = 128
LANES = 128
PAD = 8
OUT_SPEC = pl.BlockSpec(memory_space=pl.ANY)


def dot(a, b):
    return jnp.dot(a, b, preferred_element_type=F32)


def dot_nt(a, b):
    return lax.dot_general(a, b, (((1,), (1,)), ((), ())), preferred_element_type=F32)


def dot_tn(a, b):
    return lax.dot_general(a, b, (((0,), (0,)), ((), ())), preferred_element_type=F32)


def find_places(aux_ref, ranks, place_row, place_col, heads):
    rows = ranks.shape[0]
    state2 = aux_ref.shape[2] - LANES
    low = lax.broadcasted_iota(jnp.int32, (LANES, LANES), 0)
    high = lax.broadcasted_iota(jnp.int32, (LANES, LANES), 1)
    earlier = jnp.where(low > high, 1.0, 0.0).astype(BF16)
    before = jnp.where(low < high, 1.0, 0.0).astype(BF16)
    shard = high.astype(F32)
    step = 4

    def named(b):
        target = aux_ref[b, :, state2 : state2 + LANES].astype(F32)[:, heads : heads + 1]
        return jnp.where(target == shard, 1.0, 0.0)

    def count(i, total):
        for j in range(step):
            b = i * step + j
            onehot = named(b)
            ranks[pl.ds(pl.multiple_of(b * LANES, LANES), LANES), :] = dot(earlier, onehot.astype(BF16)) + total
            total = total + jnp.sum(onehot, axis=0, keepdims=True)
        return total

    total = lax.fori_loop(0, rows // LANES // step, count, jnp.zeros((1, LANES), F32))
    total = jnp.broadcast_to(total, (8, LANES))
    coarse = jnp.floor(total * (1.0 / 64.0))
    fine = total - coarse * 64.0
    start = (dot(coarse.astype(BF16), before) * 64.0 + dot(fine.astype(BF16), before))[0:1, :]

    def rank(i, _):
        for j in range(step):
            b = i * step + j
            at = pl.multiple_of(b * LANES, LANES)
            found = named(b) * (ranks[pl.ds(at, LANES), :] + start)
            place = jnp.broadcast_to(jnp.sum(found, axis=1, keepdims=True), (LANES, LANES))
            place_col[pl.ds(at, LANES), :] = place
            place_row[:, pl.ds(at, LANES)] = place.T[0:8, :]
        return 0

    lax.fori_loop(0, rows // LANES // step, rank, 0)


def one_hot_sort(place_row, first, size):
    rows = place_row.shape[1]
    number = lax.broadcasted_iota(jnp.int32, (size, rows), 0).astype(F32)
    hit = place_row[0:1, :] - lax.convert_element_type(first, F32) == number
    return jnp.where(hit, 1.0, 0.0).astype(BF16)


def one_hot_unsort(place_col, first, size):
    rows = place_col.shape[0]
    number = lax.broadcasted_iota(jnp.int32, (size, rows), 1).astype(F32)
    place = place_col[pl.ds(first, size), :]
    hit = jnp.concatenate([place] * (rows // LANES), axis=1) == number
    return jnp.where(hit, 1.0, 0.0).astype(BF16)


def doc_begins(at, starts):
    begin = jnp.zeros((CHUNK, 1), jnp.int32)
    for start in starts:
        begin = jnp.where(at >= start, start, begin)
    return begin


def conv_silu(v, par, at, begin):
    acc = par[4:5, :] + par[0:1, :] * v[PAD:, :]
    for j in range(1, 4):
        keep = jnp.where(at - j >= begin, 1.0, 0.0)
        acc = acc + par[j : j + 1, :] * (v[PAD - j : PAD - j + CHUNK, :] * keep)
    return (acc / (1.0 + jnp.exp(-acc))).astype(BF16)


def shared_chunk(c, starts, ub, ds, bcpar_ref, rate_ref, bcs, ws, ent, tails, carries, owned):
    width = ent.shape[1]
    state_width = bcs.shape[1] // 2
    base = pl.multiple_of(c * CHUNK, CHUNK)
    at = lax.broadcasted_iota(jnp.int32, (CHUNK, 1), 0) + base
    begin = doc_begins(at, starts)
    begin_last = begin[CHUNK - 1 :, :]
    act = conv_silu(ub[pl.ds(base, CHUNK + PAD), :], bcpar_ref[...], at, begin)
    bcs[pl.ds(base, CHUNK), :] = act
    b_mat, c_mat = act[:, :state_width], act[:, state_width:]

    dt = ds[pl.ds(base, CHUNK), :]
    low = lax.broadcasted_iota(jnp.int32, (CHUNK, CHUNK), 0)
    high = lax.broadcasted_iota(jnp.int32, (CHUNK, CHUNK), 1)
    tri = jnp.where(low >= high, 1.0, 0.0).astype(BF16)
    cum = -dot(tri, dt.astype(BF16)) * rate_ref[...]
    shifted = (cum - jnp.log(jnp.maximum(dt, 1e-30))).T
    cum_last = cum[CHUNK - 1 :, :]
    scores = dot_nt(c_mat, b_mat)
    scores = jnp.where((low >= high) & (high + base >= begin), scores, 0.0)
    head = lax.broadcasted_iota(jnp.int32, (1, width), 1) // (width // owned)

    def expand(e):
        out = jnp.broadcast_to(e[:, 0:1], (e.shape[0], width))
        for h in range(1, owned):
            out = jnp.where(head == h, e[:, h : h + 1], out)
        return out

    for h in range(owned):
        decay = jnp.exp(cum[:, h : h + 1] - shifted[h : h + 1, :])
        ws[h, pl.ds(base, CHUNK), :] = (scores * decay).astype(BF16)
    ent[pl.ds(base, CHUNK), :] = expand(jnp.exp(cum) * jnp.where(begin < base, 1.0, 0.0))
    tail = jnp.exp(cum_last - cum) * dt * jnp.where(at >= begin_last, 1.0, 0.0)
    tails[pl.ds(base, CHUNK), :] = expand(tail)
    carry = expand(jnp.exp(cum_last) * jnp.where(begin_last < base, 1.0, 0.0))
    carries[c] = jnp.broadcast_to(carry, (8, width))


def scan_chunk(c, part, parts, starts, ux, xpar_ref, bcs, ws, ent, tails, carries, state, ys, owned):
    size = ux.shape[1]
    lanes = slice(part * size, (part + 1) * size)
    state_width = bcs.shape[1] // 2
    base = pl.multiple_of(c * CHUNK, CHUNK)
    at = lax.broadcasted_iota(jnp.int32, (CHUNK, 1), 0) + base
    begin = doc_begins(at, starts)
    x_mat = conv_silu(ux[pl.ds(base, CHUNK + PAD), :], xpar_ref[:, lanes], at, begin)
    x_wide = x_mat.astype(F32)
    bc = bcs[pl.ds(base, CHUNK), :]
    b_mat, c_mat = bc[:, :state_width], bc[:, state_width:]
    local = owned // parts
    head = lax.broadcasted_iota(jnp.int32, (1, size), 1) // (size // local)
    y = xpar_ref[5:6, lanes] * x_wide
    for h in range(local):
        mine = jnp.where(head == h, x_wide, 0.0).astype(BF16)
        y = y + dot(ws[part * local + h, pl.ds(base, CHUNK), :], mine)
    y = y + dot(c_mat, state[...].astype(BF16)) * ent[pl.ds(base, CHUNK), lanes]
    limit = xpar_ref[6:7, lanes]
    ys[pl.ds(base, CHUNK), :] = jnp.clip(y, -limit, limit).astype(BF16)
    scaled = (x_wide * tails[pl.ds(base, CHUNK), lanes]).astype(BF16)
    state[...] = carries[c][0:1, lanes] * state[...] + dot_tn(b_mat, scaled)


def kernel(
    owned, heads, parts, plane, docs_ref, rates, skips, clips, x_ref, aux_ref, weight_ref, bias_ref, out_ref,
    xpar_ref, bcpar_ref, rate_ref, pick_ref, aux_all, x_all, sent, keys, place_row, place_col, ub, ux, ds, bcs, ws, ent, tails, carries, ys, state,
    sorter, unsorter, gate_send, gate_recv, plane_send, x_send, x_recv, out_send, out_recv,
):
    n, tok = x_all.shape[1:3]
    rows, size = ys.shape
    state2 = bcs.shape[1]
    flat = len(x_ref.shape) == 2
    block = max(tok, min(512, (1 << 20) // rows))
    keep = sorter.shape[0] == rows
    me = lax.axis_index("seq")
    inside = lax.rem(me, plane)

    def remote(source, target, send, recv, peer):
        return pltpu.make_async_remote_copy(
            src_ref=source, dst_ref=target, send_sem=send, recv_sem=recv,
            device_id={"seq": peer}, device_id_type=pl.DeviceIdType.MESH,
        )

    def every(count, do, first=0):
        def turn(k, _):
            do(k)
            return 0

        lax.fori_loop(first, count, turn, 0)

    def tile(ref, part, owner):
        if flat:
            return ref.at[:, pl.ds(pl.multiple_of((owner * parts + part) * size, size), size)]
        return ref.at[owner]

    def own_lanes(ref):
        width = size * parts
        if width % LANES == 0:
            return ref[:, pl.ds(pl.multiple_of(me * width, LANES), width)]
        per = LANES // width
        wide = ref[:, pl.ds(pl.multiple_of(me // per * LANES, LANES), LANES)]
        picked = wide[:, :width]
        for i in range(1, per):
            picked = jnp.where(lax.rem(me, per) == i, wide[:, i * width : (i + 1) * width], picked)
        return picked

    def load_params():
        width = size * parts
        head = lax.broadcasted_iota(jnp.int32, (1, width), 1) // (width // owned)
        lane = lax.broadcasted_iota(jnp.int32, (1, LANES), 1)
        gain = level = jnp.zeros((1, width), F32)
        decay = jnp.zeros((1, LANES), F32)
        for h in range(owned):
            gain = jnp.where(head == h, skips[me * owned + h], gain)
            level = jnp.where(head == h, clips[me * owned + h], level)
            decay = jnp.where(lane == h, rates[me * owned + h], decay)
        xpar_ref[0:4, :] = own_lanes(weight_ref)
        xpar_ref[4:5, :] = own_lanes(bias_ref)
        xpar_ref[5:6, :] = gain
        xpar_ref[6:7, :] = level
        first = weight_ref.shape[1] - state2
        bcpar_ref[0:4, :] = weight_ref[:, first:]
        bcpar_ref[4:5, :] = bias_ref[:, first:]
        rate_ref[...] = decay
        source = lax.broadcasted_iota(jnp.int32, (LANES, LANES), 0)
        target = lax.broadcasted_iota(jnp.int32, (LANES, LANES), 1)
        hit = (source == target + me * owned) & (target < owned)
        pick_ref[...] = jnp.where(hit, 1.0, 0.0).astype(BF16)

    barrier = pltpu.get_barrier_semaphore()

    def greet(k):
        pl.semaphore_signal(
            barrier, inc=1, device_id={"seq": lax.rem(me + k, n)}, device_id_type=pl.DeviceIdType.MESH
        )

    every(n, greet, 1)
    pl.semaphore_wait(barrier, n - 1)

    def far(k):
        peer = lax.rem(me + k * plane, n)
        return remote(aux_ref, aux_all.at[me], gate_send.at[k], gate_recv.at[me], peer)

    def landed(ref, sems, slot):
        return remote(ref.at[slot], ref.at[slot], gate_send.at[0], sems.at[slot], slot)

    across = me - inside + lax.rem(inside + 2, plane)
    sibling = me + 1 - 2 * lax.rem(me, 2)

    def relay(k, hop):
        owner = lax.rem((across if hop == 2 else me) + k * plane, n)
        peer = across if hop == 0 else sibling
        return remote(aux_all.at[owner], aux_all.at[owner], plane_send.at[k, hop], gate_recv.at[owner], peer)

    def x_copy(part, k):
        peer = lax.rem(me + k, n)
        return remote(tile(x_ref, part, peer), x_all.at[part, me], x_send.at[part, k], x_recv.at[part, me], peer)

    every(n // plane, lambda k: far(k).start(), 1)
    aux_all[me] = aux_ref[...]
    relay(0, 0).start()
    relay(0, 1).start()

    def forward(k):
        landed(aux_all, gate_recv, lax.rem(me + k * plane, n)).wait_recv()
        relay(k, 0).start()
        relay(k, 1).start()

    every(n // plane, forward, 1)
    for part in range(parts):
        x_all[part, me] = tile(x_ref, part, me)[...]

    load_params()

    def crossed(k):
        landed(aux_all, gate_recv, lax.rem(across + k * plane, n)).wait_recv()
        relay(k, 2).start()

    every(n // plane, crossed)
    every(n, lambda k: x_copy(0, k).start(), 1)
    for part in range(1, parts):
        every(n, lambda k: x_copy(part, k).start(), 1)

    def rest(k):
        for hop in (0, 2):
            owner = sibling - lax.rem(sibling, plane) + lax.rem(lax.rem(sibling, plane) + hop, plane)
            landed(aux_all, gate_recv, lax.rem(owner + k * plane, n)).wait_recv()

    every(n // plane, rest)
    aux_rows = aux_all
    find_places(aux_rows, keys, place_row, place_col, heads)
    ub[0:PAD, :] = jnp.zeros((PAD, state2), F32)
    ux[0:PAD, :] = jnp.zeros((PAD, size), F32)

    def gather(b):
        first = pl.multiple_of(b * block, block)
        onehot = one_hot_sort(place_row, first, block)
        if keep:
            sorter[pl.ds(first, block), :] = onehot
        aux_here = dot(onehot, aux_all[...].reshape(rows, aux_all.shape[2]))
        ub[pl.ds(pl.multiple_of(first + PAD, PAD), block), :] = aux_here[:, :state2]
        ds[pl.ds(first, block), :] = dot(aux_here[:, state2:].astype(BF16), pick_ref[...])

    every(rows // block, gather)

    starts, total = [], jnp.int32(0)
    for k in range(docs_ref.shape[0]):
        starts.append(total)
        total = total + docs_ref[k]

    def shared(c):
        for i in range(4):
            shared_chunk(4 * c + i, starts, ub, ds, bcpar_ref, rate_ref, bcs, ws, ent, tails, carries, owned)

    every(rows // CHUNK // 4, shared)
    if keep:

        def prepare(b):
            first = pl.multiple_of(b * block, block)
            unsorter[pl.ds(first, block), :] = one_hot_unsort(place_col, first, block)

        every(rows // block, prepare)

    def out_copy(part, owner):
        return remote(
            sent.at[part, owner], tile(out_ref, part, me), out_send.at[part, owner], out_recv.at[part, me], owner
        )

    for part in range(parts):

        def x_landed(k):
            source = lax.rem(me + k, n)
            slot = x_all.at[part, source]
            remote(slot, slot, gate_send.at[0], x_recv.at[part, source], source).wait_recv()

        every(n, x_landed, 1)

        def gather_x(b):
            first = pl.multiple_of(b * block, block)
            onehot = sorter[pl.ds(first, block), :] if keep else one_hot_sort(place_row, first, block)
            x_here = dot(onehot, x_all[part].reshape(rows, size))
            ux[pl.ds(pl.multiple_of(first + PAD, PAD), block), :] = x_here

        every(rows // block, gather_x)
        state[...] = jnp.zeros_like(state)

        def chunk(c):
            for i in range(4):
                scan_chunk(
                    4 * c + i, part, parts, starts, ux, xpar_ref, bcs, ws, ent, tails, carries, state, ys, owned
                )

        every(rows // CHUNK // 4, chunk)

        def scatter(i):
            b = lax.rem(me * tok // block + 1 + i, rows // block)
            first = pl.multiple_of(b * block, block)
            onehot = unsorter[pl.ds(first, block), :] if keep else one_hot_unsort(place_col, first, block)
            back = dot(onehot, ys[...]).astype(BF16)
            for j in range(block // tok):
                owner = b * (block // tok) + j
                sent[part, owner] = back[j * tok : (j + 1) * tok, :]

                @pl.when(owner != me)
                def _():
                    out_copy(part, owner).start()

        every(rows // block, scatter)
        tile(out_ref, part, me)[...] = sent[part, me]

    def finish(k):
        source = lax.rem(me + k, n)
        for part in range(parts):
            slot = tile(out_ref, part, source)
            remote(slot, slot, gate_send.at[0], out_recv.at[part, source], source).wait_recv()
            out_copy(part, source).wait_send()
            x_copy(part, k).wait_send()

    every(n, finish, 1)

    def finish_aux(k):
        for hop in range(3):
            relay(k, hop).wait_send()

    every(n // plane, finish_aux)
    every(n // plane, lambda k: far(k).wait_send(), 1)


def per_device(
    x_rows, bc_rows, step, route, doc_lengths, conv_weight, conv_bias, rate, skip, clip_level
):
    seq_count = lax.axis_size("seq")
    tok_rows, hp_width = x_rows.shape
    heads = step.shape[1]
    owned = heads // seq_count
    width = hp_width // seq_count
    state2 = bc_rows.shape[1]
    rows = tok_rows * seq_count

    spare = jnp.zeros((tok_rows, LANES - heads - 1), BF16)
    aux = jnp.concatenate([bc_rows, step, route.astype(BF16), spare], axis=1)
    parts = 2 if width % (2 * LANES) == 0 and owned % 2 == 0 else 1
    plane = 4
    size = width // parts
    keep = rows if rows <= 2048 else 16
    flat = size % LANES == 0
    x_send = x_rows if flat else jnp.swapaxes(x_rows.reshape(tok_rows, seq_count, width), 0, 1)

    vmem = pl.BlockSpec(memory_space=pltpu.VMEM)
    dma = pltpu.SemaphoreType.DMA
    out = pl.pallas_call(
        functools.partial(kernel, owned, heads, parts, plane),
        out_shape=jax.ShapeDtypeStruct(x_send.shape, BF16),
        in_specs=[pl.BlockSpec(memory_space=pltpu.SMEM)] * 4 + [vmem] * 4,
        out_specs=vmem,
        scratch_shapes=[
            pltpu.VMEM((8, width), F32),
            pltpu.VMEM((8, state2), F32),
            pltpu.VMEM((1, LANES), F32),
            pltpu.VMEM((LANES, LANES), BF16),
            pltpu.VMEM((seq_count, tok_rows, aux.shape[1]), BF16),
            pltpu.VMEM((parts, seq_count, tok_rows, size), BF16),
            pltpu.VMEM((parts, seq_count, tok_rows, size), BF16),
            pltpu.VMEM((rows, LANES), F32),
            pltpu.VMEM((8, rows), F32),
            pltpu.VMEM((rows, LANES), F32),
            pltpu.VMEM((PAD + rows, state2), F32),
            pltpu.VMEM((PAD + rows, size), F32),
            pltpu.VMEM((rows, LANES), F32),
            pltpu.VMEM((rows, state2), BF16),
            pltpu.VMEM((owned, rows, CHUNK), BF16),
            pltpu.VMEM((rows, width), F32),
            pltpu.VMEM((rows, width), F32),
            pltpu.VMEM((rows // CHUNK, 8, width), F32),
            pltpu.VMEM((rows, size), BF16),
            pltpu.VMEM((state2 // 2, size), F32),
            pltpu.VMEM((keep, keep), BF16),
            pltpu.VMEM((keep, keep), BF16),
            dma((seq_count // plane,)),
            dma((seq_count,)),
            dma((seq_count // plane, 3)),
            dma((parts, seq_count)),
            dma((parts, seq_count)),
            dma((parts, seq_count)),
            dma((parts, seq_count)),
        ],
        compiler_params=pltpu.CompilerParams(
            vmem_limit_bytes=60 * 1024 * 1024, collective_id=0, has_side_effects=True
        ),
    )(doc_lengths, rate, skip, clip_level, x_send, aux, conv_weight, conv_bias[None, :])
    return out if flat else jnp.swapaxes(out, 0, 1).reshape(tok_rows, hp_width)


SUB = 256
SMALL = 16


def fast_conv(rows, taps, bias, off):
    size = off.shape[0]
    acc = bias + taps[0:1, :] * rows[PAD : PAD + size, :]
    for j in range(1, 4):
        back = rows[PAD - j : PAD - j + size, :]
        acc = acc + taps[j : j + 1, :] * jnp.where(off >= j, back, 0.0)
    half = 0.5 * acc
    return (half + half * jnp.tanh(half)).astype(BF16)


def fast_kernel(
    owned, parts, plane, docs_ref, rates, skips, clips, x_ref, bc_ref, step_ref, route_ref, weight_ref, bias_ref, out_ref,
    step_v, route_v, x_taps, bc_taps, bias_v, small_out, small_all, bc_all, x_all, sent, off_ref,
    sorter, unsorter, dt_left, dt_right, places, ub, ux, lhs, b_flip, rise, fall, by_chunk, ys, state,
    load_sem, small_send, small_recv, gate_send, gate_recv, plane_send, x_send, x_recv, own_sem, out_send, out_recv,
):
    n, tok, state2 = bc_all.shape
    rows, size = ys.shape
    heads = step_v.shape[0]
    chunks = rows // CHUNK
    width = size * parts
    local = owned // parts
    me = lax.axis_index("seq")
    inside = lax.rem(me, plane)
    iota = functools.partial(lax.broadcasted_iota, jnp.int32)

    def remote(source, target, send, recv, peer):
        return pltpu.make_async_remote_copy(
            src_ref=source, dst_ref=target, send_sem=send, recv_sem=recv,
            device_id={"seq": peer}, device_id_type=pl.DeviceIdType.MESH,
        )

    def every(count, do, first=0):
        def turn(k, _):
            do(k)
            return 0

        lax.fori_loop(first, count, turn, 0)

    def tile(ref, part, owner):
        return ref.at[:, pl.ds(pl.multiple_of((owner * parts + part) * size, size), size)]

    barrier = pltpu.get_barrier_semaphore()

    def greet(k):
        pl.semaphore_signal(
            barrier, inc=1, device_id={"seq": lax.rem(me + k, n)}, device_id_type=pl.DeviceIdType.MESH
        )

    every(n, greet, 1)

    own = pl.ds(pl.multiple_of(me * width, width), width)
    shared_at = weight_ref.shape[1] - state2
    loads = [
        pltpu.make_async_copy(bc_ref, bc_all.at[me], load_sem.at[0]),
        pltpu.make_async_copy(step_ref, step_v, load_sem.at[1]),
        pltpu.make_async_copy(route_ref, route_v, load_sem.at[2]),
        pltpu.make_async_copy(weight_ref.at[:, own], x_taps, load_sem.at[3]),
        pltpu.make_async_copy(weight_ref.at[:, shared_at:], bc_taps, load_sem.at[4]),
        pltpu.make_async_copy(bias_ref, bias_v, load_sem.at[5]),
    ]
    for load in loads:
        load.start()

    loads[1].wait()
    loads[2].wait()
    wide_step = step_v[...].astype(F32)
    wide_route = jnp.broadcast_to(route_v[...].astype(F32), (8, tok))
    for p in range(n):
        mine = wide_step[p * owned : (p + 1) * owned, :]
        block = jnp.concatenate([mine, jnp.zeros((8 - owned, tok), F32), wide_route], axis=0)
        small_out[p] = block.astype(BF16)
    small_all[me] = small_out[me]
    loads[0].wait()

    pl.semaphore_wait(barrier, n - 1)

    def far(k):
        peer = lax.rem(me + k * plane, n)
        return remote(bc_all.at[me], bc_all.at[me], gate_send.at[k], gate_recv.at[me], peer)

    def small_copy(k):
        peer = lax.rem(me + k, n)
        return remote(small_out.at[peer], small_all.at[me], small_send.at[k], small_recv.at[me], peer)

    def landed(ref, sems, slot):
        return remote(ref.at[slot], ref.at[slot], gate_send.at[0], sems.at[slot], slot)

    across = me - inside + lax.rem(inside + 2, plane)
    sibling = me + 1 - 2 * lax.rem(me, 2)

    def relay(k, hop):
        owner = lax.rem((across if hop == 2 else me) + k * plane, n)
        peer = across if hop == 0 else sibling
        return remote(bc_all.at[owner], bc_all.at[owner], plane_send.at[k, hop], gate_recv.at[owner], peer)

    def x_copy(part, k):
        peer = lax.rem(me + k, n)
        return remote(tile(x_ref, part, peer), x_all.at[part, me], x_send.at[part, k], x_recv.at[part, me], peer)

    def own_copy(part):
        return pltpu.make_async_copy(tile(x_ref, part, me), x_all.at[part, me], own_sem.at[part])

    every(n, lambda k: small_copy(k).start(), 1)
    every(n // plane, lambda k: far(k).start(), 1)
    relay(0, 0).start()
    relay(0, 1).start()
    for part in range(parts):
        own_copy(part).start()
    for part in range(parts):
        every(n, lambda k: x_copy(part, k).start(), 1)

    starts, total = [], jnp.int32(0)
    for k in range(docs_ref.shape[0]):
        starts.append(total)
        total = total + docs_ref[k]

    def begins(at):
        begin = jnp.zeros(at.shape, jnp.int32)
        for start in starts:
            begin = jnp.where(at >= start, start, begin)
        return begin

    def forward(k):
        landed(bc_all, gate_recv, lax.rem(me + k * plane, n)).wait_recv()
        relay(k, 0).start()
        relay(k, 1).start()

    every(n // plane, forward, 1)

    def small_landed(k):
        landed(small_all, small_recv, lax.rem(me + k, n)).wait_recv()

    every(n, small_landed, 1)

    low, high = iota((CHUNK, CHUNK), 0), iota((CHUNK, CHUNK), 1)

    def find_places():
        number = iota((n, tok), 0).astype(F32)
        named = []
        for i in range(n):
            target = jnp.concatenate([small_all[i].astype(F32)[8:, :]] * (n // 8), axis=0)
            named.append(jnp.where(target == number, 1.0, 0.0))
        earlier = jnp.where(low < high, 1.0, 0.0).astype(BF16)
        right = jnp.concatenate([earlier, jnp.ones((tok, tok), BF16)], axis=1)
        found = dot(jnp.concatenate(named, axis=0).astype(BF16), right)
        before = jnp.zeros((n, tok), F32)
        ranks = []
        for i in range(n):
            here = found[i * n : (i + 1) * n, :]
            ranks.append(here[:, :tok] + before)
            before = before + here[:, tok:]
        base = jnp.zeros((n, tok), F32)
        for d in range(n - 1):
            base = base + jnp.where(number > d, before[d : d + 1, :], 0.0)
        for i in range(n):
            place = jnp.sum(named[i] * (ranks[i] + base), axis=0, keepdims=True)
            places[i : i + 1, :] = place
            coarse = jnp.floor(place * (1.0 / CHUNK))
            fine = place - coarse * CHUNK
            lanes = slice(i * tok, (i + 1) * tok)
            steps = small_all[i].astype(F32)[0:8, :]
            split = [jnp.where(coarse == c, steps, 0.0) for c in range(chunks)]
            dt_left[:, lanes] = jnp.concatenate(split, axis=0).astype(BF16)
            dt_right[:, lanes] = jnp.where(low.astype(F32) == fine, 1.0, 0.0).astype(BF16)

    find_places()

    row16 = iota((SUB, tok), 0).astype(F32).astype(BF16)
    one, none = jnp.ones((), BF16), jnp.zeros((), BF16)

    def make_sorter(b):
        first = lax.convert_element_type(b * SUB, F32)
        for i in range(n):
            rel = places[i : i + 1, :] - first
            rel = jnp.where((rel >= 0.0) & (rel < SUB), rel, -1.0)
            rel = jnp.broadcast_to(rel, (SUB, tok)).astype(BF16)
            hit = jnp.where(row16 == rel, one, none)
            sorter[pl.ds(pl.multiple_of(b * SUB, SUB), SUB), i * tok : (i + 1) * tok] = hit

    every(rows // SUB, make_sorter)

    def crossed(k):
        landed(bc_all, gate_recv, lax.rem(across + k * plane, n)).wait_recv()
        relay(k, 2).start()

    every(n // plane, crossed)

    def make_off(c):
        base = pl.multiple_of(c * CHUNK, CHUNK)
        at = low + base
        off_ref[pl.ds(base, CHUNK), :] = (at - begins(at)).astype(F32)

    every(chunks, make_off)

    def decays():
        dts = dot_nt(dt_left[...], dt_right[...])
        lane = iota((8, CHUNK), 1)
        slot = iota((8, CHUNK), 0)
        rate = jnp.zeros((8, CHUNK), F32)
        for h in range(owned):
            rate = jnp.where(slot == h, rates[me * owned + h], rate)
        rate = jnp.concatenate([rate] * chunks, axis=0)
        upto = jnp.where(low <= high, 1.0, 0.0).astype(BF16)
        cum = -dot(dts.astype(BF16), upto) * rate
        last = jnp.broadcast_to(cum[:, CHUNK - 1 :], cum.shape)
        middle = 0.5 * last
        up = jnp.exp(cum - middle)
        down = jnp.exp(middle - cum) * dts
        gain = jnp.exp(middle)
        number = iota((8 * chunks, CHUNK), 0) // 8
        ends = number * CHUNK + CHUNK - 1
        goes_on = jnp.where(begins(ends) < number * CHUNK, 1.0, 0.0)
        carry = jnp.exp(last) * goes_on
        by_chunk[0] = up
        by_chunk[1] = down
        by_chunk[2] = gain
        by_chunk[3] = carry

    decays()

    head = iota((1, size), 1) // (size // local)

    def spread(columns, part):
        out = jnp.broadcast_to(columns[:, part * local : part * local + 1], (CHUNK, size))
        for h in range(1, local):
            at = part * local + h
            out = jnp.where(head == h, jnp.broadcast_to(columns[:, at : at + 1], (CHUNK, size)), out)
        return out

    def expand(c):
        base = pl.multiple_of(c * CHUNK, CHUNK)
        at8 = pl.ds(pl.multiple_of(c * 8, 8), 8)
        rest = jnp.zeros((CHUNK - 16, CHUNK), F32)
        columns = jnp.concatenate([by_chunk[0, at8, :], by_chunk[1, at8, :], rest], axis=0).T
        for part in range(parts):
            rise[part, pl.ds(base, CHUNK), :] = spread(columns, part)
            fall[part, pl.ds(base, CHUNK), :] = spread(columns[:, 8:], part)

    every(chunks // 4, lambda c: [expand(4 * c + i) for i in range(4)])

    def rest(k):
        for hop in (0, 2):
            owner = sibling - lax.rem(sibling, plane) + lax.rem(lax.rem(sibling, plane) + hop, plane)
            landed(bc_all, gate_recv, lax.rem(owner + k * plane, n)).wait_recv()

    every(n // plane, rest)

    for load in loads[3:]:
        load.wait()
    ub[0:PAD, :] = jnp.zeros((PAD, state2), F32)
    ux[0:PAD, :] = jnp.zeros((PAD, size), F32)
    block = 512

    def gather(b):
        first = pl.multiple_of(b * block, block)
        here = dot(sorter[pl.ds(first, block), :], bc_all[...].reshape(rows, state2))
        ub[pl.ds(pl.multiple_of(first + PAD, PAD), block), :] = here

    every(rows // block, gather)

    gap = low - high

    def wide_bias(first, count):
        return jnp.concatenate([bias_v[pl.ds(first + i, 1), :] for i in range(count)], axis=1)

    def shared(c):
        base = pl.multiple_of(c * CHUNK, CHUNK)
        off = off_ref[pl.ds(base, CHUNK), :]
        off2 = jnp.concatenate([off] * (state2 // LANES), axis=1)
        bias = wide_bias(shared_at // LANES, state2 // LANES)
        act = fast_conv(ub[pl.ds(base, CHUNK + PAD), :], bc_taps[...], bias, off2)
        b_mat, c_mat = act[:, : state2 // 2], act[:, state2 // 2 :]
        scores = dot_nt(c_mat, b_mat)
        keep = (gap >= 0) & (gap.astype(F32) <= off)
        lhs[pl.ds(base, CHUNK), :CHUNK] = jnp.where(keep, scores, 0.0).astype(BF16)
        runs_in = jnp.where(off > low.astype(F32), c_mat.astype(F32), 0.0)
        lhs[pl.ds(base, CHUNK), CHUNK:] = runs_in.astype(BF16)
        runs_out = high[0:1, :].astype(F32) + off[CHUNK - 1 :, :] >= CHUNK - 1
        b_flip[pl.ds(base, CHUNK), :] = jnp.where(runs_out, b_mat.astype(F32).T, 0.0).astype(BF16)

    every(chunks // 4, lambda c: [shared(4 * c + i) for i in range(4)])

    col16 = iota((tok, SUB), 1).astype(F32).astype(BF16)
    flipped = jnp.concatenate([places[...], jnp.zeros((tok - n, tok), F32)], axis=0).T

    def make_unsorter(b):
        first = lax.convert_element_type(b * SUB, F32)
        for i in range(n):
            rel = jnp.broadcast_to(flipped[:, i : i + 1], (tok, tok)) - first
            rel = jnp.where((rel >= 0.0) & (rel < SUB), rel, -1.0).astype(BF16)
            hit = jnp.where(col16 == jnp.concatenate([rel] * (SUB // tok), axis=1), one, none)
            unsorter[i * tok : (i + 1) * tok, pl.ds(pl.multiple_of(b * SUB, SUB), SUB)] = hit

    every(rows // SUB, make_unsorter)

    def out_copy(part, owner):
        return remote(
            sent.at[part, owner], tile(out_ref, part, me), out_send.at[part, owner], out_recv.at[part, me], owner
        )

    def own_out(part):
        return pltpu.make_async_copy(sent.at[part, me], tile(out_ref, part, me), own_sem.at[parts + part])

    lane_head = iota((1, size), 1) // (size // local)

    def by_head(values):
        out = jnp.full((1, size), values[0], F32)
        for h in range(1, local):
            out = jnp.where(lane_head == h, values[h], out)
        return out

    for part in range(parts):

        def x_landed(k):
            source = lax.rem(me + k, n)
            slot = x_all.at[part, source]
            remote(slot, slot, gate_send.at[0], x_recv.at[part, source], source).wait_recv()

        own_copy(part).wait()
        every(n, x_landed, 1)

        def gather_x(b):
            first = pl.multiple_of(b * block, block)
            here = dot(sorter[pl.ds(first, block), :], x_all[part].reshape(rows, size))
            ux[pl.ds(pl.multiple_of(first + PAD, PAD), block), :] = here

        every(rows // block, gather_x)
        state[...] = jnp.zeros_like(state)
        skip = by_head([skips[me * owned + part * local + h] for h in range(local)])
        level = by_head([clips[me * owned + part * local + h] for h in range(local)])

        def chunk(c):
            base = pl.multiple_of(c * CHUNK, CHUNK)
            at = pl.ds(base, CHUNK)
            bias = bias_v[pl.ds(me * parts + part, 1), :]
            taps = x_taps[:, part * size : (part + 1) * size]
            wide = fast_conv(ux[pl.ds(base, CHUNK + PAD), :], taps, bias, off_ref[at, :]).astype(F32)
            scaled = (wide * fall[part, at, :]).astype(BF16)
            at8 = pl.ds(pl.multiple_of(c * 8, 8), 8)
            gains, carries = by_chunk[2, at8, :], by_chunk[3, at8, :]
            gain = by_head([gains[part * local + h : part * local + h + 1, :] for h in range(local)])
            carry = by_head([carries[part * local + h : part * local + h + 1, :] for h in range(local)])
            old = state[...]
            right = jnp.concatenate([scaled, (gain * old).astype(BF16)], axis=0)
            y = skip * wide + rise[part, at, :] * dot(lhs[at, :], right)
            ys[at, :] = jnp.clip(y, -level, level).astype(BF16)
            state[...] = carry * old + gain * dot(b_flip[at, :], scaled)

        every(chunks // 4, lambda c: [chunk(4 * c + i) for i in range(4)])

        def scatter(i):
            b = lax.rem(me * tok // block + 1 + i, rows // block)
            first = pl.multiple_of(b * block, block)
            back = dot(unsorter[pl.ds(first, block), :], ys[...]).astype(BF16)
            for j in range(block // tok):
                owner = b * (block // tok) + j
                sent[part, owner] = back[j * tok : (j + 1) * tok, :]

                @pl.when(owner != me)
                def _():
                    out_copy(part, owner).start()

        every(rows // block, scatter)
        own_out(part).start()

    def finish(k):
        source = lax.rem(me + k, n)
        for part in range(parts):
            slot = tile(out_ref, part, source)
            remote(slot, slot, gate_send.at[0], out_recv.at[part, source], source).wait_recv()
            out_copy(part, source).wait_send()
            x_copy(part, k).wait_send()
        small_copy(k).wait_send()

    every(n, finish, 1)
    for part in range(parts):
        own_out(part).wait()

    def finish_aux(k):
        for hop in range(3):
            relay(k, hop).wait_send()

    every(n // plane, finish_aux)
    every(n // plane, lambda k: far(k).wait_send(), 1)


def fast_device(
    x_rows, bc_rows, step, route, doc_lengths, conv_weight, conv_bias, rate, skip, clip_level
):
    n = lax.axis_size("seq")
    tok, hp_width = x_rows.shape
    heads = step.shape[1]
    owned = heads // n
    width = hp_width // n
    state2 = bc_rows.shape[1]
    rows = tok * n
    parts = width // LANES
    size = LANES
    plane = 4
    chunks = rows // CHUNK
    bias = conv_bias.reshape(conv_bias.shape[0] // LANES, LANES)

    hbm = pl.BlockSpec(memory_space=pl.ANY)
    dma = pltpu.SemaphoreType.DMA
    return pl.pallas_call(
        functools.partial(fast_kernel, owned, parts, plane),
        out_shape=jax.ShapeDtypeStruct(x_rows.shape, BF16),
        in_specs=[pl.BlockSpec(memory_space=pltpu.SMEM)] * 4 + [hbm] * 6,
        out_specs=OUT_SPEC,
        scratch_shapes=[
            pltpu.VMEM((heads, tok), BF16),
            pltpu.VMEM((1, tok), jnp.int32),
            pltpu.VMEM((4, width), F32),
            pltpu.VMEM((4, state2), F32),
            pltpu.VMEM(bias.shape, F32),
            pltpu.VMEM((n, SMALL, tok), BF16),
            pltpu.VMEM((n, SMALL, tok), BF16),
            pltpu.VMEM((n, tok, state2), BF16),
            pltpu.VMEM((parts, n, tok, size), BF16),
            pltpu.VMEM((parts, n, tok, size), BF16),
            pltpu.VMEM((rows, LANES), F32),
            pltpu.VMEM((rows, rows), BF16),
            pltpu.VMEM((rows, rows), BF16),
            pltpu.VMEM((8 * chunks, rows), BF16),
            pltpu.VMEM((CHUNK, rows), BF16),
            pltpu.VMEM((n, tok), F32),
            pltpu.VMEM((PAD + rows, state2), F32),
            pltpu.VMEM((PAD + rows, size), F32),
            pltpu.VMEM((rows, 2 * CHUNK), BF16),
            pltpu.VMEM((rows, CHUNK), BF16),
            pltpu.VMEM((parts, rows, size), F32),
            pltpu.VMEM((parts, rows, size), F32),
            pltpu.VMEM((4, 8 * chunks, CHUNK), F32),
            pltpu.VMEM((rows, size), BF16),
            pltpu.VMEM((state2 // 2, size), F32),
            dma((6,)),
            dma((n,)),
            dma((n,)),
            dma((n // plane,)),
            dma((n,)),
            dma((n // plane, 3)),
            dma((parts, n)),
            dma((parts, n)),
            dma((2 * parts,)),
            dma((parts, n)),
            dma((parts, n)),
        ],
        compiler_params=pltpu.CompilerParams(
            vmem_limit_bytes=48 * 1024 * 1024, collective_id=1, has_side_effects=True
        ),
    )(doc_lengths, rate, skip, clip_level, x_rows, bc_rows, step.T, route.T, conv_weight, bias)


def fits_fast(n, x_shape, heads, state2):
    width = x_shape[1] // n
    owned = heads // n
    return (
        n % 8 == 0 and n * x_shape[0] <= 2048 and x_shape[0] == LANES and width % LANES == 0 and state2 == 2 * CHUNK
        and owned <= 8 and owned % (width // LANES) == 0 and 8 * n * LANES // CHUNK <= CHUNK
    )


def solution(mesh):
    placed = (
        P(("groups", "seq"), None),
        P(("groups", "seq"), None),
        P(("groups", "seq"), None),
        P(("groups", "seq"), None),
        P("groups"),
        P(),
        P(),
        P(),
        P(),
        P(),
    )

    def run(*arrays):
        x_rows, bc_rows, step = arrays[:3]
        fast = fits_fast(lax.axis_size("seq"), x_rows.shape, step.shape[1], bc_rows.shape[1])
        return (fast_device if fast else per_device)(*arrays)

    return jax.shard_map(
        run,
        mesh=mesh,
        in_specs=placed,
        out_specs=P(("groups", "seq"), None),
        check_vma=False,
    )
```

```python
import functools

import jax
import jax.numpy as jnp
from jax import lax
from jax.experimental import pallas as pl
from jax.experimental.pallas import tpu as pltpu
from jax.sharding import PartitionSpec as P

F32 = jnp.float32
BF16 = jnp.bfloat16
CHUNK = 128
LANES = 128
PAD = 8
OUT_SPEC = pl.BlockSpec(memory_space=pl.ANY)


def dot(a, b):
    return jnp.dot(a, b, preferred_element_type=F32)


def dot_nt(a, b):
    return lax.dot_general(a, b, (((1,), (1,)), ((), ())), preferred_element_type=F32)


def dot_tn(a, b):
    return lax.dot_general(a, b, (((0,), (0,)), ((), ())), preferred_element_type=F32)


def find_places(aux_ref, ranks, place_row, place_col, heads):
    rows = ranks.shape[0]
    state2 = aux_ref.shape[2] - LANES
    low = lax.broadcasted_iota(jnp.int32, (LANES, LANES), 0)
    high = lax.broadcasted_iota(jnp.int32, (LANES, LANES), 1)
    earlier = jnp.where(low > high, 1.0, 0.0).astype(BF16)
    before = jnp.where(low < high, 1.0, 0.0).astype(BF16)
    shard = high.astype(F32)
    step = 4

    def named(b):
        target = aux_ref[b, :, state2 : state2 + LANES].astype(F32)[:, heads : heads + 1]
        return jnp.where(target == shard, 1.0, 0.0)

    def count(i, total):
        for j in range(step):
            b = i * step + j
            onehot = named(b)
            ranks[pl.ds(pl.multiple_of(b * LANES, LANES), LANES), :] = dot(earlier, onehot.astype(BF16)) + total
            total = total + jnp.sum(onehot, axis=0, keepdims=True)
        return total

    total = lax.fori_loop(0, rows // LANES // step, count, jnp.zeros((1, LANES), F32))
    total = jnp.broadcast_to(total, (8, LANES))
    coarse = jnp.floor(total * (1.0 / 64.0))
    fine = total - coarse * 64.0
    start = (dot(coarse.astype(BF16), before) * 64.0 + dot(fine.astype(BF16), before))[0:1, :]

    def rank(i, _):
        for j in range(step):
            b = i * step + j
            at = pl.multiple_of(b * LANES, LANES)
            found = named(b) * (ranks[pl.ds(at, LANES), :] + start)
            place = jnp.broadcast_to(jnp.sum(found, axis=1, keepdims=True), (LANES, LANES))
            place_col[pl.ds(at, LANES), :] = place
            place_row[:, pl.ds(at, LANES)] = place.T[0:8, :]
        return 0

    lax.fori_loop(0, rows // LANES // step, rank, 0)


def one_hot_sort(place_row, first, size):
    rows = place_row.shape[1]
    number = lax.broadcasted_iota(jnp.int32, (size, rows), 0).astype(F32)
    hit = place_row[0:1, :] - lax.convert_element_type(first, F32) == number
    return jnp.where(hit, 1.0, 0.0).astype(BF16)


def one_hot_unsort(place_col, first, size):
    rows = place_col.shape[0]
    number = lax.broadcasted_iota(jnp.int32, (size, rows), 1).astype(F32)
    place = place_col[pl.ds(first, size), :]
    hit = jnp.concatenate([place] * (rows // LANES), axis=1) == number
    return jnp.where(hit, 1.0, 0.0).astype(BF16)


def doc_begins(at, starts):
    begin = jnp.zeros((CHUNK, 1), jnp.int32)
    for start in starts:
        begin = jnp.where(at >= start, start, begin)
    return begin


def conv_silu(v, par, at, begin):
    acc = par[4:5, :] + par[0:1, :] * v[PAD:, :]
    for j in range(1, 4):
        keep = jnp.where(at - j >= begin, 1.0, 0.0)
        acc = acc + par[j : j + 1, :] * (v[PAD - j : PAD - j + CHUNK, :] * keep)
    return (acc / (1.0 + jnp.exp(-acc))).astype(BF16)


def shared_chunk(c, starts, ub, ds, bcpar_ref, rate_ref, bcs, ws, ent, tails, carries, owned):
    width = ent.shape[1]
    state_width = bcs.shape[1] // 2
    base = pl.multiple_of(c * CHUNK, CHUNK)
    at = lax.broadcasted_iota(jnp.int32, (CHUNK, 1), 0) + base
    begin = doc_begins(at, starts)
    begin_last = begin[CHUNK - 1 :, :]
    act = conv_silu(ub[pl.ds(base, CHUNK + PAD), :], bcpar_ref[...], at, begin)
    bcs[pl.ds(base, CHUNK), :] = act
    b_mat, c_mat = act[:, :state_width], act[:, state_width:]

    dt = ds[pl.ds(base, CHUNK), :]
    low = lax.broadcasted_iota(jnp.int32, (CHUNK, CHUNK), 0)
    high = lax.broadcasted_iota(jnp.int32, (CHUNK, CHUNK), 1)
    tri = jnp.where(low >= high, 1.0, 0.0).astype(BF16)
    cum = -dot(tri, dt.astype(BF16)) * rate_ref[...]
    shifted = (cum - jnp.log(jnp.maximum(dt, 1e-30))).T
    cum_last = cum[CHUNK - 1 :, :]
    scores = dot_nt(c_mat, b_mat)
    scores = jnp.where((low >= high) & (high + base >= begin), scores, 0.0)
    head = lax.broadcasted_iota(jnp.int32, (1, width), 1) // (width // owned)

    def expand(e):
        out = jnp.broadcast_to(e[:, 0:1], (e.shape[0], width))
        for h in range(1, owned):
            out = jnp.where(head == h, e[:, h : h + 1], out)
        return out

    for h in range(owned):
        decay = jnp.exp(cum[:, h : h + 1] - shifted[h : h + 1, :])
        ws[h, pl.ds(base, CHUNK), :] = (scores * decay).astype(BF16)
    ent[pl.ds(base, CHUNK), :] = expand(jnp.exp(cum) * jnp.where(begin < base, 1.0, 0.0))
    tail = jnp.exp(cum_last - cum) * dt * jnp.where(at >= begin_last, 1.0, 0.0)
    tails[pl.ds(base, CHUNK), :] = expand(tail)
    carry = expand(jnp.exp(cum_last) * jnp.where(begin_last < base, 1.0, 0.0))
    carries[c] = jnp.broadcast_to(carry, (8, width))


def scan_chunk(c, part, parts, starts, ux, xpar_ref, bcs, ws, ent, tails, carries, state, ys, owned):
    size = ux.shape[1]
    lanes = slice(part * size, (part + 1) * size)
    state_width = bcs.shape[1] // 2
    base = pl.multiple_of(c * CHUNK, CHUNK)
    at = lax.broadcasted_iota(jnp.int32, (CHUNK, 1), 0) + base
    begin = doc_begins(at, starts)
    x_mat = conv_silu(ux[pl.ds(base, CHUNK + PAD), :], xpar_ref[:, lanes], at, begin)
    x_wide = x_mat.astype(F32)
    bc = bcs[pl.ds(base, CHUNK), :]
    b_mat, c_mat = bc[:, :state_width], bc[:, state_width:]
    local = owned // parts
    head = lax.broadcasted_iota(jnp.int32, (1, size), 1) // (size // local)
    y = xpar_ref[5:6, lanes] * x_wide
    for h in range(local):
        mine = jnp.where(head == h, x_wide, 0.0).astype(BF16)
        y = y + dot(ws[part * local + h, pl.ds(base, CHUNK), :], mine)
    y = y + dot(c_mat, state[...].astype(BF16)) * ent[pl.ds(base, CHUNK), lanes]
    limit = xpar_ref[6:7, lanes]
    ys[pl.ds(base, CHUNK), :] = jnp.clip(y, -limit, limit).astype(BF16)
    scaled = (x_wide * tails[pl.ds(base, CHUNK), lanes]).astype(BF16)
    state[...] = carries[c][0:1, lanes] * state[...] + dot_tn(b_mat, scaled)


def kernel(
    owned, heads, parts, plane, docs_ref, rates, skips, clips, x_ref, aux_ref, weight_ref, bias_ref, out_ref,
    xpar_ref, bcpar_ref, rate_ref, pick_ref, aux_all, x_all, sent, keys, place_row, place_col, ub, ux, ds, bcs, ws, ent, tails, carries, ys, state,
    sorter, unsorter, gate_send, gate_recv, plane_send, x_send, x_recv, out_send, out_recv,
):
    n, tok = x_all.shape[1:3]
    rows, size = ys.shape
    state2 = bcs.shape[1]
    flat = len(x_ref.shape) == 2
    block = max(tok, min(512, (1 << 20) // rows))
    keep = sorter.shape[0] == rows
    me = lax.axis_index("seq")
    inside = lax.rem(me, plane)

    def remote(source, target, send, recv, peer):
        return pltpu.make_async_remote_copy(
            src_ref=source, dst_ref=target, send_sem=send, recv_sem=recv,
            device_id={"seq": peer}, device_id_type=pl.DeviceIdType.MESH,
        )

    def every(count, do, first=0):
        def turn(k, _):
            do(k)
            return 0

        lax.fori_loop(first, count, turn, 0)

    def tile(ref, part, owner):
        if flat:
            return ref.at[:, pl.ds(pl.multiple_of((owner * parts + part) * size, size), size)]
        return ref.at[owner]

    def own_lanes(ref):
        width = size * parts
        if width % LANES == 0:
            return ref[:, pl.ds(pl.multiple_of(me * width, LANES), width)]
        per = LANES // width
        wide = ref[:, pl.ds(pl.multiple_of(me // per * LANES, LANES), LANES)]
        picked = wide[:, :width]
        for i in range(1, per):
            picked = jnp.where(lax.rem(me, per) == i, wide[:, i * width : (i + 1) * width], picked)
        return picked

    def load_params():
        width = size * parts
        head = lax.broadcasted_iota(jnp.int32, (1, width), 1) // (width // owned)
        lane = lax.broadcasted_iota(jnp.int32, (1, LANES), 1)
        gain = level = jnp.zeros((1, width), F32)
        decay = jnp.zeros((1, LANES), F32)
        for h in range(owned):
            gain = jnp.where(head == h, skips[me * owned + h], gain)
            level = jnp.where(head == h, clips[me * owned + h], level)
            decay = jnp.where(lane == h, rates[me * owned + h], decay)
        xpar_ref[0:4, :] = own_lanes(weight_ref)
        xpar_ref[4:5, :] = own_lanes(bias_ref)
        xpar_ref[5:6, :] = gain
        xpar_ref[6:7, :] = level
        first = weight_ref.shape[1] - state2
        bcpar_ref[0:4, :] = weight_ref[:, first:]
        bcpar_ref[4:5, :] = bias_ref[:, first:]
        rate_ref[...] = decay
        source = lax.broadcasted_iota(jnp.int32, (LANES, LANES), 0)
        target = lax.broadcasted_iota(jnp.int32, (LANES, LANES), 1)
        hit = (source == target + me * owned) & (target < owned)
        pick_ref[...] = jnp.where(hit, 1.0, 0.0).astype(BF16)

    barrier = pltpu.get_barrier_semaphore()

    def greet(k):
        pl.semaphore_signal(
            barrier, inc=1, device_id={"seq": lax.rem(me + k, n)}, device_id_type=pl.DeviceIdType.MESH
        )

    every(n, greet, 1)
    pl.semaphore_wait(barrier, n - 1)

    def far(k):
        peer = lax.rem(me + k * plane, n)
        return remote(aux_ref, aux_all.at[me], gate_send.at[k], gate_recv.at[me], peer)

    def landed(ref, sems, slot):
        return remote(ref.at[slot], ref.at[slot], gate_send.at[0], sems.at[slot], slot)

    across = me - inside + lax.rem(inside + 2, plane)
    sibling = me + 1 - 2 * lax.rem(me, 2)

    def relay(k, hop):
        owner = lax.rem((across if hop == 2 else me) + k * plane, n)
        peer = across if hop == 0 else sibling
        return remote(aux_all.at[owner], aux_all.at[owner], plane_send.at[k, hop], gate_recv.at[owner], peer)

    def x_copy(part, k):
        peer = lax.rem(me + k, n)
        return remote(tile(x_ref, part, peer), x_all.at[part, me], x_send.at[part, k], x_recv.at[part, me], peer)

    every(n // plane, lambda k: far(k).start(), 1)
    aux_all[me] = aux_ref[...]
    relay(0, 0).start()
    relay(0, 1).start()

    def forward(k):
        landed(aux_all, gate_recv, lax.rem(me + k * plane, n)).wait_recv()
        relay(k, 0).start()
        relay(k, 1).start()

    every(n // plane, forward, 1)
    for part in range(parts):
        x_all[part, me] = tile(x_ref, part, me)[...]

    load_params()

    def crossed(k):
        landed(aux_all, gate_recv, lax.rem(across + k * plane, n)).wait_recv()
        relay(k, 2).start()

    every(n // plane, crossed)
    every(n, lambda k: x_copy(0, k).start(), 1)
    for part in range(1, parts):
        every(n, lambda k: x_copy(part, k).start(), 1)

    def rest(k):
        for hop in (0, 2):
            owner = sibling - lax.rem(sibling, plane) + lax.rem(lax.rem(sibling, plane) + hop, plane)
            landed(aux_all, gate_recv, lax.rem(owner + k * plane, n)).wait_recv()

    every(n // plane, rest)
    aux_rows = aux_all
    find_places(aux_rows, keys, place_row, place_col, heads)
    ub[0:PAD, :] = jnp.zeros((PAD, state2), F32)
    ux[0:PAD, :] = jnp.zeros((PAD, size), F32)

    def gather(b):
        first = pl.multiple_of(b * block, block)
        onehot = one_hot_sort(place_row, first, block)
        if keep:
            sorter[pl.ds(first, block), :] = onehot
        aux_here = dot(onehot, aux_all[...].reshape(rows, aux_all.shape[2]))
        ub[pl.ds(pl.multiple_of(first + PAD, PAD), block), :] = aux_here[:, :state2]
        ds[pl.ds(first, block), :] = dot(aux_here[:, state2:].astype(BF16), pick_ref[...])

    every(rows // block, gather)

    starts, total = [], jnp.int32(0)
    for k in range(docs_ref.shape[0]):
        starts.append(total)
        total = total + docs_ref[k]

    def shared(c):
        for i in range(4):
            shared_chunk(4 * c + i, starts, ub, ds, bcpar_ref, rate_ref, bcs, ws, ent, tails, carries, owned)

    every(rows // CHUNK // 4, shared)
    if keep:

        def prepare(b):
            first = pl.multiple_of(b * block, block)
            unsorter[pl.ds(first, block), :] = one_hot_unsort(place_col, first, block)

        every(rows // block, prepare)

    def out_copy(part, owner):
        return remote(
            sent.at[part, owner], tile(out_ref, part, me), out_send.at[part, owner], out_recv.at[part, me], owner
        )

    for part in range(parts):

        def x_landed(k):
            source = lax.rem(me + k, n)
            slot = x_all.at[part, source]
            remote(slot, slot, gate_send.at[0], x_recv.at[part, source], source).wait_recv()

        every(n, x_landed, 1)

        def gather_x(b):
            first = pl.multiple_of(b * block, block)
            onehot = sorter[pl.ds(first, block), :] if keep else one_hot_sort(place_row, first, block)
            x_here = dot(onehot, x_all[part].reshape(rows, size))
            ux[pl.ds(pl.multiple_of(first + PAD, PAD), block), :] = x_here

        every(rows // block, gather_x)
        state[...] = jnp.zeros_like(state)

        def chunk(c):
            for i in range(4):
                scan_chunk(
                    4 * c + i, part, parts, starts, ux, xpar_ref, bcs, ws, ent, tails, carries, state, ys, owned
                )

        every(rows // CHUNK // 4, chunk)

        def scatter(i):
            b = lax.rem(me * tok // block + 1 + i, rows // block)
            first = pl.multiple_of(b * block, block)
            onehot = unsorter[pl.ds(first, block), :] if keep else one_hot_unsort(place_col, first, block)
            back = dot(onehot, ys[...]).astype(BF16)
            for j in range(block // tok):
                owner = b * (block // tok) + j
                sent[part, owner] = back[j * tok : (j + 1) * tok, :]

                @pl.when(owner != me)
                def _():
                    out_copy(part, owner).start()

        every(rows // block, scatter)
        tile(out_ref, part, me)[...] = sent[part, me]

    def finish(k):
        source = lax.rem(me + k, n)
        for part in range(parts):
            slot = tile(out_ref, part, source)
            remote(slot, slot, gate_send.at[0], out_recv.at[part, source], source).wait_recv()
            out_copy(part, source).wait_send()
            x_copy(part, k).wait_send()

    every(n, finish, 1)

    def finish_aux(k):
        for hop in range(3):
            relay(k, hop).wait_send()

    every(n // plane, finish_aux)
    every(n // plane, lambda k: far(k).wait_send(), 1)


def per_device(
    x_rows, bc_rows, step, route, doc_lengths, conv_weight, conv_bias, rate, skip, clip_level
):
    seq_count = lax.axis_size("seq")
    tok_rows, hp_width = x_rows.shape
    heads = step.shape[1]
    owned = heads // seq_count
    width = hp_width // seq_count
    state2 = bc_rows.shape[1]
    rows = tok_rows * seq_count

    spare = jnp.zeros((tok_rows, LANES - heads - 1), BF16)
    aux = jnp.concatenate([bc_rows, step, route.astype(BF16), spare], axis=1)
    parts = 2 if width % (2 * LANES) == 0 and owned % 2 == 0 else 1
    plane = 4
    size = width // parts
    keep = rows if rows <= 2048 else 16
    flat = size % LANES == 0
    x_send = x_rows if flat else jnp.swapaxes(x_rows.reshape(tok_rows, seq_count, width), 0, 1)

    vmem = pl.BlockSpec(memory_space=pltpu.VMEM)
    dma = pltpu.SemaphoreType.DMA
    out = pl.pallas_call(
        functools.partial(kernel, owned, heads, parts, plane),
        out_shape=jax.ShapeDtypeStruct(x_send.shape, BF16),
        in_specs=[pl.BlockSpec(memory_space=pltpu.SMEM)] * 4 + [vmem] * 4,
        out_specs=vmem,
        scratch_shapes=[
            pltpu.VMEM((8, width), F32),
            pltpu.VMEM((8, state2), F32),
            pltpu.VMEM((1, LANES), F32),
            pltpu.VMEM((LANES, LANES), BF16),
            pltpu.VMEM((seq_count, tok_rows, aux.shape[1]), BF16),
            pltpu.VMEM((parts, seq_count, tok_rows, size), BF16),
            pltpu.VMEM((parts, seq_count, tok_rows, size), BF16),
            pltpu.VMEM((rows, LANES), F32),
            pltpu.VMEM((8, rows), F32),
            pltpu.VMEM((rows, LANES), F32),
            pltpu.VMEM((PAD + rows, state2), F32),
            pltpu.VMEM((PAD + rows, size), F32),
            pltpu.VMEM((rows, LANES), F32),
            pltpu.VMEM((rows, state2), BF16),
            pltpu.VMEM((owned, rows, CHUNK), BF16),
            pltpu.VMEM((rows, width), F32),
            pltpu.VMEM((rows, width), F32),
            pltpu.VMEM((rows // CHUNK, 8, width), F32),
            pltpu.VMEM((rows, size), BF16),
            pltpu.VMEM((state2 // 2, size), F32),
            pltpu.VMEM((keep, keep), BF16),
            pltpu.VMEM((keep, keep), BF16),
            dma((seq_count // plane,)),
            dma((seq_count,)),
            dma((seq_count // plane, 3)),
            dma((parts, seq_count)),
            dma((parts, seq_count)),
            dma((parts, seq_count)),
            dma((parts, seq_count)),
        ],
        compiler_params=pltpu.CompilerParams(
            vmem_limit_bytes=60 * 1024 * 1024, collective_id=0, has_side_effects=True
        ),
    )(doc_lengths, rate, skip, clip_level, x_send, aux, conv_weight, conv_bias[None, :])
    return out if flat else jnp.swapaxes(out, 0, 1).reshape(tok_rows, hp_width)


SUB = 256
SMALL = 16


def fast_conv(rows, taps, bias, off):
    size = off.shape[0]
    acc = bias + taps[0:1, :] * rows[PAD : PAD + size, :]
    for j in range(1, 4):
        back = rows[PAD - j : PAD - j + size, :]
        acc = acc + taps[j : j + 1, :] * jnp.where(off >= j, back, 0.0)
    half = 0.5 * acc
    return (half + half * jnp.tanh(half)).astype(BF16)


def fast_kernel(
    owned, parts, plane, docs_ref, rates, skips, clips, x_ref, bc_ref, step_ref, route_ref, weight_ref, bias_ref, out_ref,
    step_v, route_v, x_taps, bc_taps, bias_v, small_out, small_all, bc_all, x_all, sent, off_ref,
    sorter, unsorter, columns, dt_left, dt_right, places, ub, ux, lhs, b_flip, rise, fall, by_chunk, ys, state,
    load_sem, small_send, small_recv, gate_send, gate_recv, plane_send, x_send, x_recv, own_sem, out_send, out_recv,
):
    n, tok, state2 = bc_all.shape
    rows, size = ys.shape
    heads = step_v.shape[0]
    chunks = rows // CHUNK
    width = size * parts
    local = owned // parts
    me = lax.axis_index("seq")
    inside = lax.rem(me, plane)
    iota = functools.partial(lax.broadcasted_iota, jnp.int32)

    def remote(source, target, send, recv, peer):
        return pltpu.make_async_remote_copy(
            src_ref=source, dst_ref=target, send_sem=send, recv_sem=recv,
            device_id={"seq": peer}, device_id_type=pl.DeviceIdType.MESH,
        )

    def every(count, do, first=0):
        def turn(k, _):
            do(k)
            return 0

        lax.fori_loop(first, count, turn, 0)

    def tile(ref, part, owner):
        return ref.at[:, pl.ds(pl.multiple_of((owner * parts + part) * size, size), size)]

    barrier = pltpu.get_barrier_semaphore()

    def greet(k):
        pl.semaphore_signal(
            barrier, inc=1, device_id={"seq": lax.rem(me + k, n)}, device_id_type=pl.DeviceIdType.MESH
        )

    every(n, greet, 1)

    own = pl.ds(pl.multiple_of(me * width, width), width)
    shared_at = weight_ref.shape[1] - state2
    loads = [
        pltpu.make_async_copy(bc_ref, bc_all.at[me], load_sem.at[0]),
        pltpu.make_async_copy(step_ref, step_v, load_sem.at[1]),
        pltpu.make_async_copy(route_ref, route_v, load_sem.at[2]),
        pltpu.make_async_copy(weight_ref.at[:, own], x_taps, load_sem.at[3]),
        pltpu.make_async_copy(weight_ref.at[:, shared_at:], bc_taps, load_sem.at[4]),
        pltpu.make_async_copy(bias_ref, bias_v, load_sem.at[5]),
    ]
    for load in loads:
        load.start()

    loads[1].wait()
    loads[2].wait()
    wide_step = step_v[...].astype(F32)
    wide_route = jnp.broadcast_to(route_v[...].astype(F32), (8, tok))
    for p in range(n):
        mine = wide_step[p * owned : (p + 1) * owned, :]
        block = jnp.concatenate([mine, jnp.zeros((8 - owned, tok), F32), wide_route], axis=0)
        small_out[p] = block.astype(BF16)
    small_all[me] = small_out[me]
    loads[0].wait()

    pl.semaphore_wait(barrier, n - 1)

    def far(k):
        peer = lax.rem(me + k * plane, n)
        return remote(bc_all.at[me], bc_all.at[me], gate_send.at[k], gate_recv.at[me], peer)

    def small_copy(k):
        peer = lax.rem(me + k, n)
        return remote(small_out.at[peer], small_all.at[me], small_send.at[k], small_recv.at[me], peer)

    def landed(ref, sems, slot):
        return remote(ref.at[slot], ref.at[slot], gate_send.at[0], sems.at[slot], slot)

    across = me - inside + lax.rem(inside + 2, plane)
    sibling = me + 1 - 2 * lax.rem(me, 2)

    def relay(k, hop):
        owner = lax.rem((across if hop == 2 else me) + k * plane, n)
        peer = across if hop == 0 else sibling
        return remote(bc_all.at[owner], bc_all.at[owner], plane_send.at[k, hop], gate_recv.at[owner], peer)

    def x_copy(part, peer):
        return remote(tile(x_ref, part, peer), x_all.at[part, me], x_send.at[part, peer], x_recv.at[part, me], peer)

    planes = n // plane
    half = planes // 2
    mine = me // plane

    def plane_at(i):
        turn = lax.rem(i, half)
        side = lax.rem(mine // half + 1 + i // half, 2)
        return side * half + lax.rem(lax.rem(mine, half) + turn + i // half, half)

    def own_copy(part):
        return pltpu.make_async_copy(tile(x_ref, part, me), x_all.at[part, me], own_sem.at[part])

    def start_x(part):
        def to_plane(i):
            for j in range(plane):
                peer = plane_at(i) * plane + lax.rem(inside + 1 + j, plane)

                @pl.when(peer != me)
                def _():
                    x_copy(part, peer).start()

        every(planes, to_plane)

    every(n, lambda k: small_copy(k).start(), 1)
    every(n // plane, lambda k: far(k).start(), 1)
    relay(0, 0).start()
    relay(0, 1).start()
    for part in range(parts):
        own_copy(part).start()

    starts, total = [], jnp.int32(0)
    for k in range(docs_ref.shape[0]):
        starts.append(total)
        total = total + docs_ref[k]

    def begins(at):
        begin = jnp.zeros(at.shape, jnp.int32)
        for start in starts:
            begin = jnp.where(at >= start, start, begin)
        return begin

    low, high = iota((CHUNK, CHUNK), 0), iota((CHUNK, CHUNK), 1)

    def make_off(c):
        base = pl.multiple_of(c * CHUNK, CHUNK)
        at = low + base
        off_ref[pl.ds(base, CHUNK), :] = (at - begins(at)).astype(F32)

    every(chunks, make_off)

    def small_landed(k):
        landed(small_all, small_recv, lax.rem(me + k, n)).wait_recv()

    every(n, small_landed, 1)

    def find_places():
        number = iota((n, tok), 0).astype(F32)
        named = []
        for i in range(n):
            target = jnp.concatenate([small_all[i].astype(F32)[8:, :]] * (n // 8), axis=0)
            named.append(jnp.where(target == number, 1.0, 0.0))
        earlier = jnp.where(low < high, 1.0, 0.0).astype(BF16)
        right = jnp.concatenate([earlier, jnp.ones((tok, tok), BF16)], axis=1)
        found = dot(jnp.concatenate(named, axis=0).astype(BF16), right)
        before = jnp.zeros((n, tok), F32)
        ranks = []
        for i in range(n):
            here = found[i * n : (i + 1) * n, :]
            ranks.append(here[:, :tok] + before)
            before = before + here[:, tok:]
        base = jnp.zeros((n, tok), F32)
        for d in range(n - 1):
            base = base + jnp.where(number > d, before[d : d + 1, :], 0.0)
        all_places = []
        for i in range(n):
            place = jnp.sum(named[i] * (ranks[i] + base), axis=0, keepdims=True)
            places[i : i + 1, :] = place
            all_places.append(place)
            coarse = jnp.floor(place * (1.0 / CHUNK))
            fine = place - coarse * CHUNK
            lanes = slice(i * tok, (i + 1) * tok)
            steps = small_all[i].astype(F32)[0:8, :]
            split = [jnp.where(coarse == c, steps, 0.0) for c in range(chunks)]
            dt_left[:, lanes] = jnp.concatenate(split, axis=0).astype(BF16)
            dt_right[:, lanes] = jnp.where(low.astype(F32) == fine, 1.0, 0.0).astype(BF16)

    find_places()

    row16 = iota((SUB, tok), 0).astype(F32).astype(BF16)
    one, none = jnp.ones((), BF16), jnp.zeros((), BF16)

    def make_sorter(b):
        first = lax.convert_element_type(b * SUB, F32)
        for i in range(n):
            rel = places[i : i + 1, :] - first
            rel = jnp.where((rel >= 0.0) & (rel < SUB), rel, -1.0)
            rel = jnp.broadcast_to(rel, (SUB, tok)).astype(BF16)
            hit = jnp.where(row16 == rel, one, none)
            sorter[pl.ds(pl.multiple_of(b * SUB, SUB), SUB), i * tok : (i + 1) * tok] = hit

    every(rows // SUB, make_sorter)

    def forward(k):
        landed(bc_all, gate_recv, lax.rem(me + k * plane, n)).wait_recv()
        relay(k, 0).start()
        relay(k, 1).start()

    every(n // plane, forward, 1)
    start_x(0)

    def crossed(k):
        landed(bc_all, gate_recv, lax.rem(across + k * plane, n)).wait_recv()
        relay(k, 2).start()

    every(n // plane, crossed)


    def decays():
        dts = dot_nt(dt_left[...], dt_right[...])
        lane = iota((8, CHUNK), 1)
        slot = iota((8, CHUNK), 0)
        rate = jnp.zeros((8, CHUNK), F32)
        for h in range(owned):
            rate = jnp.where(slot == h, rates[me * owned + h], rate)
        rate = jnp.concatenate([rate] * chunks, axis=0)
        upto = jnp.where(low <= high, 1.0, 0.0).astype(BF16)
        cum = -dot(dts.astype(BF16), upto) * rate
        last = jnp.broadcast_to(cum[:, CHUNK - 1 :], cum.shape)
        middle = 0.5 * last
        up = jnp.exp(cum - middle)
        down = jnp.exp(middle - cum) * dts
        gain = jnp.exp(middle)
        number = iota((8 * chunks, CHUNK), 0) // 8
        ends = number * CHUNK + CHUNK - 1
        goes_on = jnp.where(begins(ends) < number * CHUNK, 1.0, 0.0)
        carry = jnp.exp(last) * goes_on
        by_chunk[0] = up
        by_chunk[1] = down
        by_chunk[2] = gain
        by_chunk[3] = carry

    decays()

    head = iota((1, size), 1) // (size // local)

    def spread(columns, part):
        out = jnp.broadcast_to(columns[:, part * local : part * local + 1], (CHUNK, size))
        for h in range(1, local):
            at = part * local + h
            out = jnp.where(head == h, jnp.broadcast_to(columns[:, at : at + 1], (CHUNK, size)), out)
        return out

    def expand():
        pair = by_chunk[0].reshape(chunks, 8, CHUNK)[:, :4], by_chunk[1].reshape(chunks, 8, CHUNK)[:, :4]
        turned = jnp.concatenate(pair, axis=1).reshape(8 * chunks, CHUNK).T
        for c in range(chunks):
            at = slice(c * CHUNK, (c + 1) * CHUNK)
            for part in range(parts):
                rise[part, at, :] = spread(turned[:, 8 * c :], part)
                fall[part, at, :] = spread(turned[:, 8 * c + 4 :], part)

    expand()

    lane16 = [(iota((tok, LANES), 1) + j * LANES).astype(F32).astype(BF16) for j in range(SUB // LANES)]
    flipped = jnp.concatenate([places[...], jnp.zeros((tok - n, tok), F32)], axis=0).T
    flipped_coarse = jnp.floor(flipped * (1.0 / SUB))
    flipped_fine = flipped - flipped_coarse * SUB

    def make_columns():
        for i in range(n):
            at = slice(i * tok, (i + 1) * tok)
            columns[0, at, :] = jnp.broadcast_to(flipped_coarse[:, i : i + 1], (tok, LANES)).astype(BF16)
            columns[1, at, :] = jnp.broadcast_to(flipped_fine[:, i : i + 1], (tok, LANES)).astype(BF16)

    def make_unsorter(i):
        at = pl.ds(pl.multiple_of(i * tok, tok), tok)
        coarse, fine = columns[0, at, :], columns[1, at, :]
        for b in range(rows // SUB):
            rel = jnp.where(coarse == jnp.full((), b, BF16), fine, -one)
            for j in range(SUB // LANES):
                unsorter[at, b * SUB + j * LANES : b * SUB + (j + 1) * LANES] = jnp.where(lane16[j] == rel, one, none)

    make_columns()
    every(n, make_unsorter)

    def rest(k):
        for hop in (0, 2):
            owner = sibling - lax.rem(sibling, plane) + lax.rem(lax.rem(sibling, plane) + hop, plane)
            landed(bc_all, gate_recv, lax.rem(owner + k * plane, n)).wait_recv()

    every(n // plane, rest)

    start_x(1)

    for load in loads[3:]:
        load.wait()
    ub[0:PAD, :] = jnp.zeros((PAD, state2), F32)
    ux[0:PAD, :] = jnp.zeros((PAD, size), F32)
    block = plane * tok

    def gather(b):
        first = pl.multiple_of(b * block, block)
        here = dot(sorter[pl.ds(first, block), :], bc_all[...].reshape(rows, state2))
        ub[pl.ds(pl.multiple_of(first + PAD, PAD), block), :] = here

    every(rows // block, gather)

    gap = low - high

    def wide_bias(first, count):
        return jnp.concatenate([bias_v[pl.ds(first + i, 1), :] for i in range(count)], axis=1)

    def shared(c):
        base = pl.multiple_of(c * CHUNK, CHUNK)
        off = off_ref[pl.ds(base, CHUNK), :]
        off2 = jnp.concatenate([off] * (state2 // LANES), axis=1)
        bias = wide_bias(shared_at // LANES, state2 // LANES)
        act = fast_conv(ub[pl.ds(base, CHUNK + PAD), :], bc_taps[...], bias, off2)
        b_mat, c_mat = act[:, : state2 // 2], act[:, state2 // 2 :]
        scores = dot_nt(c_mat, b_mat)
        keep = (gap >= 0) & (gap.astype(F32) <= off)
        lhs[pl.ds(base, CHUNK), :CHUNK] = jnp.where(keep, scores, 0.0).astype(BF16)
        runs_in = jnp.where(off > low.astype(F32), c_mat.astype(F32), 0.0)
        lhs[pl.ds(base, CHUNK), CHUNK:] = runs_in.astype(BF16)
        runs_out = high[0:1, :].astype(F32) + off[CHUNK - 1 :, :] >= CHUNK - 1
        b_flip[pl.ds(base, CHUNK), :] = jnp.where(runs_out, b_mat.astype(F32).T, 0.0).astype(BF16)

    every(chunks // 4, lambda c: [shared(4 * c + i) for i in range(4)])

    def out_copy(part, owner):
        return remote(
            sent.at[part, owner], tile(out_ref, part, me), out_send.at[part, owner], out_recv.at[part, me], owner
        )

    def own_out(part):
        return pltpu.make_async_copy(sent.at[part, me], tile(out_ref, part, me), own_sem.at[parts + part])

    lane_head = iota((1, size), 1) // (size // local)

    def by_head(values):
        out = jnp.full((1, size), values[0], F32)
        for h in range(1, local):
            out = jnp.where(lane_head == h, values[h], out)
        return out

    for part in range(parts):

        def x_landed(k):
            source = lax.rem(me + k, n)
            slot = x_all.at[part, source]
            remote(slot, slot, gate_send.at[0], x_recv.at[part, source], source).wait_recv()

        own_copy(part).wait()
        every(n, x_landed, 1)

        def gather_x(b):
            first = pl.multiple_of(b * block, block)
            here = dot(sorter[pl.ds(first, block), :], x_all[part].reshape(rows, size))
            ux[pl.ds(pl.multiple_of(first + PAD, PAD), block), :] = here

        every(rows // block, gather_x)
        state[...] = jnp.zeros_like(state)
        skip = by_head([skips[me * owned + part * local + h] for h in range(local)])
        level = by_head([clips[me * owned + part * local + h] for h in range(local)])

        def chunk(c):
            base = pl.multiple_of(c * CHUNK, CHUNK)
            at = pl.ds(base, CHUNK)
            bias = bias_v[pl.ds(me * parts + part, 1), :]
            taps = x_taps[:, part * size : (part + 1) * size]
            wide = fast_conv(ux[pl.ds(base, CHUNK + PAD), :], taps, bias, off_ref[at, :]).astype(F32)
            scaled = (wide * fall[part, at, :]).astype(BF16)
            at8 = pl.ds(pl.multiple_of(c * 8, 8), 8)
            gains, carries = by_chunk[2, at8, :], by_chunk[3, at8, :]
            gain = by_head([gains[part * local + h : part * local + h + 1, :] for h in range(local)])
            carry = by_head([carries[part * local + h : part * local + h + 1, :] for h in range(local)])
            old = state[...]
            right = jnp.concatenate([scaled, (gain * old).astype(BF16)], axis=0)
            y = skip * wide + rise[part, at, :] * dot(lhs[at, :], right)
            ys[at, :] = jnp.clip(y, -level, level).astype(BF16)
            state[...] = carry * old + gain * dot(b_flip[at, :], scaled)

        every(chunks // 4, lambda c: [chunk(4 * c + i) for i in range(4)])

        def scatter(i):
            b = plane_at(i)
            first = pl.multiple_of(b * block, block)
            back = dot(unsorter[pl.ds(first, block), :], ys[...]).astype(BF16)
            for j in range(block // tok):
                owner = b * (block // tok) + j
                sent[part, owner] = back[j * tok : (j + 1) * tok, :]

                @pl.when(owner != me)
                def _():
                    out_copy(part, owner).start()

        every(rows // block, scatter)
        own_out(part).start()

    def finish(k):
        source = lax.rem(me + k, n)
        for part in range(parts):
            slot = tile(out_ref, part, source)
            remote(slot, slot, gate_send.at[0], out_recv.at[part, source], source).wait_recv()
            out_copy(part, source).wait_send()
            x_copy(part, source).wait_send()
        small_copy(k).wait_send()

    every(n, finish, 1)
    for part in range(parts):
        own_out(part).wait()

    def finish_aux(k):
        for hop in range(3):
            relay(k, hop).wait_send()

    every(n // plane, finish_aux)
    every(n // plane, lambda k: far(k).wait_send(), 1)


def fast_device(
    x_rows, bc_rows, step, route, doc_lengths, conv_weight, conv_bias, rate, skip, clip_level
):
    n = lax.axis_size("seq")
    tok, hp_width = x_rows.shape
    heads = step.shape[1]
    owned = heads // n
    width = hp_width // n
    state2 = bc_rows.shape[1]
    rows = tok * n
    parts = width // LANES
    size = LANES
    plane = 4
    chunks = rows // CHUNK
    bias = conv_bias.reshape(conv_bias.shape[0] // LANES, LANES)

    hbm = pl.BlockSpec(memory_space=pl.ANY)
    dma = pltpu.SemaphoreType.DMA
    return pl.pallas_call(
        functools.partial(fast_kernel, owned, parts, plane),
        out_shape=jax.ShapeDtypeStruct(x_rows.shape, BF16),
        in_specs=[pl.BlockSpec(memory_space=pltpu.SMEM)] * 4 + [hbm] * 6,
        out_specs=OUT_SPEC,
        scratch_shapes=[
            pltpu.VMEM((heads, tok), BF16),
            pltpu.VMEM((1, tok), jnp.int32),
            pltpu.VMEM((4, width), F32),
            pltpu.VMEM((4, state2), F32),
            pltpu.VMEM(bias.shape, F32),
            pltpu.VMEM((n, SMALL, tok), BF16),
            pltpu.VMEM((n, SMALL, tok), BF16),
            pltpu.VMEM((n, tok, state2), BF16),
            pltpu.VMEM((parts, n, tok, size), BF16),
            pltpu.VMEM((parts, n, tok, size), BF16),
            pltpu.VMEM((rows, LANES), F32),
            pltpu.VMEM((rows, rows), BF16),
            pltpu.VMEM((rows, rows), BF16),
            pltpu.VMEM((2, rows, LANES), BF16),
            pltpu.VMEM((8 * chunks, rows), BF16),
            pltpu.VMEM((CHUNK, rows), BF16),
            pltpu.VMEM((n, tok), F32),
            pltpu.VMEM((PAD + rows, state2), F32),
            pltpu.VMEM((PAD + rows, size), F32),
            pltpu.VMEM((rows, 2 * CHUNK), BF16),
            pltpu.VMEM((rows, CHUNK), BF16),
            pltpu.VMEM((parts, rows, size), F32),
            pltpu.VMEM((parts, rows, size), F32),
            pltpu.VMEM((4, 8 * chunks, CHUNK), F32),
            pltpu.VMEM((rows, size), BF16),
            pltpu.VMEM((state2 // 2, size), F32),
            dma((6,)),
            dma((n,)),
            dma((n,)),
            dma((n // plane,)),
            dma((n,)),
            dma((n // plane, 3)),
            dma((parts, n)),
            dma((parts, n)),
            dma((2 * parts,)),
            dma((parts, n)),
            dma((parts, n)),
        ],
        compiler_params=pltpu.CompilerParams(
            vmem_limit_bytes=48 * 1024 * 1024, collective_id=1, has_side_effects=True
        ),
    )(*[pltpu.with_memory_space_constraint(a, pltpu.HBM) for a in (
        doc_lengths, rate, skip, clip_level, x_rows, bc_rows, step.T, route.T, conv_weight, bias
    )])


def fits_fast(n, x_shape, heads, state2):
    width = x_shape[1] // n
    owned = heads // n
    return (
        n % 8 == 0 and n * x_shape[0] <= 2048 and x_shape[0] == LANES and width % LANES == 0 and state2 == 2 * CHUNK
        and owned == 4 and owned % (width // LANES) == 0 and 8 * n * LANES // CHUNK <= CHUNK
    )


def solution(mesh):
    placed = (
        P(("groups", "seq"), None),
        P(("groups", "seq"), None),
        P(("groups", "seq"), None),
        P(("groups", "seq"), None),
        P("groups"),
        P(),
        P(),
        P(),
        P(),
        P(),
    )

    def run(*arrays):
        x_rows, bc_rows, step = arrays[:3]
        fast = fits_fast(lax.axis_size("seq"), x_rows.shape, step.shape[1], bc_rows.shape[1])
        return (fast_device if fast else per_device)(*arrays)

    return jax.shard_map(
        run,
        mesh=mesh,
        in_specs=placed,
        out_specs=P(("groups", "seq"), None),
        check_vma=False,
    )
```

```python
import functools

import jax
import jax.numpy as jnp
from jax import lax
from jax.experimental import pallas as pl
from jax.experimental.pallas import tpu as pltpu
from jax.sharding import PartitionSpec as P

F32 = jnp.float32
BF16 = jnp.bfloat16
CHUNK = 128
LANES = 128
PAD = 8
SCHEDULE = {7:[(0,0)],1:[(0,1)],2:[(0,2),(0,3)],3:[(1,0),(1,1),(1,2),(1,3)]}
OUT_SPEC = pl.BlockSpec(memory_space=pl.ANY)


def dot(a, b):
    return jnp.dot(a, b, preferred_element_type=F32)


def dot_nt(a, b):
    return lax.dot_general(a, b, (((1,), (1,)), ((), ())), preferred_element_type=F32)


def dot_tn(a, b):
    return lax.dot_general(a, b, (((0,), (0,)), ((), ())), preferred_element_type=F32)


def find_places(aux_ref, ranks, place_row, place_col, heads):
    rows = ranks.shape[0]
    state2 = aux_ref.shape[2] - LANES
    low = lax.broadcasted_iota(jnp.int32, (LANES, LANES), 0)
    high = lax.broadcasted_iota(jnp.int32, (LANES, LANES), 1)
    earlier = jnp.where(low > high, 1.0, 0.0).astype(BF16)
    before = jnp.where(low < high, 1.0, 0.0).astype(BF16)
    shard = high.astype(F32)
    step = 4

    def named(b):
        target = aux_ref[b, :, state2 : state2 + LANES].astype(F32)[:, heads : heads + 1]
        return jnp.where(target == shard, 1.0, 0.0)

    def count(i, total):
        for j in range(step):
            b = i * step + j
            onehot = named(b)
            ranks[pl.ds(pl.multiple_of(b * LANES, LANES), LANES), :] = dot(earlier, onehot.astype(BF16)) + total
            total = total + jnp.sum(onehot, axis=0, keepdims=True)
        return total

    total = lax.fori_loop(0, rows // LANES // step, count, jnp.zeros((1, LANES), F32))
    total = jnp.broadcast_to(total, (8, LANES))
    coarse = jnp.floor(total * (1.0 / 64.0))
    fine = total - coarse * 64.0
    start = (dot(coarse.astype(BF16), before) * 64.0 + dot(fine.astype(BF16), before))[0:1, :]

    def rank(i, _):
        for j in range(step):
            b = i * step + j
            at = pl.multiple_of(b * LANES, LANES)
            found = named(b) * (ranks[pl.ds(at, LANES), :] + start)
            place = jnp.broadcast_to(jnp.sum(found, axis=1, keepdims=True), (LANES, LANES))
            place_col[pl.ds(at, LANES), :] = place
            place_row[:, pl.ds(at, LANES)] = place.T[0:8, :]
        return 0

    lax.fori_loop(0, rows // LANES // step, rank, 0)


def one_hot_sort(place_row, first, size):
    rows = place_row.shape[1]
    number = lax.broadcasted_iota(jnp.int32, (size, rows), 0).astype(F32)
    hit = place_row[0:1, :] - lax.convert_element_type(first, F32) == number
    return jnp.where(hit, 1.0, 0.0).astype(BF16)


def one_hot_unsort(place_col, first, size):
    rows = place_col.shape[0]
    number = lax.broadcasted_iota(jnp.int32, (size, rows), 1).astype(F32)
    place = place_col[pl.ds(first, size), :]
    hit = jnp.concatenate([place] * (rows // LANES), axis=1) == number
    return jnp.where(hit, 1.0, 0.0).astype(BF16)


def doc_begins(at, starts):
    begin = jnp.zeros((CHUNK, 1), jnp.int32)
    for start in starts:
        begin = jnp.where(at >= start, start, begin)
    return begin


def conv_silu(v, par, at, begin):
    acc = par[4:5, :] + par[0:1, :] * v[PAD:, :]
    for j in range(1, 4):
        keep = jnp.where(at - j >= begin, 1.0, 0.0)
        acc = acc + par[j : j + 1, :] * (v[PAD - j : PAD - j + CHUNK, :] * keep)
    return (acc / (1.0 + jnp.exp(-acc))).astype(BF16)


def shared_chunk(c, starts, ub, ds, bcpar_ref, rate_ref, bcs, ws, ent, tails, carries, owned):
    width = ent.shape[1]
    state_width = bcs.shape[1] // 2
    base = pl.multiple_of(c * CHUNK, CHUNK)
    at = lax.broadcasted_iota(jnp.int32, (CHUNK, 1), 0) + base
    begin = doc_begins(at, starts)
    begin_last = begin[CHUNK - 1 :, :]
    act = conv_silu(ub[pl.ds(base, CHUNK + PAD), :], bcpar_ref[...], at, begin)
    bcs[pl.ds(base, CHUNK), :] = act
    b_mat, c_mat = act[:, :state_width], act[:, state_width:]

    dt = ds[pl.ds(base, CHUNK), :]
    low = lax.broadcasted_iota(jnp.int32, (CHUNK, CHUNK), 0)
    high = lax.broadcasted_iota(jnp.int32, (CHUNK, CHUNK), 1)
    tri = jnp.where(low >= high, 1.0, 0.0).astype(BF16)
    cum = -dot(tri, dt.astype(BF16)) * rate_ref[...]
    shifted = (cum - jnp.log(jnp.maximum(dt, 1e-30))).T
    cum_last = cum[CHUNK - 1 :, :]
    scores = dot_nt(c_mat, b_mat)
    scores = jnp.where((low >= high) & (high + base >= begin), scores, 0.0)
    head = lax.broadcasted_iota(jnp.int32, (1, width), 1) // (width // owned)

    def expand(e):
        out = jnp.broadcast_to(e[:, 0:1], (e.shape[0], width))
        for h in range(1, owned):
            out = jnp.where(head == h, e[:, h : h + 1], out)
        return out

    for h in range(owned):
        decay = jnp.exp(cum[:, h : h + 1] - shifted[h : h + 1, :])
        ws[h, pl.ds(base, CHUNK), :] = (scores * decay).astype(BF16)
    ent[pl.ds(base, CHUNK), :] = expand(jnp.exp(cum) * jnp.where(begin < base, 1.0, 0.0))
    tail = jnp.exp(cum_last - cum) * dt * jnp.where(at >= begin_last, 1.0, 0.0)
    tails[pl.ds(base, CHUNK), :] = expand(tail)
    carry = expand(jnp.exp(cum_last) * jnp.where(begin_last < base, 1.0, 0.0))
    carries[c] = jnp.broadcast_to(carry, (8, width))


def scan_chunk(c, part, parts, starts, ux, xpar_ref, bcs, ws, ent, tails, carries, state, ys, owned):
    size = ux.shape[1]
    lanes = slice(part * size, (part + 1) * size)
    state_width = bcs.shape[1] // 2
    base = pl.multiple_of(c * CHUNK, CHUNK)
    at = lax.broadcasted_iota(jnp.int32, (CHUNK, 1), 0) + base
    begin = doc_begins(at, starts)
    x_mat = conv_silu(ux[pl.ds(base, CHUNK + PAD), :], xpar_ref[:, lanes], at, begin)
    x_wide = x_mat.astype(F32)
    bc = bcs[pl.ds(base, CHUNK), :]
    b_mat, c_mat = bc[:, :state_width], bc[:, state_width:]
    local = owned // parts
    head = lax.broadcasted_iota(jnp.int32, (1, size), 1) // (size // local)
    y = xpar_ref[5:6, lanes] * x_wide
    for h in range(local):
        mine = jnp.where(head == h, x_wide, 0.0).astype(BF16)
        y = y + dot(ws[part * local + h, pl.ds(base, CHUNK), :], mine)
    y = y + dot(c_mat, state[...].astype(BF16)) * ent[pl.ds(base, CHUNK), lanes]
    limit = xpar_ref[6:7, lanes]
    ys[pl.ds(base, CHUNK), :] = jnp.clip(y, -limit, limit).astype(BF16)
    scaled = (x_wide * tails[pl.ds(base, CHUNK), lanes]).astype(BF16)
    state[...] = carries[c][0:1, lanes] * state[...] + dot_tn(b_mat, scaled)


def kernel(
    owned, heads, parts, plane, docs_ref, rates, skips, clips, x_ref, aux_ref, weight_ref, bias_ref, out_ref,
    xpar_ref, bcpar_ref, rate_ref, pick_ref, aux_all, x_all, sent, keys, place_row, place_col, ub, ux, ds, bcs, ws, ent, tails, carries, ys, state,
    sorter, unsorter, gate_send, gate_recv, plane_send, x_send, x_recv, out_send, out_recv,
):
    n, tok = x_all.shape[1:3]
    rows, size = ys.shape
    state2 = bcs.shape[1]
    flat = len(x_ref.shape) == 2
    block = max(tok, min(512, (1 << 20) // rows))
    keep = sorter.shape[0] == rows
    me = lax.axis_index("seq")
    inside = lax.rem(me, plane)

    def remote(source, target, send, recv, peer):
        return pltpu.make_async_remote_copy(
            src_ref=source, dst_ref=target, send_sem=send, recv_sem=recv,
            device_id={"seq": peer}, device_id_type=pl.DeviceIdType.MESH,
        )

    def every(count, do, first=0):
        def turn(k, _):
            do(k)
            return 0

        lax.fori_loop(first, count, turn, 0)

    def tile(ref, part, owner):
        if flat:
            return ref.at[:, pl.ds(pl.multiple_of((owner * parts + part) * size, size), size)]
        return ref.at[owner]

    def own_lanes(ref):
        width = size * parts
        if width % LANES == 0:
            return ref[:, pl.ds(pl.multiple_of(me * width, LANES), width)]
        per = LANES // width
        wide = ref[:, pl.ds(pl.multiple_of(me // per * LANES, LANES), LANES)]
        picked = wide[:, :width]
        for i in range(1, per):
            picked = jnp.where(lax.rem(me, per) == i, wide[:, i * width : (i + 1) * width], picked)
        return picked

    def load_params():
        width = size * parts
        head = lax.broadcasted_iota(jnp.int32, (1, width), 1) // (width // owned)
        lane = lax.broadcasted_iota(jnp.int32, (1, LANES), 1)
        gain = level = jnp.zeros((1, width), F32)
        decay = jnp.zeros((1, LANES), F32)
        for h in range(owned):
            gain = jnp.where(head == h, skips[me * owned + h], gain)
            level = jnp.where(head == h, clips[me * owned + h], level)
            decay = jnp.where(lane == h, rates[me * owned + h], decay)
        xpar_ref[0:4, :] = own_lanes(weight_ref)
        xpar_ref[4:5, :] = own_lanes(bias_ref)
        xpar_ref[5:6, :] = gain
        xpar_ref[6:7, :] = level
        first = weight_ref.shape[1] - state2
        bcpar_ref[0:4, :] = weight_ref[:, first:]
        bcpar_ref[4:5, :] = bias_ref[:, first:]
        rate_ref[...] = decay
        source = lax.broadcasted_iota(jnp.int32, (LANES, LANES), 0)
        target = lax.broadcasted_iota(jnp.int32, (LANES, LANES), 1)
        hit = (source == target + me * owned) & (target < owned)
        pick_ref[...] = jnp.where(hit, 1.0, 0.0).astype(BF16)

    barrier = pltpu.get_barrier_semaphore()

    def greet(k):
        pl.semaphore_signal(
            barrier, inc=1, device_id={"seq": lax.rem(me + k, n)}, device_id_type=pl.DeviceIdType.MESH
        )

    every(n, greet, 1)
    pl.semaphore_wait(barrier, n - 1)

    def far(k):
        peer = lax.rem(me + k * plane, n)
        return remote(aux_ref, aux_all.at[me], gate_send.at[k], gate_recv.at[me], peer)

    def landed(ref, sems, slot):
        return remote(ref.at[slot], ref.at[slot], gate_send.at[0], sems.at[slot], slot)

    across = me - inside + lax.rem(inside + 2, plane)
    sibling = me + 1 - 2 * lax.rem(me, 2)

    def relay(k, hop):
        owner = lax.rem((across if hop == 2 else me) + k * plane, n)
        peer = across if hop == 0 else sibling
        return remote(aux_all.at[owner], aux_all.at[owner], plane_send.at[k, hop], gate_recv.at[owner], peer)

    def x_copy(part, k):
        peer = lax.rem(me + k, n)
        return remote(tile(x_ref, part, peer), x_all.at[part, me], x_send.at[part, k], x_recv.at[part, me], peer)

    every(n // plane, lambda k: far(k).start(), 1)
    aux_all[me] = aux_ref[...]
    relay(0, 0).start()
    relay(0, 1).start()

    def forward(k):
        landed(aux_all, gate_recv, lax.rem(me + k * plane, n)).wait_recv()
        relay(k, 0).start()
        relay(k, 1).start()

    every(n // plane, forward, 1)
    for part in range(parts):
        x_all[part, me] = tile(x_ref, part, me)[...]

    load_params()

    def crossed(k):
        landed(aux_all, gate_recv, lax.rem(across + k * plane, n)).wait_recv()
        relay(k, 2).start()

    every(n // plane, crossed)
    every(n, lambda k: x_copy(0, k).start(), 1)
    for part in range(1, parts):
        every(n, lambda k: x_copy(part, k).start(), 1)

    def rest(k):
        for hop in (0, 2):
            owner = sibling - lax.rem(sibling, plane) + lax.rem(lax.rem(sibling, plane) + hop, plane)
            landed(aux_all, gate_recv, lax.rem(owner + k * plane, n)).wait_recv()

    every(n // plane, rest)
    aux_rows = aux_all
    find_places(aux_rows, keys, place_row, place_col, heads)
    ub[0:PAD, :] = jnp.zeros((PAD, state2), F32)
    ux[0:PAD, :] = jnp.zeros((PAD, size), F32)

    def gather(b):
        first = pl.multiple_of(b * block, block)
        onehot = one_hot_sort(place_row, first, block)
        if keep:
            sorter[pl.ds(first, block), :] = onehot
        aux_here = dot(onehot, aux_all[...].reshape(rows, aux_all.shape[2]))
        ub[pl.ds(pl.multiple_of(first + PAD, PAD), block), :] = aux_here[:, :state2]
        ds[pl.ds(first, block), :] = dot(aux_here[:, state2:].astype(BF16), pick_ref[...])

    every(rows // block, gather)

    starts, total = [], jnp.int32(0)
    for k in range(docs_ref.shape[0]):
        starts.append(total)
        total = total + docs_ref[k]

    def shared(c):
        for i in range(4):
            shared_chunk(4 * c + i, starts, ub, ds, bcpar_ref, rate_ref, bcs, ws, ent, tails, carries, owned)

    every(rows // CHUNK // 4, shared)
    if keep:

        def prepare(b):
            first = pl.multiple_of(b * block, block)
            unsorter[pl.ds(first, block), :] = one_hot_unsort(place_col, first, block)

        every(rows // block, prepare)

    def out_copy(part, owner):
        return remote(
            sent.at[part, owner], tile(out_ref, part, me), out_send.at[part, owner], out_recv.at[part, me], owner
        )

    for part in range(parts):

        def x_landed(k):
            source = lax.rem(me + k, n)
            slot = x_all.at[part, source]
            remote(slot, slot, gate_send.at[0], x_recv.at[part, source], source).wait_recv()

        every(n, x_landed, 1)

        def gather_x(b):
            first = pl.multiple_of(b * block, block)
            onehot = sorter[pl.ds(first, block), :] if keep else one_hot_sort(place_row, first, block)
            x_here = dot(onehot, x_all[part].reshape(rows, size))
            ux[pl.ds(pl.multiple_of(first + PAD, PAD), block), :] = x_here

        every(rows // block, gather_x)
        state[...] = jnp.zeros_like(state)

        def chunk(c):
            for i in range(4):
                scan_chunk(
                    4 * c + i, part, parts, starts, ux, xpar_ref, bcs, ws, ent, tails, carries, state, ys, owned
                )

        every(rows // CHUNK // 4, chunk)

        def scatter(i):
            b = lax.rem(me * tok // block + 1 + i, rows // block)
            first = pl.multiple_of(b * block, block)
            onehot = unsorter[pl.ds(first, block), :] if keep else one_hot_unsort(place_col, first, block)
            back = dot(onehot, ys[...]).astype(BF16)
            for j in range(block // tok):
                owner = b * (block // tok) + j
                sent[part, owner] = back[j * tok : (j + 1) * tok, :]

                @pl.when(owner != me)
                def _():
                    out_copy(part, owner).start()

        every(rows // block, scatter)
        tile(out_ref, part, me)[...] = sent[part, me]

    def finish(k):
        source = lax.rem(me + k, n)
        for part in range(parts):
            slot = tile(out_ref, part, source)
            remote(slot, slot, gate_send.at[0], out_recv.at[part, source], source).wait_recv()
            out_copy(part, source).wait_send()
            x_copy(part, k).wait_send()

    every(n, finish, 1)

    def finish_aux(k):
        for hop in range(3):
            relay(k, hop).wait_send()

    every(n // plane, finish_aux)
    every(n // plane, lambda k: far(k).wait_send(), 1)


def per_device(
    x_rows, bc_rows, step, route, doc_lengths, conv_weight, conv_bias, rate, skip, clip_level
):
    seq_count = lax.axis_size("seq")
    tok_rows, hp_width = x_rows.shape
    heads = step.shape[1]
    owned = heads // seq_count
    width = hp_width // seq_count
    state2 = bc_rows.shape[1]
    rows = tok_rows * seq_count

    spare = jnp.zeros((tok_rows, LANES - heads - 1), BF16)
    aux = jnp.concatenate([bc_rows, step, route.astype(BF16), spare], axis=1)
    parts = 2 if width % (2 * LANES) == 0 and owned % 2 == 0 else 1
    plane = 4
    size = width // parts
    keep = rows if rows <= 2048 else 16
    flat = size % LANES == 0
    x_send = x_rows if flat else jnp.swapaxes(x_rows.reshape(tok_rows, seq_count, width), 0, 1)

    vmem = pl.BlockSpec(memory_space=pltpu.VMEM)
    dma = pltpu.SemaphoreType.DMA
    out = pl.pallas_call(
        functools.partial(kernel, owned, heads, parts, plane),
        out_shape=jax.ShapeDtypeStruct(x_send.shape, BF16),
        in_specs=[pl.BlockSpec(memory_space=pltpu.SMEM)] * 4 + [vmem] * 4,
        out_specs=vmem,
        scratch_shapes=[
            pltpu.VMEM((8, width), F32),
            pltpu.VMEM((8, state2), F32),
            pltpu.VMEM((1, LANES), F32),
            pltpu.VMEM((LANES, LANES), BF16),
            pltpu.VMEM((seq_count, tok_rows, aux.shape[1]), BF16),
            pltpu.VMEM((parts, seq_count, tok_rows, size), BF16),
            pltpu.VMEM((parts, seq_count, tok_rows, size), BF16),
            pltpu.VMEM((rows, LANES), F32),
            pltpu.VMEM((8, rows), F32),
            pltpu.VMEM((rows, LANES), F32),
            pltpu.VMEM((PAD + rows, state2), F32),
            pltpu.VMEM((PAD + rows, size), F32),
            pltpu.VMEM((rows, LANES), F32),
            pltpu.VMEM((rows, state2), BF16),
            pltpu.VMEM((owned, rows, CHUNK), BF16),
            pltpu.VMEM((rows, width), F32),
            pltpu.VMEM((rows, width), F32),
            pltpu.VMEM((rows // CHUNK, 8, width), F32),
            pltpu.VMEM((rows, size), BF16),
            pltpu.VMEM((state2 // 2, size), F32),
            pltpu.VMEM((keep, keep), BF16),
            pltpu.VMEM((keep, keep), BF16),
            dma((seq_count // plane,)),
            dma((seq_count,)),
            dma((seq_count // plane, 3)),
            dma((parts, seq_count)),
            dma((parts, seq_count)),
            dma((parts, seq_count)),
            dma((parts, seq_count)),
        ],
        compiler_params=pltpu.CompilerParams(
            vmem_limit_bytes=60 * 1024 * 1024, collective_id=0, has_side_effects=True
        ),
    )(doc_lengths, rate, skip, clip_level, x_send, aux, conv_weight, conv_bias[None, :])
    return out if flat else jnp.swapaxes(out, 0, 1).reshape(tok_rows, hp_width)


SUB = 256
SMALL = 16


def fast_conv(rows, taps, bias, off):
    size = off.shape[0]
    acc = bias + taps[0:1, :] * rows[PAD : PAD + size, :]
    for j in range(1, 4):
        back = rows[PAD - j : PAD - j + size, :]
        acc = acc + taps[j : j + 1, :] * jnp.where(off >= j, back, 0.0)
    half = 0.5 * acc
    return (half + half * jnp.tanh(half)).astype(BF16)


def fast_kernel(
    owned, parts, plane, docs_ref, rates, skips, clips, x_ref, bc_ref, step_ref, route_ref, weight_ref, bias_ref, out_ref,
    step_v, route_v, x_taps, bc_taps, bias_v, small_out, small_all, bc_all, x_all, sent, off_ref,
    sorter, unsorter, columns, dt_left, dt_right, places, ub, ux, lhs, b_flip, rise, fall, by_chunk, ys, state,
    load_sem, small_send, small_recv, gate_send, gate_recv, plane_send, x_send, x_recv, own_sem, out_send, out_recv,
):
    n, tok, state2 = bc_all.shape
    rows, size = ys.shape
    heads = step_v.shape[0]
    chunks = rows // CHUNK
    width = size * parts
    local = owned // parts
    me = lax.axis_index("seq")
    inside = lax.rem(me, plane)
    iota = functools.partial(lax.broadcasted_iota, jnp.int32)

    def remote(source, target, send, recv, peer):
        return pltpu.make_async_remote_copy(
            src_ref=source, dst_ref=target, send_sem=send, recv_sem=recv,
            device_id={"seq": peer}, device_id_type=pl.DeviceIdType.MESH,
        )

    def every(count, do, first=0):
        def turn(k, _):
            do(k)
            return 0

        lax.fori_loop(first, count, turn, 0)

    def tile(ref, part, owner):
        return ref.at[:, pl.ds(pl.multiple_of((owner * parts + part) * size, size), size)]

    barrier = pltpu.get_barrier_semaphore()

    def greet(k):
        pl.semaphore_signal(
            barrier, inc=1, device_id={"seq": lax.rem(me + k, n)}, device_id_type=pl.DeviceIdType.MESH
        )

    every(n, greet, 1)

    own = pl.ds(pl.multiple_of(me * width, width), width)
    shared_at = weight_ref.shape[1] - state2
    loads = [
        pltpu.make_async_copy(bc_ref, bc_all.at[me], load_sem.at[0]),
        pltpu.make_async_copy(step_ref, step_v, load_sem.at[1]),
        pltpu.make_async_copy(route_ref, route_v, load_sem.at[2]),
        pltpu.make_async_copy(weight_ref.at[:, own], x_taps, load_sem.at[3]),
        pltpu.make_async_copy(weight_ref.at[:, shared_at:], bc_taps, load_sem.at[4]),
        pltpu.make_async_copy(bias_ref, bias_v, load_sem.at[5]),
    ]
    for load in loads:
        load.start()

    loads[1].wait()
    loads[2].wait()
    wide_step = step_v[...].astype(F32)
    wide_route = jnp.broadcast_to(route_v[...].astype(F32), (8, tok))
    for p in range(n):
        mine = wide_step[p * owned : (p + 1) * owned, :]
        block = jnp.concatenate([mine, jnp.zeros((8 - owned, tok), F32), wide_route], axis=0)
        small_out[p] = block.astype(BF16)
    small_all[me] = small_out[me]
    loads[0].wait()

    pl.semaphore_wait(barrier, n - 1)

    low_plane = lax.rem(me // plane, 2)
    mate_turn, last_turn = 1 + 2 * low_plane, 3 - 2 * low_plane

    def far(step):
        owner = lax.rem(me + 2 * plane, n) if step == 2 else me
        peer = lax.rem(me + (2 if step == 0 else mate_turn) * plane, n)
        return remote(bc_all.at[owner], bc_all.at[owner], gate_send.at[step], gate_recv.at[owner], peer)

    def small_copy(k):
        peer = lax.rem(me + k, n)
        return remote(small_out.at[peer], small_all.at[me], small_send.at[k], small_recv.at[me], peer)

    def landed(ref, sems, slot):
        return remote(ref.at[slot], ref.at[slot], gate_send.at[0], sems.at[slot], slot)

    across = me - inside + lax.rem(inside + 2, plane)
    sibling = me + 1 - 2 * lax.rem(me, 2)

    def relay(k, hop):
        owner = lax.rem((across if hop == 2 else me) + k * plane, n)
        peer = across if hop == 0 else sibling
        return remote(bc_all.at[owner], bc_all.at[owner], plane_send.at[k, hop], gate_recv.at[owner], peer)

    def x_copy(part, peer):
        return remote(tile(x_ref, part, peer), x_all.at[part, me], x_send.at[part, peer], x_recv.at[part, me], peer)

    planes = n // plane
    half = planes // 2
    mine = me // plane

    def plane_at(i):
        turn = lax.rem(i, half)
        side = lax.rem(mine // half + 1 + i // half, 2)
        return side * half + lax.rem(lax.rem(mine, half) + turn + i // half, half)

    def own_copy(part):
        return pltpu.make_async_copy(tile(x_ref, part, me), x_all.at[part, me], own_sem.at[part])

    def start_at(moment):
        for part, turn in SCHEDULE.get(moment, ()):
            first = plane_at(jnp.int32(turn)) * plane

            def to_peer(j, part=part, first=first):
                peer = first + lax.rem(inside + 1 + j, plane)

                @pl.when(peer != me)
                def _():
                    x_copy(part, peer).start()

            every(plane, to_peer)

    every(n, lambda k: small_copy(k).start(), 1)
    far(0).start()
    far(1).start()
    relay(0, 0).start()
    relay(0, 1).start()
    start_at(0)
    for part in range(parts):
        own_copy(part).start()

    starts, total = [], jnp.int32(0)
    for k in range(docs_ref.shape[0]):
        starts.append(total)
        total = total + docs_ref[k]

    def begins(at):
        begin = jnp.zeros(at.shape, jnp.int32)
        for start in starts:
            begin = jnp.where(at >= start, start, begin)
        return begin

    low, high = iota((CHUNK, CHUNK), 0), iota((CHUNK, CHUNK), 1)

    def make_off(c):
        base = pl.multiple_of(c * CHUNK, CHUNK)
        at = low + base
        off_ref[pl.ds(base, CHUNK), :] = (at - begins(at)).astype(F32)

    every(chunks, make_off)

    def small_landed(k):
        landed(small_all, small_recv, lax.rem(me + k, n)).wait_recv()

    every(n, small_landed, 1)

    def find_places():
        number = iota((n, tok), 0).astype(F32)
        named = []
        for i in range(n):
            target = jnp.concatenate([small_all[i].astype(F32)[8:, :]] * (n // 8), axis=0)
            named.append(jnp.where(target == number, 1.0, 0.0))
        earlier = jnp.where(low < high, 1.0, 0.0).astype(BF16)
        right = jnp.concatenate([earlier, jnp.ones((tok, tok), BF16)], axis=1)
        found = dot(jnp.concatenate(named, axis=0).astype(BF16), right)
        before = jnp.zeros((n, tok), F32)
        ranks = []
        for i in range(n):
            here = found[i * n : (i + 1) * n, :]
            ranks.append(here[:, :tok] + before)
            before = before + here[:, tok:]
        base = jnp.zeros((n, tok), F32)
        for d in range(n - 1):
            base = base + jnp.where(number > d, before[d : d + 1, :], 0.0)
        all_places = []
        for i in range(n):
            place = jnp.sum(named[i] * (ranks[i] + base), axis=0, keepdims=True)
            places[i : i + 1, :] = place
            all_places.append(place)
            coarse = jnp.floor(place * (1.0 / CHUNK))
            fine = place - coarse * CHUNK
            lanes = slice(i * tok, (i + 1) * tok)
            steps = small_all[i].astype(F32)[0:8, :]
            split = [jnp.where(coarse == c, steps, 0.0) for c in range(chunks)]
            dt_left[:, lanes] = jnp.concatenate(split, axis=0).astype(BF16)
            dt_right[:, lanes] = jnp.where(low.astype(F32) == fine, 1.0, 0.0).astype(BF16)

    find_places()

    start_at(6)
    row16 = iota((SUB, tok), 0).astype(F32).astype(BF16)
    one, none = jnp.ones((), BF16), jnp.zeros((), BF16)

    def make_sorter(b):
        first = lax.convert_element_type(b * SUB, F32)
        for i in range(n):
            rel = places[i : i + 1, :] - first
            rel = jnp.where((rel >= 0.0) & (rel < SUB), rel, -1.0)
            rel = jnp.broadcast_to(rel, (SUB, tok)).astype(BF16)
            hit = jnp.where(row16 == rel, one, none)
            sorter[pl.ds(pl.multiple_of(b * SUB, SUB), SUB), i * tok : (i + 1) * tok] = hit

    every(rows // SUB, make_sorter)

    start_at(8)
    def forward(k):
        landed(bc_all, gate_recv, lax.rem(me + k * plane, n)).wait_recv()
        if isinstance(k, int):
            far(2).start()
        relay(k, 0).start()
        relay(k, 1).start()

    forward(2)
    forward(mate_turn)
    start_at(7)
    forward(last_turn)
    start_at(1)

    def crossed(k):
        landed(bc_all, gate_recv, lax.rem(across + k * plane, n)).wait_recv()
        relay(k, 2).start()

    for k in (0, 2, mate_turn, last_turn):
        crossed(k)

    start_at(2)

    def decays():
        dts = dot_nt(dt_left[...], dt_right[...])
        lane = iota((8, CHUNK), 1)
        slot = iota((8, CHUNK), 0)
        rate = jnp.zeros((8, CHUNK), F32)
        for h in range(owned):
            rate = jnp.where(slot == h, rates[me * owned + h], rate)
        rate = jnp.concatenate([rate] * chunks, axis=0)
        upto = jnp.where(low <= high, 1.0, 0.0).astype(BF16)
        cum = -dot(dts.astype(BF16), upto) * rate
        last = jnp.broadcast_to(cum[:, CHUNK - 1 :], cum.shape)
        middle = 0.5 * last
        up = jnp.exp(cum - middle)
        down = jnp.exp(middle - cum) * dts
        gain = jnp.exp(middle)
        number = iota((8 * chunks, CHUNK), 0) // 8
        ends = number * CHUNK + CHUNK - 1
        goes_on = jnp.where(begins(ends) < number * CHUNK, 1.0, 0.0)
        carry = jnp.exp(last) * goes_on
        by_chunk[0] = up
        by_chunk[1] = down
        by_chunk[2] = gain
        by_chunk[3] = carry

    decays()

    head = iota((1, size), 1) // (size // local)

    def spread(columns, part):
        out = jnp.broadcast_to(columns[:, part * local : part * local + 1], (CHUNK, size))
        for h in range(1, local):
            at = part * local + h
            out = jnp.where(head == h, jnp.broadcast_to(columns[:, at : at + 1], (CHUNK, size)), out)
        return out

    def expand():
        pair = by_chunk[0].reshape(chunks, 8, CHUNK)[:, :4], by_chunk[1].reshape(chunks, 8, CHUNK)[:, :4]
        turned = jnp.concatenate(pair, axis=1).reshape(8 * chunks, CHUNK).T
        for c in range(chunks):
            at = slice(c * CHUNK, (c + 1) * CHUNK)
            for part in range(parts):
                rise[part, at, :] = spread(turned[:, 8 * c :], part)
                fall[part, at, :] = spread(turned[:, 8 * c + 4 :], part)

    expand()

    lane16 = [(iota((tok, LANES), 1) + j * LANES).astype(F32).astype(BF16) for j in range(SUB // LANES)]
    flipped = jnp.concatenate([places[...], jnp.zeros((tok - n, tok), F32)], axis=0).T
    flipped_coarse = jnp.floor(flipped * (1.0 / SUB))
    flipped_fine = flipped - flipped_coarse * SUB

    def make_columns():
        for i in range(n):
            at = slice(i * tok, (i + 1) * tok)
            columns[0, at, :] = jnp.broadcast_to(flipped_coarse[:, i : i + 1], (tok, LANES)).astype(BF16)
            columns[1, at, :] = jnp.broadcast_to(flipped_fine[:, i : i + 1], (tok, LANES)).astype(BF16)

    def make_unsorter(i):
        at = pl.ds(pl.multiple_of(i * tok, tok), tok)
        coarse, fine = columns[0, at, :], columns[1, at, :]
        for b in range(rows // SUB):
            rel = jnp.where(coarse == jnp.full((), b, BF16), fine, -one)
            for j in range(SUB // LANES):
                unsorter[at, b * SUB + j * LANES : b * SUB + (j + 1) * LANES] = jnp.where(lane16[j] == rel, one, none)

    start_at(9)
    make_columns()
    every(n, make_unsorter)

    def rest(k):
        for hop in (0, 2):
            owner = sibling - lax.rem(sibling, plane) + lax.rem(lax.rem(sibling, plane) + hop, plane)
            landed(bc_all, gate_recv, lax.rem(owner + k * plane, n)).wait_recv()

    every(n // plane, rest)

    start_at(3)

    for load in loads[3:]:
        load.wait()
    ub[0:PAD, :] = jnp.zeros((PAD, state2), F32)
    ux[0:PAD, :] = jnp.zeros((PAD, size), F32)
    block = plane * tok

    def gather(b):
        first = pl.multiple_of(b * block, block)
        here = dot(sorter[pl.ds(first, block), :], bc_all[...].reshape(rows, state2))
        ub[pl.ds(pl.multiple_of(first + PAD, PAD), block), :] = here

    every(rows // block, gather)
    start_at(4)

    gap = low - high

    def wide_bias(first, count):
        return jnp.concatenate([bias_v[pl.ds(first + i, 1), :] for i in range(count)], axis=1)

    def shared(c):
        base = pl.multiple_of(c * CHUNK, CHUNK)
        off = off_ref[pl.ds(base, CHUNK), :]
        off2 = jnp.concatenate([off] * (state2 // LANES), axis=1)
        bias = wide_bias(shared_at // LANES, state2 // LANES)
        act = fast_conv(ub[pl.ds(base, CHUNK + PAD), :], bc_taps[...], bias, off2)
        b_mat, c_mat = act[:, : state2 // 2], act[:, state2 // 2 :]
        scores = dot_nt(c_mat, b_mat)
        keep = (gap >= 0) & (gap.astype(F32) <= off)
        lhs[pl.ds(base, CHUNK), :CHUNK] = jnp.where(keep, scores, 0.0).astype(BF16)
        runs_in = jnp.where(off > low.astype(F32), c_mat.astype(F32), 0.0)
        lhs[pl.ds(base, CHUNK), CHUNK:] = runs_in.astype(BF16)
        runs_out = high[0:1, :].astype(F32) + off[CHUNK - 1 :, :] >= CHUNK - 1
        b_flip[pl.ds(base, CHUNK), :] = jnp.where(runs_out, b_mat.astype(F32).T, 0.0).astype(BF16)

    every(chunks // 4, lambda c: [shared(4 * c + i) for i in range(4)])
    start_at(5)

    def out_copy(part, owner):
        return remote(
            sent.at[part, owner], tile(out_ref, part, me), out_send.at[part, owner], out_recv.at[part, me], owner
        )

    def own_out(part):
        return pltpu.make_async_copy(sent.at[part, me], tile(out_ref, part, me), own_sem.at[parts + part])

    lane_head = iota((1, size), 1) // (size // local)

    def by_head(values):
        out = jnp.full((1, size), values[0], F32)
        for h in range(1, local):
            out = jnp.where(lane_head == h, values[h], out)
        return out

    for part in range(parts):

        def x_landed(k):
            source = lax.rem(me + k, n)
            slot = x_all.at[part, source]
            remote(slot, slot, gate_send.at[0], x_recv.at[part, source], source).wait_recv()

        own_copy(part).wait()
        every(n, x_landed, 1)

        def gather_x(b):
            first = pl.multiple_of(b * block, block)
            here = dot(sorter[pl.ds(first, block), :], x_all[part].reshape(rows, size))
            ux[pl.ds(pl.multiple_of(first + PAD, PAD), block), :] = here

        every(rows // block, gather_x)
        state[...] = jnp.zeros_like(state)
        skip = by_head([skips[me * owned + part * local + h] for h in range(local)])
        level = by_head([clips[me * owned + part * local + h] for h in range(local)])

        def chunk(c):
            base = pl.multiple_of(c * CHUNK, CHUNK)
            at = pl.ds(base, CHUNK)
            bias = bias_v[pl.ds(me * parts + part, 1), :]
            taps = x_taps[:, part * size : (part + 1) * size]
            wide = fast_conv(ux[pl.ds(base, CHUNK + PAD), :], taps, bias, off_ref[at, :]).astype(F32)
            scaled = (wide * fall[part, at, :]).astype(BF16)
            at8 = pl.ds(pl.multiple_of(c * 8, 8), 8)
            gains, carries = by_chunk[2, at8, :], by_chunk[3, at8, :]
            gain = by_head([gains[part * local + h : part * local + h + 1, :] for h in range(local)])
            carry = by_head([carries[part * local + h : part * local + h + 1, :] for h in range(local)])
            old = state[...]
            right = jnp.concatenate([scaled, (gain * old).astype(BF16)], axis=0)
            y = skip * wide + rise[part, at, :] * dot(lhs[at, :], right)
            ys[at, :] = jnp.clip(y, -level, level).astype(BF16)
            state[...] = carry * old + gain * dot(b_flip[at, :], scaled)

        every(chunks // 4, lambda c: [chunk(4 * c + i) for i in range(4)])

        def scatter(i):
            b = plane_at(i)
            first = pl.multiple_of(b * block, block)
            back = dot(unsorter[pl.ds(first, block), :], ys[...]).astype(BF16)
            for j in range(block // tok):
                owner = b * (block // tok) + j
                sent[part, owner] = back[j * tok : (j + 1) * tok, :]

                @pl.when(owner != me)
                def _():
                    out_copy(part, owner).start()

        every(rows // block, scatter)
        own_out(part).start()

    def finish(k):
        source = lax.rem(me + k, n)
        for part in range(parts):
            slot = tile(out_ref, part, source)
            remote(slot, slot, gate_send.at[0], out_recv.at[part, source], source).wait_recv()
            out_copy(part, source).wait_send()
            x_copy(part, source).wait_send()
        small_copy(k).wait_send()

    every(n, finish, 1)
    for part in range(parts):
        own_out(part).wait()

    def finish_aux(k):
        for hop in range(3):
            relay(k, hop).wait_send()

    every(n // plane, finish_aux)
    for step in range(3):
        far(step).wait_send()


def fast_device(
    x_rows, bc_rows, step, route, doc_lengths, conv_weight, conv_bias, rate, skip, clip_level
):
    n = lax.axis_size("seq")
    tok, hp_width = x_rows.shape
    heads = step.shape[1]
    owned = heads // n
    width = hp_width // n
    state2 = bc_rows.shape[1]
    rows = tok * n
    parts = width // LANES
    size = LANES
    plane = 4
    chunks = rows // CHUNK
    bias = conv_bias.reshape(conv_bias.shape[0] // LANES, LANES)

    hbm = pl.BlockSpec(memory_space=pl.ANY)
    dma = pltpu.SemaphoreType.DMA
    return pl.pallas_call(
        functools.partial(fast_kernel, owned, parts, plane),
        out_shape=jax.ShapeDtypeStruct(x_rows.shape, BF16),
        in_specs=[pl.BlockSpec(memory_space=pltpu.SMEM)] * 4 + [hbm] * 6,
        out_specs=OUT_SPEC,
        scratch_shapes=[
            pltpu.VMEM((heads, tok), BF16),
            pltpu.VMEM((1, tok), jnp.int32),
            pltpu.VMEM((4, width), F32),
            pltpu.VMEM((4, state2), F32),
            pltpu.VMEM(bias.shape, F32),
            pltpu.VMEM((n, SMALL, tok), BF16),
            pltpu.VMEM((n, SMALL, tok), BF16),
            pltpu.VMEM((n, tok, state2), BF16),
            pltpu.VMEM((parts, n, tok, size), BF16),
            pltpu.VMEM((parts, n, tok, size), BF16),
            pltpu.VMEM((rows, LANES), F32),
            pltpu.VMEM((rows, rows), BF16),
            pltpu.VMEM((rows, rows), BF16),
            pltpu.VMEM((2, rows, LANES), BF16),
            pltpu.VMEM((8 * chunks, rows), BF16),
            pltpu.VMEM((CHUNK, rows), BF16),
            pltpu.VMEM((n, tok), F32),
            pltpu.VMEM((PAD + rows, state2), F32),
            pltpu.VMEM((PAD + rows, size), F32),
            pltpu.VMEM((rows, 2 * CHUNK), BF16),
            pltpu.VMEM((rows, CHUNK), BF16),
            pltpu.VMEM((parts, rows, size), F32),
            pltpu.VMEM((parts, rows, size), F32),
            pltpu.VMEM((4, 8 * chunks, CHUNK), F32),
            pltpu.VMEM((rows, size), BF16),
            pltpu.VMEM((state2 // 2, size), F32),
            dma((6,)),
            dma((n,)),
            dma((n,)),
            dma((n // plane,)),
            dma((n,)),
            dma((n // plane, 3)),
            dma((parts, n)),
            dma((parts, n)),
            dma((2 * parts,)),
            dma((parts, n)),
            dma((parts, n)),
        ],
        compiler_params=pltpu.CompilerParams(
            vmem_limit_bytes=48 * 1024 * 1024, collective_id=1, has_side_effects=True
        ),
    )(*[pltpu.with_memory_space_constraint(a, pltpu.HBM) for a in (
        doc_lengths, rate, skip, clip_level, x_rows, bc_rows, step.T, route.T, conv_weight, bias
    )])


def fits_fast(n, x_shape, heads, state2):
    width = x_shape[1] // n
    owned = heads // n
    return (
        n == 16 and n * x_shape[0] <= 2048 and x_shape[0] == LANES and width % LANES == 0 and state2 == 2 * CHUNK
        and owned == 4 and owned % (width // LANES) == 0 and 8 * n * LANES // CHUNK <= CHUNK
    )


def solution(mesh):
    placed = (
        P(("groups", "seq"), None),
        P(("groups", "seq"), None),
        P(("groups", "seq"), None),
        P(("groups", "seq"), None),
        P("groups"),
        P(),
        P(),
        P(),
        P(),
        P(),
    )

    def run(*arrays):
        x_rows, bc_rows, step = arrays[:3]
        fast = fits_fast(lax.axis_size("seq"), x_rows.shape, step.shape[1], bc_rows.shape[1])
        return (fast_device if fast else per_device)(*arrays)

    return jax.shard_map(
        run,
        mesh=mesh,
        in_specs=placed,
        out_specs=P(("groups", "seq"), None),
        check_vma=False,
    )
```

```python
import functools

import jax
import jax.numpy as jnp
from jax import lax
from jax.experimental import pallas as pl
from jax.experimental.pallas import tpu as pltpu
from jax.sharding import PartitionSpec as P

F32 = jnp.float32
BF16 = jnp.bfloat16
CHUNK = 128
LANES = 128
PAD = 8
SCHEDULE = {
    0: ((0, 0, 0, 2),),
    7: ((0, 0, 2, 4),),
    1: ((0, 1),),
    2: ((0, 2), (0, 3)),
    3: ((1, 0), (1, 1), (1, 2), (1, 3)),
}
OUT_SPEC = pl.BlockSpec(memory_space=pl.ANY)


def dot(a, b):
    return jnp.dot(a, b, preferred_element_type=F32)


def dot_nt(a, b):
    return lax.dot_general(a, b, (((1,), (1,)), ((), ())), preferred_element_type=F32)


def dot_tn(a, b):
    return lax.dot_general(a, b, (((0,), (0,)), ((), ())), preferred_element_type=F32)


def find_places(aux_ref, ranks, place_row, place_col, heads):
    rows = ranks.shape[0]
    state2 = aux_ref.shape[2] - LANES
    low = lax.broadcasted_iota(jnp.int32, (LANES, LANES), 0)
    high = lax.broadcasted_iota(jnp.int32, (LANES, LANES), 1)
    earlier = jnp.where(low > high, 1.0, 0.0).astype(BF16)
    before = jnp.where(low < high, 1.0, 0.0).astype(BF16)
    shard = high.astype(F32)
    step = 4

    def named(b):
        target = aux_ref[b, :, state2 : state2 + LANES].astype(F32)[:, heads : heads + 1]
        return jnp.where(target == shard, 1.0, 0.0)

    def count(i, total):
        for j in range(step):
            b = i * step + j
            onehot = named(b)
            ranks[pl.ds(pl.multiple_of(b * LANES, LANES), LANES), :] = dot(earlier, onehot.astype(BF16)) + total
            total = total + jnp.sum(onehot, axis=0, keepdims=True)
        return total

    total = lax.fori_loop(0, rows // LANES // step, count, jnp.zeros((1, LANES), F32))
    total = jnp.broadcast_to(total, (8, LANES))
    coarse = jnp.floor(total * (1.0 / 64.0))
    fine = total - coarse * 64.0
    start = (dot(coarse.astype(BF16), before) * 64.0 + dot(fine.astype(BF16), before))[0:1, :]

    def rank(i, _):
        for j in range(step):
            b = i * step + j
            at = pl.multiple_of(b * LANES, LANES)
            found = named(b) * (ranks[pl.ds(at, LANES), :] + start)
            place = jnp.broadcast_to(jnp.sum(found, axis=1, keepdims=True), (LANES, LANES))
            place_col[pl.ds(at, LANES), :] = place
            place_row[:, pl.ds(at, LANES)] = place.T[0:8, :]
        return 0

    lax.fori_loop(0, rows // LANES // step, rank, 0)


def one_hot_sort(place_row, first, size):
    rows = place_row.shape[1]
    number = lax.broadcasted_iota(jnp.int32, (size, rows), 0).astype(F32)
    hit = place_row[0:1, :] - lax.convert_element_type(first, F32) == number
    return jnp.where(hit, 1.0, 0.0).astype(BF16)


def one_hot_unsort(place_col, first, size):
    rows = place_col.shape[0]
    number = lax.broadcasted_iota(jnp.int32, (size, rows), 1).astype(F32)
    place = place_col[pl.ds(first, size), :]
    hit = jnp.concatenate([place] * (rows // LANES), axis=1) == number
    return jnp.where(hit, 1.0, 0.0).astype(BF16)


def doc_begins(at, starts):
    begin = jnp.zeros((CHUNK, 1), jnp.int32)
    for start in starts:
        begin = jnp.where(at >= start, start, begin)
    return begin


def conv_silu(v, par, at, begin):
    acc = par[4:5, :] + par[0:1, :] * v[PAD:, :]
    for j in range(1, 4):
        keep = jnp.where(at - j >= begin, 1.0, 0.0)
        acc = acc + par[j : j + 1, :] * (v[PAD - j : PAD - j + CHUNK, :] * keep)
    return (acc / (1.0 + jnp.exp(-acc))).astype(BF16)


def shared_chunk(c, starts, ub, ds, bcpar_ref, rate_ref, bcs, ws, ent, tails, carries, owned):
    width = ent.shape[1]
    state_width = bcs.shape[1] // 2
    base = pl.multiple_of(c * CHUNK, CHUNK)
    at = lax.broadcasted_iota(jnp.int32, (CHUNK, 1), 0) + base
    begin = doc_begins(at, starts)
    begin_last = begin[CHUNK - 1 :, :]
    act = conv_silu(ub[pl.ds(base, CHUNK + PAD), :], bcpar_ref[...], at, begin)
    bcs[pl.ds(base, CHUNK), :] = act
    b_mat, c_mat = act[:, :state_width], act[:, state_width:]

    dt = ds[pl.ds(base, CHUNK), :]
    low = lax.broadcasted_iota(jnp.int32, (CHUNK, CHUNK), 0)
    high = lax.broadcasted_iota(jnp.int32, (CHUNK, CHUNK), 1)
    tri = jnp.where(low >= high, 1.0, 0.0).astype(BF16)
    cum = -dot(tri, dt.astype(BF16)) * rate_ref[...]
    shifted = (cum - jnp.log(jnp.maximum(dt, 1e-30))).T
    cum_last = cum[CHUNK - 1 :, :]
    scores = dot_nt(c_mat, b_mat)
    scores = jnp.where((low >= high) & (high + base >= begin), scores, 0.0)
    head = lax.broadcasted_iota(jnp.int32, (1, width), 1) // (width // owned)

    def expand(e):
        out = jnp.broadcast_to(e[:, 0:1], (e.shape[0], width))
        for h in range(1, owned):
            out = jnp.where(head == h, e[:, h : h + 1], out)
        return out

    for h in range(owned):
        decay = jnp.exp(cum[:, h : h + 1] - shifted[h : h + 1, :])
        ws[h, pl.ds(base, CHUNK), :] = (scores * decay).astype(BF16)
    ent[pl.ds(base, CHUNK), :] = expand(jnp.exp(cum) * jnp.where(begin < base, 1.0, 0.0))
    tail = jnp.exp(cum_last - cum) * dt * jnp.where(at >= begin_last, 1.0, 0.0)
    tails[pl.ds(base, CHUNK), :] = expand(tail)
    carry = expand(jnp.exp(cum_last) * jnp.where(begin_last < base, 1.0, 0.0))
    carries[c] = jnp.broadcast_to(carry, (8, width))


def scan_chunk(c, part, parts, starts, ux, xpar_ref, bcs, ws, ent, tails, carries, state, ys, owned):
    size = ux.shape[1]
    lanes = slice(part * size, (part + 1) * size)
    state_width = bcs.shape[1] // 2
    base = pl.multiple_of(c * CHUNK, CHUNK)
    at = lax.broadcasted_iota(jnp.int32, (CHUNK, 1), 0) + base
    begin = doc_begins(at, starts)
    x_mat = conv_silu(ux[pl.ds(base, CHUNK + PAD), :], xpar_ref[:, lanes], at, begin)
    x_wide = x_mat.astype(F32)
    bc = bcs[pl.ds(base, CHUNK), :]
    b_mat, c_mat = bc[:, :state_width], bc[:, state_width:]
    local = owned // parts
    head = lax.broadcasted_iota(jnp.int32, (1, size), 1) // (size // local)
    y = xpar_ref[5:6, lanes] * x_wide
    for h in range(local):
        mine = jnp.where(head == h, x_wide, 0.0).astype(BF16)
        y = y + dot(ws[part * local + h, pl.ds(base, CHUNK), :], mine)
    y = y + dot(c_mat, state[...].astype(BF16)) * ent[pl.ds(base, CHUNK), lanes]
    limit = xpar_ref[6:7, lanes]
    ys[pl.ds(base, CHUNK), :] = jnp.clip(y, -limit, limit).astype(BF16)
    scaled = (x_wide * tails[pl.ds(base, CHUNK), lanes]).astype(BF16)
    state[...] = carries[c][0:1, lanes] * state[...] + dot_tn(b_mat, scaled)


def kernel(
    owned, heads, parts, plane, docs_ref, rates, skips, clips, x_ref, aux_ref, weight_ref, bias_ref, out_ref,
    xpar_ref, bcpar_ref, rate_ref, pick_ref, aux_all, x_all, sent, keys, place_row, place_col, ub, ux, ds, bcs, ws, ent, tails, carries, ys, state,
    sorter, unsorter, gate_send, gate_recv, plane_send, x_send, x_recv, out_send, out_recv,
):
    n, tok = x_all.shape[1:3]
    rows, size = ys.shape
    state2 = bcs.shape[1]
    flat = len(x_ref.shape) == 2
    block = max(tok, min(512, (1 << 20) // rows))
    keep = sorter.shape[0] == rows
    me = lax.axis_index("seq")
    inside = lax.rem(me, plane)

    def remote(source, target, send, recv, peer):
        return pltpu.make_async_remote_copy(
            src_ref=source, dst_ref=target, send_sem=send, recv_sem=recv,
            device_id={"seq": peer}, device_id_type=pl.DeviceIdType.MESH,
        )

    def every(count, do, first=0):
        def turn(k, _):
            do(k)
            return 0

        lax.fori_loop(first, count, turn, 0)

    def tile(ref, part, owner):
        if flat:
            return ref.at[:, pl.ds(pl.multiple_of((owner * parts + part) * size, size), size)]
        return ref.at[owner]

    def own_lanes(ref):
        width = size * parts
        if width % LANES == 0:
            return ref[:, pl.ds(pl.multiple_of(me * width, LANES), width)]
        per = LANES // width
        wide = ref[:, pl.ds(pl.multiple_of(me // per * LANES, LANES), LANES)]
        picked = wide[:, :width]
        for i in range(1, per):
            picked = jnp.where(lax.rem(me, per) == i, wide[:, i * width : (i + 1) * width], picked)
        return picked

    def load_params():
        width = size * parts
        head = lax.broadcasted_iota(jnp.int32, (1, width), 1) // (width // owned)
        lane = lax.broadcasted_iota(jnp.int32, (1, LANES), 1)
        gain = level = jnp.zeros((1, width), F32)
        decay = jnp.zeros((1, LANES), F32)
        for h in range(owned):
            gain = jnp.where(head == h, skips[me * owned + h], gain)
            level = jnp.where(head == h, clips[me * owned + h], level)
            decay = jnp.where(lane == h, rates[me * owned + h], decay)
        xpar_ref[0:4, :] = own_lanes(weight_ref)
        xpar_ref[4:5, :] = own_lanes(bias_ref)
        xpar_ref[5:6, :] = gain
        xpar_ref[6:7, :] = level
        first = weight_ref.shape[1] - state2
        bcpar_ref[0:4, :] = weight_ref[:, first:]
        bcpar_ref[4:5, :] = bias_ref[:, first:]
        rate_ref[...] = decay
        source = lax.broadcasted_iota(jnp.int32, (LANES, LANES), 0)
        target = lax.broadcasted_iota(jnp.int32, (LANES, LANES), 1)
        hit = (source == target + me * owned) & (target < owned)
        pick_ref[...] = jnp.where(hit, 1.0, 0.0).astype(BF16)

    barrier = pltpu.get_barrier_semaphore()

    def greet(k):
        pl.semaphore_signal(
            barrier, inc=1, device_id={"seq": lax.rem(me + k, n)}, device_id_type=pl.DeviceIdType.MESH
        )

    every(n, greet, 1)
    pl.semaphore_wait(barrier, n - 1)

    def far(k):
        peer = lax.rem(me + k * plane, n)
        return remote(aux_ref, aux_all.at[me], gate_send.at[k], gate_recv.at[me], peer)

    def landed(ref, sems, slot):
        return remote(ref.at[slot], ref.at[slot], gate_send.at[0], sems.at[slot], slot)

    across = me - inside + lax.rem(inside + 2, plane)
    sibling = me + 1 - 2 * lax.rem(me, 2)

    def relay(k, hop):
        owner = lax.rem((across if hop == 2 else me) + k * plane, n)
        peer = across if hop == 0 else sibling
        return remote(aux_all.at[owner], aux_all.at[owner], plane_send.at[k, hop], gate_recv.at[owner], peer)

    def x_copy(part, k):
        peer = lax.rem(me + k, n)
        return remote(tile(x_ref, part, peer), x_all.at[part, me], x_send.at[part, k], x_recv.at[part, me], peer)

    every(n // plane, lambda k: far(k).start(), 1)
    aux_all[me] = aux_ref[...]
    relay(0, 0).start()
    relay(0, 1).start()

    def forward(k):
        landed(aux_all, gate_recv, lax.rem(me + k * plane, n)).wait_recv()
        relay(k, 0).start()
        relay(k, 1).start()

    every(n // plane, forward, 1)
    for part in range(parts):
        x_all[part, me] = tile(x_ref, part, me)[...]

    load_params()

    def crossed(k):
        landed(aux_all, gate_recv, lax.rem(across + k * plane, n)).wait_recv()
        relay(k, 2).start()

    every(n // plane, crossed)
    every(n, lambda k: x_copy(0, k).start(), 1)
    for part in range(1, parts):
        every(n, lambda k: x_copy(part, k).start(), 1)

    def rest(k):
        for hop in (0, 2):
            owner = sibling - lax.rem(sibling, plane) + lax.rem(lax.rem(sibling, plane) + hop, plane)
            landed(aux_all, gate_recv, lax.rem(owner + k * plane, n)).wait_recv()

    every(n // plane, rest)
    aux_rows = aux_all
    find_places(aux_rows, keys, place_row, place_col, heads)
    ub[0:PAD, :] = jnp.zeros((PAD, state2), F32)
    ux[0:PAD, :] = jnp.zeros((PAD, size), F32)

    def gather(b):
        first = pl.multiple_of(b * block, block)
        onehot = one_hot_sort(place_row, first, block)
        if keep:
            sorter[pl.ds(first, block), :] = onehot
        aux_here = dot(onehot, aux_all[...].reshape(rows, aux_all.shape[2]))
        ub[pl.ds(pl.multiple_of(first + PAD, PAD), block), :] = aux_here[:, :state2]
        ds[pl.ds(first, block), :] = dot(aux_here[:, state2:].astype(BF16), pick_ref[...])

    every(rows // block, gather)

    starts, total = [], jnp.int32(0)
    for k in range(docs_ref.shape[0]):
        starts.append(total)
        total = total + docs_ref[k]

    def shared(c):
        for i in range(4):
            shared_chunk(4 * c + i, starts, ub, ds, bcpar_ref, rate_ref, bcs, ws, ent, tails, carries, owned)

    every(rows // CHUNK // 4, shared)
    if keep:

        def prepare(b):
            first = pl.multiple_of(b * block, block)
            unsorter[pl.ds(first, block), :] = one_hot_unsort(place_col, first, block)

        every(rows // block, prepare)

    def out_copy(part, owner):
        return remote(
            sent.at[part, owner], tile(out_ref, part, me), out_send.at[part, owner], out_recv.at[part, me], owner
        )

    for part in range(parts):

        def x_landed(k):
            source = lax.rem(me + k, n)
            slot = x_all.at[part, source]
            remote(slot, slot, gate_send.at[0], x_recv.at[part, source], source).wait_recv()

        every(n, x_landed, 1)

        def gather_x(b):
            first = pl.multiple_of(b * block, block)
            onehot = sorter[pl.ds(first, block), :] if keep else one_hot_sort(place_row, first, block)
            x_here = dot(onehot, x_all[part].reshape(rows, size))
            ux[pl.ds(pl.multiple_of(first + PAD, PAD), block), :] = x_here

        every(rows // block, gather_x)
        state[...] = jnp.zeros_like(state)

        def chunk(c):
            for i in range(4):
                scan_chunk(
                    4 * c + i, part, parts, starts, ux, xpar_ref, bcs, ws, ent, tails, carries, state, ys, owned
                )

        every(rows // CHUNK // 4, chunk)

        def scatter(i):
            b = lax.rem(me * tok // block + 1 + i, rows // block)
            first = pl.multiple_of(b * block, block)
            onehot = unsorter[pl.ds(first, block), :] if keep else one_hot_unsort(place_col, first, block)
            back = dot(onehot, ys[...]).astype(BF16)
            for j in range(block // tok):
                owner = b * (block // tok) + j
                sent[part, owner] = back[j * tok : (j + 1) * tok, :]

                @pl.when(owner != me)
                def _():
                    out_copy(part, owner).start()

        every(rows // block, scatter)
        tile(out_ref, part, me)[...] = sent[part, me]

    def finish(k):
        source = lax.rem(me + k, n)
        for part in range(parts):
            slot = tile(out_ref, part, source)
            remote(slot, slot, gate_send.at[0], out_recv.at[part, source], source).wait_recv()
            out_copy(part, source).wait_send()
            x_copy(part, k).wait_send()

    every(n, finish, 1)

    def finish_aux(k):
        for hop in range(3):
            relay(k, hop).wait_send()

    every(n // plane, finish_aux)
    every(n // plane, lambda k: far(k).wait_send(), 1)


def per_device(
    x_rows, bc_rows, step, route, doc_lengths, conv_weight, conv_bias, rate, skip, clip_level
):
    seq_count = lax.axis_size("seq")
    tok_rows, hp_width = x_rows.shape
    heads = step.shape[1]
    owned = heads // seq_count
    width = hp_width // seq_count
    state2 = bc_rows.shape[1]
    rows = tok_rows * seq_count

    spare = jnp.zeros((tok_rows, LANES - heads - 1), BF16)
    aux = jnp.concatenate([bc_rows, step, route.astype(BF16), spare], axis=1)
    parts = 2 if width % (2 * LANES) == 0 and owned % 2 == 0 else 1
    plane = 4
    size = width // parts
    keep = rows if rows <= 2048 else 16
    flat = size % LANES == 0
    x_send = x_rows if flat else jnp.swapaxes(x_rows.reshape(tok_rows, seq_count, width), 0, 1)

    vmem = pl.BlockSpec(memory_space=pltpu.VMEM)
    dma = pltpu.SemaphoreType.DMA
    out = pl.pallas_call(
        functools.partial(kernel, owned, heads, parts, plane),
        out_shape=jax.ShapeDtypeStruct(x_send.shape, BF16),
        in_specs=[pl.BlockSpec(memory_space=pltpu.SMEM)] * 4 + [vmem] * 4,
        out_specs=vmem,
        scratch_shapes=[
            pltpu.VMEM((8, width), F32),
            pltpu.VMEM((8, state2), F32),
            pltpu.VMEM((1, LANES), F32),
            pltpu.VMEM((LANES, LANES), BF16),
            pltpu.VMEM((seq_count, tok_rows, aux.shape[1]), BF16),
            pltpu.VMEM((parts, seq_count, tok_rows, size), BF16),
            pltpu.VMEM((parts, seq_count, tok_rows, size), BF16),
            pltpu.VMEM((rows, LANES), F32),
            pltpu.VMEM((8, rows), F32),
            pltpu.VMEM((rows, LANES), F32),
            pltpu.VMEM((PAD + rows, state2), F32),
            pltpu.VMEM((PAD + rows, size), F32),
            pltpu.VMEM((rows, LANES), F32),
            pltpu.VMEM((rows, state2), BF16),
            pltpu.VMEM((owned, rows, CHUNK), BF16),
            pltpu.VMEM((rows, width), F32),
            pltpu.VMEM((rows, width), F32),
            pltpu.VMEM((rows // CHUNK, 8, width), F32),
            pltpu.VMEM((rows, size), BF16),
            pltpu.VMEM((state2 // 2, size), F32),
            pltpu.VMEM((keep, keep), BF16),
            pltpu.VMEM((keep, keep), BF16),
            dma((seq_count // plane,)),
            dma((seq_count,)),
            dma((seq_count // plane, 3)),
            dma((parts, seq_count)),
            dma((parts, seq_count)),
            dma((parts, seq_count)),
            dma((parts, seq_count)),
        ],
        compiler_params=pltpu.CompilerParams(
            vmem_limit_bytes=60 * 1024 * 1024, collective_id=0, has_side_effects=True
        ),
    )(doc_lengths, rate, skip, clip_level, x_send, aux, conv_weight, conv_bias[None, :])
    return out if flat else jnp.swapaxes(out, 0, 1).reshape(tok_rows, hp_width)


SUB = 256
SMALL = 16


def fast_conv(rows, taps, bias, off):
    size = off.shape[0]
    acc = bias + taps[0:1, :] * rows[PAD : PAD + size, :]
    for j in range(1, 4):
        back = rows[PAD - j : PAD - j + size, :]
        acc = acc + taps[j : j + 1, :] * jnp.where(off >= j, back, 0.0)
    half = 0.5 * acc
    return (half + half * jnp.tanh(half)).astype(BF16)


def fast_kernel(
    owned, parts, plane, docs_ref, rates, skips, clips, x_ref, bc_ref, step_ref, route_ref, weight_ref, bias_ref, out_ref,
    step_v, route_v, x_taps, bc_taps, bias_v, small_out, small_all, bc_all, x_all, sent, off_ref,
    sorter, unsorter, columns, dt_left, dt_right, places, ub, ux, lhs, b_flip, rise, fall, by_chunk, ys, state,
    load_sem, small_send, small_recv, gate_send, gate_recv, plane_send, x_send, x_recv, own_sem, out_send, out_recv,
):
    n, tok, state2 = bc_all.shape
    rows, size = ys.shape
    heads = step_v.shape[0]
    chunks = rows // CHUNK
    width = size * parts
    local = owned // parts
    me = lax.axis_index("seq")
    inside = lax.rem(me, plane)
    iota = functools.partial(lax.broadcasted_iota, jnp.int32)

    def remote(source, target, send, recv, peer):
        return pltpu.make_async_remote_copy(
            src_ref=source, dst_ref=target, send_sem=send, recv_sem=recv,
            device_id={"seq": peer}, device_id_type=pl.DeviceIdType.MESH,
        )

    def every(count, do, first=0):
        def turn(k, _):
            do(k)
            return 0

        lax.fori_loop(first, count, turn, 0)

    def tile(ref, part, owner):
        return ref.at[:, pl.ds(pl.multiple_of((owner * parts + part) * size, size), size)]

    barrier = pltpu.get_barrier_semaphore()

    def greet(k):
        pl.semaphore_signal(
            barrier, inc=1, device_id={"seq": lax.rem(me + k, n)}, device_id_type=pl.DeviceIdType.MESH
        )

    every(n, greet, 1)

    own = pl.ds(pl.multiple_of(me * width, width), width)
    shared_at = weight_ref.shape[1] - state2
    loads = [
        pltpu.make_async_copy(bc_ref, bc_all.at[me], load_sem.at[0]),
        pltpu.make_async_copy(step_ref, step_v, load_sem.at[1]),
        pltpu.make_async_copy(route_ref, route_v, load_sem.at[2]),
        pltpu.make_async_copy(weight_ref.at[:, own], x_taps, load_sem.at[3]),
        pltpu.make_async_copy(weight_ref.at[:, shared_at:], bc_taps, load_sem.at[4]),
        pltpu.make_async_copy(bias_ref, bias_v, load_sem.at[5]),
    ]
    for load in loads:
        load.start()

    loads[1].wait()
    loads[2].wait()
    wide_step = step_v[...].astype(F32)
    wide_route = jnp.broadcast_to(route_v[...].astype(F32), (8, tok))
    for p in range(n):
        mine = wide_step[p * owned : (p + 1) * owned, :]
        block = jnp.concatenate([mine, jnp.zeros((8 - owned, tok), F32), wide_route], axis=0)
        small_out[p] = block.astype(BF16)
    small_all[me] = small_out[me]
    loads[0].wait()

    pl.semaphore_wait(barrier, n - 1)

    low_plane = lax.rem(me // plane, 2)
    mate_turn, last_turn = 1 + 2 * low_plane, 3 - 2 * low_plane

    def far(step):
        owner = lax.rem(me + 2 * plane, n) if step == 2 else me
        peer = lax.rem(me + (2 if step == 0 else mate_turn) * plane, n)
        return remote(bc_all.at[owner], bc_all.at[owner], gate_send.at[step], gate_recv.at[owner], peer)

    def small_copy(k):
        peer = lax.rem(me + k, n)
        return remote(small_out.at[peer], small_all.at[me], small_send.at[k], small_recv.at[me], peer)

    def landed(ref, sems, slot):
        return remote(ref.at[slot], ref.at[slot], gate_send.at[0], sems.at[slot], slot)

    across = me - inside + lax.rem(inside + 2, plane)
    sibling = me + 1 - 2 * lax.rem(me, 2)

    def relay(k, hop):
        owner = lax.rem((across if hop == 2 else me) + k * plane, n)
        peer = across if hop == 0 else sibling
        return remote(bc_all.at[owner], bc_all.at[owner], plane_send.at[k, hop], gate_recv.at[owner], peer)

    def x_copy(part, peer):
        return remote(tile(x_ref, part, peer), x_all.at[part, me], x_send.at[part, peer], x_recv.at[part, me], peer)

    planes = n // plane
    half = planes // 2
    mine = me // plane

    def plane_at(i):
        turn = lax.rem(i, half)
        side = lax.rem(mine // half + 1 + i // half, 2)
        return side * half + lax.rem(lax.rem(mine, half) + turn + i // half, half)

    def own_copy(part):
        return pltpu.make_async_copy(tile(x_ref, part, me), x_all.at[part, me], own_sem.at[part])

    def start_at(moment):
        for part, turn, *span in SCHEDULE.get(moment, ()):
            begin, end = span or (0, plane)
            first = plane_at(jnp.int32(turn)) * plane

            def to_peer(j, part=part, first=first):
                peer = first + lax.rem(inside + 1 + j, plane)

                @pl.when(peer != me)
                def _():
                    x_copy(part, peer).start()

            every(end, to_peer, begin)

    every(n, lambda k: small_copy(k).start(), 1)
    far(0).start()
    far(1).start()
    relay(0, 0).start()
    relay(0, 1).start()
    start_at(0)
    for part in range(parts):
        own_copy(part).start()

    starts, total = [], jnp.int32(0)
    for k in range(docs_ref.shape[0]):
        starts.append(total)
        total = total + docs_ref[k]

    def begins(at):
        begin = jnp.zeros(at.shape, jnp.int32)
        for start in starts:
            begin = jnp.where(at >= start, start, begin)
        return begin

    low, high = iota((CHUNK, CHUNK), 0), iota((CHUNK, CHUNK), 1)

    def make_off(c):
        base = pl.multiple_of(c * CHUNK, CHUNK)
        at = low + base
        off_ref[pl.ds(base, CHUNK), :] = (at - begins(at)).astype(F32)

    every(chunks, make_off)

    def small_landed(k):
        landed(small_all, small_recv, lax.rem(me + k, n)).wait_recv()

    every(n, small_landed, 1)

    def find_places():
        number = iota((n, tok), 0).astype(F32)
        named = []
        for i in range(n):
            target = jnp.concatenate([small_all[i].astype(F32)[8:, :]] * (n // 8), axis=0)
            named.append(jnp.where(target == number, 1.0, 0.0))
        earlier = jnp.where(low < high, 1.0, 0.0).astype(BF16)
        right = jnp.concatenate([earlier, jnp.ones((tok, tok), BF16)], axis=1)
        found = dot(jnp.concatenate(named, axis=0).astype(BF16), right)
        before = jnp.zeros((n, tok), F32)
        ranks = []
        for i in range(n):
            here = found[i * n : (i + 1) * n, :]
            ranks.append(here[:, :tok] + before)
            before = before + here[:, tok:]
        base = jnp.zeros((n, tok), F32)
        for d in range(n - 1):
            base = base + jnp.where(number > d, before[d : d + 1, :], 0.0)
        all_places = []
        for i in range(n):
            place = jnp.sum(named[i] * (ranks[i] + base), axis=0, keepdims=True)
            places[i : i + 1, :] = place
            all_places.append(place)
            coarse = jnp.floor(place * (1.0 / CHUNK))
            fine = place - coarse * CHUNK
            lanes = slice(i * tok, (i + 1) * tok)
            steps = small_all[i].astype(F32)[0:8, :]
            split = [jnp.where(coarse == c, steps, 0.0) for c in range(chunks)]
            dt_left[:, lanes] = jnp.concatenate(split, axis=0).astype(BF16)
            dt_right[:, lanes] = jnp.where(low.astype(F32) == fine, 1.0, 0.0).astype(BF16)

    find_places()

    start_at(6)
    row16 = iota((SUB, tok), 0).astype(F32).astype(BF16)
    one, none = jnp.ones((), BF16), jnp.zeros((), BF16)

    def make_sorter(b):
        first = lax.convert_element_type(b * SUB, F32)
        for i in range(n):
            rel = places[i : i + 1, :] - first
            rel = jnp.where((rel >= 0.0) & (rel < SUB), rel, -1.0)
            rel = jnp.broadcast_to(rel, (SUB, tok)).astype(BF16)
            hit = jnp.where(row16 == rel, one, none)
            sorter[pl.ds(pl.multiple_of(b * SUB, SUB), SUB), i * tok : (i + 1) * tok] = hit

    every(rows // SUB, make_sorter)

    start_at(8)
    def forward(k):
        landed(bc_all, gate_recv, lax.rem(me + k * plane, n)).wait_recv()
        if isinstance(k, int):
            far(2).start()
        relay(k, 0).start()
        relay(k, 1).start()

    forward(2)
    forward(mate_turn)
    start_at(7)
    forward(last_turn)
    start_at(1)

    def decays():
        dts = dot_nt(dt_left[...], dt_right[...])
        lane = iota((8, CHUNK), 1)
        slot = iota((8, CHUNK), 0)
        rate = jnp.zeros((8, CHUNK), F32)
        for h in range(owned):
            rate = jnp.where(slot == h, rates[me * owned + h], rate)
        rate = jnp.concatenate([rate] * chunks, axis=0)
        upto = jnp.where(low <= high, 1.0, 0.0).astype(BF16)
        cum = -dot(dts.astype(BF16), upto) * rate
        last = jnp.broadcast_to(cum[:, CHUNK - 1 :], cum.shape)
        middle = 0.5 * last
        up = jnp.exp(cum - middle)
        down = jnp.exp(middle - cum) * dts
        gain = jnp.exp(middle)
        number = iota((8 * chunks, CHUNK), 0) // 8
        ends = number * CHUNK + CHUNK - 1
        goes_on = jnp.where(begins(ends) < number * CHUNK, 1.0, 0.0)
        carry = jnp.exp(last) * goes_on
        by_chunk[0] = up
        by_chunk[1] = down
        by_chunk[2] = gain
        by_chunk[3] = carry

    decays()

    head = iota((1, size), 1) // (size // local)

    def spread(columns, part):
        out = jnp.broadcast_to(columns[:, part * local : part * local + 1], (CHUNK, size))
        for h in range(1, local):
            at = part * local + h
            out = jnp.where(head == h, jnp.broadcast_to(columns[:, at : at + 1], (CHUNK, size)), out)
        return out

    def expand(part):
        pair = by_chunk[0].reshape(chunks, 8, CHUNK)[:, :4], by_chunk[1].reshape(chunks, 8, CHUNK)[:, :4]
        turned = jnp.concatenate(pair, axis=1).reshape(8 * chunks, CHUNK).T
        for c in range(chunks):
            at = slice(c * CHUNK, (c + 1) * CHUNK)
            rise[part, at, :] = spread(turned[:, 8 * c :], part)
            fall[part, at, :] = spread(turned[:, 8 * c + 4 :], part)

    expand(0)

    def crossed(k):
        landed(bc_all, gate_recv, lax.rem(across + k * plane, n)).wait_recv()
        relay(k, 2).start()

    for k in (0, 2, mate_turn, last_turn):
        crossed(k)

    start_at(2)

    block = plane * tok
    core = lax.rem(me, 2)
    ub[0:PAD, :] = jnp.zeros((PAD, state2), F32)

    def gather(b, side):
        first = pl.multiple_of(b * block, block)
        owners = [2 * i + side for i in range(n // 2)]
        lefts = [sorter[pl.ds(first, block), pl.ds(pl.multiple_of(o * tok, tok), tok)] for o in owners]
        here = dot(jnp.concatenate(lefts, axis=1), jnp.concatenate([bc_all[o] for o in owners], axis=0))
        at = pl.ds(pl.multiple_of(first + PAD, PAD), block)
        ub[at, :] = here if side is core else ub[at, :] + here

    every(rows // block, lambda b: gather(b, core))

    lane16 = [(iota((tok, LANES), 1) + j * LANES).astype(F32).astype(BF16) for j in range(SUB // LANES)]
    flipped = jnp.concatenate([places[...], jnp.zeros((tok - n, tok), F32)], axis=0).T
    flipped_coarse = jnp.floor(flipped * (1.0 / SUB))
    flipped_fine = flipped - flipped_coarse * SUB

    def make_columns():
        for i in range(n):
            at = slice(i * tok, (i + 1) * tok)
            columns[0, at, :] = jnp.broadcast_to(flipped_coarse[:, i : i + 1], (tok, LANES)).astype(BF16)
            columns[1, at, :] = jnp.broadcast_to(flipped_fine[:, i : i + 1], (tok, LANES)).astype(BF16)

    def make_unsorter(i):
        at = pl.ds(pl.multiple_of(i * tok, tok), tok)
        coarse, fine = columns[0, at, :], columns[1, at, :]
        for b in range(rows // SUB):
            rel = jnp.where(coarse == jnp.full((), b, BF16), fine, -one)
            for j in range(SUB // LANES):
                unsorter[at, b * SUB + j * LANES : b * SUB + (j + 1) * LANES] = jnp.where(lane16[j] == rel, one, none)

    start_at(9)
    make_columns()

    def rest(k):
        for hop in (0, 2):
            owner = sibling - lax.rem(sibling, plane) + lax.rem(lax.rem(sibling, plane) + hop, plane)
            landed(bc_all, gate_recv, lax.rem(owner + k * plane, n)).wait_recv()

    every(n // plane, rest)

    start_at(3)

    for load in loads[3:]:
        load.wait()
    ux[0:PAD, :] = jnp.zeros((PAD, size), F32)
    every(rows // block, lambda b: gather(b, 1 - core))
    start_at(4)

    gap = low - high

    def wide_bias(first, count):
        return jnp.concatenate([bias_v[pl.ds(first + i, 1), :] for i in range(count)], axis=1)

    def shared(c):
        base = pl.multiple_of(c * CHUNK, CHUNK)
        off = off_ref[pl.ds(base, CHUNK), :]
        off2 = jnp.concatenate([off] * (state2 // LANES), axis=1)
        bias = wide_bias(shared_at // LANES, state2 // LANES)
        act = fast_conv(ub[pl.ds(base, CHUNK + PAD), :], bc_taps[...], bias, off2)
        b_mat, c_mat = act[:, : state2 // 2], act[:, state2 // 2 :]
        scores = dot_nt(c_mat, b_mat)
        keep = (gap >= 0) & (gap.astype(F32) <= off)
        lhs[pl.ds(base, CHUNK), :CHUNK] = jnp.where(keep, scores, 0.0).astype(BF16)
        runs_in = jnp.where(off > low.astype(F32), c_mat.astype(F32), 0.0)
        lhs[pl.ds(base, CHUNK), CHUNK:] = runs_in.astype(BF16)
        runs_out = high[0:1, :].astype(F32) + off[CHUNK - 1 :, :] >= CHUNK - 1
        b_flip[pl.ds(base, CHUNK), :] = jnp.where(runs_out, b_mat.astype(F32).T, 0.0).astype(BF16)

    every(chunks // 4, lambda c: [shared(4 * c + i) for i in range(4)])
    start_at(5)

    def out_copy(part, owner):
        return remote(
            sent.at[part, owner], tile(out_ref, part, me), out_send.at[part, owner], out_recv.at[part, me], owner
        )

    def own_out(part):
        return pltpu.make_async_copy(sent.at[part, me], tile(out_ref, part, me), own_sem.at[parts + part])

    lane_head = iota((1, size), 1) // (size // local)

    def by_head(values):
        out = jnp.full((1, size), values[0], F32)
        for h in range(1, local):
            out = jnp.where(lane_head == h, values[h], out)
        return out

    for part in range(parts):

        def x_landed(k):
            source = lax.rem(me + k, n)
            slot = x_all.at[part, source]
            remote(slot, slot, gate_send.at[0], x_recv.at[part, source], source).wait_recv()

        if part > 0:
            expand(part)
        own_copy(part).wait()
        every(n, x_landed, 1)

        def gather_x(b):
            first = pl.multiple_of(b * block, block)
            here = dot(sorter[pl.ds(first, block), :], x_all[part].reshape(rows, size))
            ux[pl.ds(pl.multiple_of(first + PAD, PAD), block), :] = here

        every(rows // block, gather_x)
        state[...] = jnp.zeros_like(state)
        skip = by_head([skips[me * owned + part * local + h] for h in range(local)])
        level = by_head([clips[me * owned + part * local + h] for h in range(local)])

        def chunk(c):
            base = pl.multiple_of(c * CHUNK, CHUNK)
            at = pl.ds(base, CHUNK)
            bias = bias_v[pl.ds(me * parts + part, 1), :]
            taps = x_taps[:, part * size : (part + 1) * size]
            wide = fast_conv(ux[pl.ds(base, CHUNK + PAD), :], taps, bias, off_ref[at, :]).astype(F32)
            scaled = (wide * fall[part, at, :]).astype(BF16)
            at8 = pl.ds(pl.multiple_of(c * 8, 8), 8)
            gains, carries = by_chunk[2, at8, :], by_chunk[3, at8, :]
            gain = by_head([gains[part * local + h : part * local + h + 1, :] for h in range(local)])
            carry = by_head([carries[part * local + h : part * local + h + 1, :] for h in range(local)])
            old = state[...]
            right = jnp.concatenate([scaled, (gain * old).astype(BF16)], axis=0)
            y = skip * wide + rise[part, at, :] * dot(lhs[at, :], right)
            ys[at, :] = jnp.clip(y, -level, level).astype(BF16)
            state[...] = carry * old + gain * dot(b_flip[at, :], scaled)

        every(chunks // 4, lambda c: [chunk(4 * c + i) for i in range(4)])

        def scatter(i):
            b = plane_at(i)
            first = pl.multiple_of(b * block, block)
            if part == 0:
                every(plane, lambda j: make_unsorter(b * plane + j))
            back = dot(unsorter[pl.ds(first, block), :], ys[...]).astype(BF16)
            for j in range(block // tok):
                owner = b * (block // tok) + j
                sent[part, owner] = back[j * tok : (j + 1) * tok, :]

                @pl.when(owner != me)
                def _():
                    out_copy(part, owner).start()

        every(rows // block, scatter)
        own_out(part).start()

    def finish(k):
        source = lax.rem(me + k, n)
        for part in range(parts):
            slot = tile(out_ref, part, source)
            remote(slot, slot, gate_send.at[0], out_recv.at[part, source], source).wait_recv()
            out_copy(part, source).wait_send()
            x_copy(part, source).wait_send()
        small_copy(k).wait_send()

    every(n, finish, 1)
    for part in range(parts):
        own_out(part).wait()

    def finish_aux(k):
        for hop in range(3):
            relay(k, hop).wait_send()

    every(n // plane, finish_aux)
    for step in range(3):
        far(step).wait_send()


def fast_device(
    x_rows, bc_rows, step, route, doc_lengths, conv_weight, conv_bias, rate, skip, clip_level
):
    n = lax.axis_size("seq")
    tok, hp_width = x_rows.shape
    heads = step.shape[1]
    owned = heads // n
    width = hp_width // n
    state2 = bc_rows.shape[1]
    rows = tok * n
    parts = width // LANES
    size = LANES
    plane = 4
    chunks = rows // CHUNK
    bias = conv_bias.reshape(conv_bias.shape[0] // LANES, LANES)

    hbm = pl.BlockSpec(memory_space=pl.ANY)
    dma = pltpu.SemaphoreType.DMA
    return pl.pallas_call(
        functools.partial(fast_kernel, owned, parts, plane),
        out_shape=jax.ShapeDtypeStruct(x_rows.shape, BF16),
        in_specs=[pl.BlockSpec(memory_space=pltpu.SMEM)] * 4 + [hbm] * 6,
        out_specs=OUT_SPEC,
        scratch_shapes=[
            pltpu.VMEM((heads, tok), BF16),
            pltpu.VMEM((1, tok), jnp.int32),
            pltpu.VMEM((4, width), F32),
            pltpu.VMEM((4, state2), F32),
            pltpu.VMEM(bias.shape, F32),
            pltpu.VMEM((n, SMALL, tok), BF16),
            pltpu.VMEM((n, SMALL, tok), BF16),
            pltpu.VMEM((n, tok, state2), BF16),
            pltpu.VMEM((parts, n, tok, size), BF16),
            pltpu.VMEM((parts, n, tok, size), BF16),
            pltpu.VMEM((rows, LANES), F32),
            pltpu.VMEM((rows, rows), BF16),
            pltpu.VMEM((rows, rows), BF16),
            pltpu.VMEM((2, rows, LANES), BF16),
            pltpu.VMEM((8 * chunks, rows), BF16),
            pltpu.VMEM((CHUNK, rows), BF16),
            pltpu.VMEM((n, tok), F32),
            pltpu.VMEM((PAD + rows, state2), F32),
            pltpu.VMEM((PAD + rows, size), F32),
            pltpu.VMEM((rows, 2 * CHUNK), BF16),
            pltpu.VMEM((rows, CHUNK), BF16),
            pltpu.VMEM((parts, rows, size), F32),
            pltpu.VMEM((parts, rows, size), F32),
            pltpu.VMEM((4, 8 * chunks, CHUNK), F32),
            pltpu.VMEM((rows, size), BF16),
            pltpu.VMEM((state2 // 2, size), F32),
            dma((6,)),
            dma((n,)),
            dma((n,)),
            dma((n // plane,)),
            dma((n,)),
            dma((n // plane, 3)),
            dma((parts, n)),
            dma((parts, n)),
            dma((2 * parts,)),
            dma((parts, n)),
            dma((parts, n)),
        ],
        compiler_params=pltpu.CompilerParams(
            vmem_limit_bytes=48 * 1024 * 1024, collective_id=1, has_side_effects=True
        ),
    )(*[pltpu.with_memory_space_constraint(a, pltpu.HBM) for a in (
        doc_lengths, rate, skip, clip_level, x_rows, bc_rows, step.T, route.T, conv_weight, bias
    )])


def fits_fast(n, x_shape, heads, state2):
    width = x_shape[1] // n
    owned = heads // n
    return (
        n == 16 and n * x_shape[0] <= 2048 and x_shape[0] == LANES and width % LANES == 0 and state2 == 2 * CHUNK
        and owned == 4 and owned % (width // LANES) == 0 and 8 * n * LANES // CHUNK <= CHUNK
    )


def solution(mesh):
    placed = (
        P(("groups", "seq"), None),
        P(("groups", "seq"), None),
        P(("groups", "seq"), None),
        P(("groups", "seq"), None),
        P("groups"),
        P(),
        P(),
        P(),
        P(),
        P(),
    )

    def run(*arrays):
        x_rows, bc_rows, step = arrays[:3]
        fast = fits_fast(lax.axis_size("seq"), x_rows.shape, step.shape[1], bc_rows.shape[1])
        return (fast_device if fast else per_device)(*arrays)

    return jax.shard_map(
        run,
        mesh=mesh,
        in_specs=placed,
        out_specs=P(("groups", "seq"), None),
        check_vma=False,
    )
```

```python
import functools

import jax
import jax.numpy as jnp
from jax import lax
from jax.experimental import pallas as pl
from jax.experimental.pallas import tpu as pltpu
from jax.sharding import PartitionSpec as P

F32 = jnp.float32
BF16 = jnp.bfloat16
CHUNK = 128
LANES = 128
PAD = 8
SCHEDULE = {0:[(0,0,0,2)],7:[(0,0,2,4)],1:[(0,1)],2:[(0,2),(0,3)],3:[(1,0),(1,1),(1,2),(1,3)]}
OUT_SPEC = pl.BlockSpec(memory_space=pl.ANY)


def dot(a, b):
    return jnp.dot(a, b, preferred_element_type=F32)


def dot_nt(a, b):
    return lax.dot_general(a, b, (((1,), (1,)), ((), ())), preferred_element_type=F32)


def dot_tn(a, b):
    return lax.dot_general(a, b, (((0,), (0,)), ((), ())), preferred_element_type=F32)


def find_places(aux_ref, ranks, place_row, place_col, heads):
    rows = ranks.shape[0]
    state2 = aux_ref.shape[2] - LANES
    low = lax.broadcasted_iota(jnp.int32, (LANES, LANES), 0)
    high = lax.broadcasted_iota(jnp.int32, (LANES, LANES), 1)
    earlier = jnp.where(low > high, 1.0, 0.0).astype(BF16)
    before = jnp.where(low < high, 1.0, 0.0).astype(BF16)
    shard = high.astype(F32)
    step = 4

    def named(b):
        target = aux_ref[b, :, state2 : state2 + LANES].astype(F32)[:, heads : heads + 1]
        return jnp.where(target == shard, 1.0, 0.0)

    def count(i, total):
        for j in range(step):
            b = i * step + j
            onehot = named(b)
            ranks[pl.ds(pl.multiple_of(b * LANES, LANES), LANES), :] = dot(earlier, onehot.astype(BF16)) + total
            total = total + jnp.sum(onehot, axis=0, keepdims=True)
        return total

    total = lax.fori_loop(0, rows // LANES // step, count, jnp.zeros((1, LANES), F32))
    total = jnp.broadcast_to(total, (8, LANES))
    coarse = jnp.floor(total * (1.0 / 64.0))
    fine = total - coarse * 64.0
    start = (dot(coarse.astype(BF16), before) * 64.0 + dot(fine.astype(BF16), before))[0:1, :]

    def rank(i, _):
        for j in range(step):
            b = i * step + j
            at = pl.multiple_of(b * LANES, LANES)
            found = named(b) * (ranks[pl.ds(at, LANES), :] + start)
            place = jnp.broadcast_to(jnp.sum(found, axis=1, keepdims=True), (LANES, LANES))
            place_col[pl.ds(at, LANES), :] = place
            place_row[:, pl.ds(at, LANES)] = place.T[0:8, :]
        return 0

    lax.fori_loop(0, rows // LANES // step, rank, 0)


def one_hot_sort(place_row, first, size):
    rows = place_row.shape[1]
    number = lax.broadcasted_iota(jnp.int32, (size, rows), 0).astype(F32)
    hit = place_row[0:1, :] - lax.convert_element_type(first, F32) == number
    return jnp.where(hit, 1.0, 0.0).astype(BF16)


def one_hot_unsort(place_col, first, size):
    rows = place_col.shape[0]
    number = lax.broadcasted_iota(jnp.int32, (size, rows), 1).astype(F32)
    place = place_col[pl.ds(first, size), :]
    hit = jnp.concatenate([place] * (rows // LANES), axis=1) == number
    return jnp.where(hit, 1.0, 0.0).astype(BF16)


def doc_begins(at, starts):
    begin = jnp.zeros((CHUNK, 1), jnp.int32)
    for start in starts:
        begin = jnp.where(at >= start, start, begin)
    return begin


def conv_silu(v, par, at, begin):
    acc = par[4:5, :] + par[0:1, :] * v[PAD:, :]
    for j in range(1, 4):
        keep = jnp.where(at - j >= begin, 1.0, 0.0)
        acc = acc + par[j : j + 1, :] * (v[PAD - j : PAD - j + CHUNK, :] * keep)
    return (acc / (1.0 + jnp.exp(-acc))).astype(BF16)


def shared_chunk(c, starts, ub, ds, bcpar_ref, rate_ref, bcs, ws, ent, tails, carries, owned):
    width = ent.shape[1]
    state_width = bcs.shape[1] // 2
    base = pl.multiple_of(c * CHUNK, CHUNK)
    at = lax.broadcasted_iota(jnp.int32, (CHUNK, 1), 0) + base
    begin = doc_begins(at, starts)
    begin_last = begin[CHUNK - 1 :, :]
    act = conv_silu(ub[pl.ds(base, CHUNK + PAD), :], bcpar_ref[...], at, begin)
    bcs[pl.ds(base, CHUNK), :] = act
    b_mat, c_mat = act[:, :state_width], act[:, state_width:]

    dt = ds[pl.ds(base, CHUNK), :]
    low = lax.broadcasted_iota(jnp.int32, (CHUNK, CHUNK), 0)
    high = lax.broadcasted_iota(jnp.int32, (CHUNK, CHUNK), 1)
    tri = jnp.where(low >= high, 1.0, 0.0).astype(BF16)
    cum = -dot(tri, dt.astype(BF16)) * rate_ref[...]
    shifted = (cum - jnp.log(jnp.maximum(dt, 1e-30))).T
    cum_last = cum[CHUNK - 1 :, :]
    scores = dot_nt(c_mat, b_mat)
    scores = jnp.where((low >= high) & (high + base >= begin), scores, 0.0)
    head = lax.broadcasted_iota(jnp.int32, (1, width), 1) // (width // owned)

    def expand(e):
        out = jnp.broadcast_to(e[:, 0:1], (e.shape[0], width))
        for h in range(1, owned):
            out = jnp.where(head == h, e[:, h : h + 1], out)
        return out

    for h in range(owned):
        decay = jnp.exp(cum[:, h : h + 1] - shifted[h : h + 1, :])
        ws[h, pl.ds(base, CHUNK), :] = (scores * decay).astype(BF16)
    ent[pl.ds(base, CHUNK), :] = expand(jnp.exp(cum) * jnp.where(begin < base, 1.0, 0.0))
    tail = jnp.exp(cum_last - cum) * dt * jnp.where(at >= begin_last, 1.0, 0.0)
    tails[pl.ds(base, CHUNK), :] = expand(tail)
    carry = expand(jnp.exp(cum_last) * jnp.where(begin_last < base, 1.0, 0.0))
    carries[c] = jnp.broadcast_to(carry, (8, width))


def scan_chunk(c, part, parts, starts, ux, xpar_ref, bcs, ws, ent, tails, carries, state, ys, owned):
    size = ux.shape[1]
    lanes = slice(part * size, (part + 1) * size)
    state_width = bcs.shape[1] // 2
    base = pl.multiple_of(c * CHUNK, CHUNK)
    at = lax.broadcasted_iota(jnp.int32, (CHUNK, 1), 0) + base
    begin = doc_begins(at, starts)
    x_mat = conv_silu(ux[pl.ds(base, CHUNK + PAD), :], xpar_ref[:, lanes], at, begin)
    x_wide = x_mat.astype(F32)
    bc = bcs[pl.ds(base, CHUNK), :]
    b_mat, c_mat = bc[:, :state_width], bc[:, state_width:]
    local = owned // parts
    head = lax.broadcasted_iota(jnp.int32, (1, size), 1) // (size // local)
    y = xpar_ref[5:6, lanes] * x_wide
    for h in range(local):
        mine = jnp.where(head == h, x_wide, 0.0).astype(BF16)
        y = y + dot(ws[part * local + h, pl.ds(base, CHUNK), :], mine)
    y = y + dot(c_mat, state[...].astype(BF16)) * ent[pl.ds(base, CHUNK), lanes]
    limit = xpar_ref[6:7, lanes]
    ys[pl.ds(base, CHUNK), :] = jnp.clip(y, -limit, limit).astype(BF16)
    scaled = (x_wide * tails[pl.ds(base, CHUNK), lanes]).astype(BF16)
    state[...] = carries[c][0:1, lanes] * state[...] + dot_tn(b_mat, scaled)


def kernel(
    owned, heads, parts, plane, docs_ref, rates, skips, clips, x_ref, aux_ref, weight_ref, bias_ref, out_ref,
    xpar_ref, bcpar_ref, rate_ref, pick_ref, aux_all, x_all, sent, keys, place_row, place_col, ub, ux, ds, bcs, ws, ent, tails, carries, ys, state,
    sorter, unsorter, gate_send, gate_recv, plane_send, x_send, x_recv, out_send, out_recv,
):
    n, tok = x_all.shape[1:3]
    rows, size = ys.shape
    state2 = bcs.shape[1]
    flat = len(x_ref.shape) == 2
    block = max(tok, min(512, (1 << 20) // rows))
    keep = sorter.shape[0] == rows
    me = lax.axis_index("seq")
    inside = lax.rem(me, plane)

    def remote(source, target, send, recv, peer):
        return pltpu.make_async_remote_copy(
            src_ref=source, dst_ref=target, send_sem=send, recv_sem=recv,
            device_id={"seq": peer}, device_id_type=pl.DeviceIdType.MESH,
        )

    def every(count, do, first=0):
        def turn(k, _):
            do(k)
            return 0

        lax.fori_loop(first, count, turn, 0)

    def tile(ref, part, owner):
        if flat:
            return ref.at[:, pl.ds(pl.multiple_of((owner * parts + part) * size, size), size)]
        return ref.at[owner]

    def own_lanes(ref):
        width = size * parts
        if width % LANES == 0:
            return ref[:, pl.ds(pl.multiple_of(me * width, LANES), width)]
        per = LANES // width
        wide = ref[:, pl.ds(pl.multiple_of(me // per * LANES, LANES), LANES)]
        picked = wide[:, :width]
        for i in range(1, per):
            picked = jnp.where(lax.rem(me, per) == i, wide[:, i * width : (i + 1) * width], picked)
        return picked

    def load_params():
        width = size * parts
        head = lax.broadcasted_iota(jnp.int32, (1, width), 1) // (width // owned)
        lane = lax.broadcasted_iota(jnp.int32, (1, LANES), 1)
        gain = level = jnp.zeros((1, width), F32)
        decay = jnp.zeros((1, LANES), F32)
        for h in range(owned):
            gain = jnp.where(head == h, skips[me * owned + h], gain)
            level = jnp.where(head == h, clips[me * owned + h], level)
            decay = jnp.where(lane == h, rates[me * owned + h], decay)
        xpar_ref[0:4, :] = own_lanes(weight_ref)
        xpar_ref[4:5, :] = own_lanes(bias_ref)
        xpar_ref[5:6, :] = gain
        xpar_ref[6:7, :] = level
        first = weight_ref.shape[1] - state2
        bcpar_ref[0:4, :] = weight_ref[:, first:]
        bcpar_ref[4:5, :] = bias_ref[:, first:]
        rate_ref[...] = decay
        source = lax.broadcasted_iota(jnp.int32, (LANES, LANES), 0)
        target = lax.broadcasted_iota(jnp.int32, (LANES, LANES), 1)
        hit = (source == target + me * owned) & (target < owned)
        pick_ref[...] = jnp.where(hit, 1.0, 0.0).astype(BF16)

    barrier = pltpu.get_barrier_semaphore()

    def greet(k):
        pl.semaphore_signal(
            barrier, inc=1, device_id={"seq": lax.rem(me + k, n)}, device_id_type=pl.DeviceIdType.MESH
        )

    every(n, greet, 1)
    pl.semaphore_wait(barrier, n - 1)

    def far(k):
        peer = lax.rem(me + k * plane, n)
        return remote(aux_ref, aux_all.at[me], gate_send.at[k], gate_recv.at[me], peer)

    def landed(ref, sems, slot):
        return remote(ref.at[slot], ref.at[slot], gate_send.at[0], sems.at[slot], slot)

    across = me - inside + lax.rem(inside + 2, plane)
    sibling = me + 1 - 2 * lax.rem(me, 2)

    def relay(k, hop):
        owner = lax.rem((across if hop == 2 else me) + k * plane, n)
        peer = across if hop == 0 else sibling
        return remote(aux_all.at[owner], aux_all.at[owner], plane_send.at[k, hop], gate_recv.at[owner], peer)

    def x_copy(part, k):
        peer = lax.rem(me + k, n)
        return remote(tile(x_ref, part, peer), x_all.at[part, me], x_send.at[part, k], x_recv.at[part, me], peer)

    every(n // plane, lambda k: far(k).start(), 1)
    aux_all[me] = aux_ref[...]
    relay(0, 0).start()
    relay(0, 1).start()

    def forward(k):
        landed(aux_all, gate_recv, lax.rem(me + k * plane, n)).wait_recv()
        relay(k, 0).start()
        relay(k, 1).start()

    every(n // plane, forward, 1)
    for part in range(parts):
        x_all[part, me] = tile(x_ref, part, me)[...]

    load_params()

    def crossed(k):
        landed(aux_all, gate_recv, lax.rem(across + k * plane, n)).wait_recv()
        relay(k, 2).start()

    every(n // plane, crossed)
    every(n, lambda k: x_copy(0, k).start(), 1)
    for part in range(1, parts):
        every(n, lambda k: x_copy(part, k).start(), 1)

    def rest(k):
        for hop in (0, 2):
            owner = sibling - lax.rem(sibling, plane) + lax.rem(lax.rem(sibling, plane) + hop, plane)
            landed(aux_all, gate_recv, lax.rem(owner + k * plane, n)).wait_recv()

    every(n // plane, rest)
    aux_rows = aux_all
    find_places(aux_rows, keys, place_row, place_col, heads)
    ub[0:PAD, :] = jnp.zeros((PAD, state2), F32)
    ux[0:PAD, :] = jnp.zeros((PAD, size), F32)

    def gather(b):
        first = pl.multiple_of(b * block, block)
        onehot = one_hot_sort(place_row, first, block)
        if keep:
            sorter[pl.ds(first, block), :] = onehot
        aux_here = dot(onehot, aux_all[...].reshape(rows, aux_all.shape[2]))
        ub[pl.ds(pl.multiple_of(first + PAD, PAD), block), :] = aux_here[:, :state2]
        ds[pl.ds(first, block), :] = dot(aux_here[:, state2:].astype(BF16), pick_ref[...])

    every(rows // block, gather)

    starts, total = [], jnp.int32(0)
    for k in range(docs_ref.shape[0]):
        starts.append(total)
        total = total + docs_ref[k]

    def shared(c):
        for i in range(4):
            shared_chunk(4 * c + i, starts, ub, ds, bcpar_ref, rate_ref, bcs, ws, ent, tails, carries, owned)

    every(rows // CHUNK // 4, shared)
    if keep:

        def prepare(b):
            first = pl.multiple_of(b * block, block)
            unsorter[pl.ds(first, block), :] = one_hot_unsort(place_col, first, block)

        every(rows // block, prepare)

    def out_copy(part, owner):
        return remote(
            sent.at[part, owner], tile(out_ref, part, me), out_send.at[part, owner], out_recv.at[part, me], owner
        )

    for part in range(parts):

        def x_landed(k):
            source = lax.rem(me + k, n)
            slot = x_all.at[part, source]
            remote(slot, slot, gate_send.at[0], x_recv.at[part, source], source).wait_recv()

        every(n, x_landed, 1)

        def gather_x(b):
            first = pl.multiple_of(b * block, block)
            onehot = sorter[pl.ds(first, block), :] if keep else one_hot_sort(place_row, first, block)
            x_here = dot(onehot, x_all[part].reshape(rows, size))
            ux[pl.ds(pl.multiple_of(first + PAD, PAD), block), :] = x_here

        every(rows // block, gather_x)
        state[...] = jnp.zeros_like(state)

        def chunk(c):
            for i in range(4):
                scan_chunk(
                    4 * c + i, part, parts, starts, ux, xpar_ref, bcs, ws, ent, tails, carries, state, ys, owned
                )

        every(rows // CHUNK // 4, chunk)

        def scatter(i):
            b = lax.rem(me * tok // block + 1 + i, rows // block)
            first = pl.multiple_of(b * block, block)
            onehot = unsorter[pl.ds(first, block), :] if keep else one_hot_unsort(place_col, first, block)
            back = dot(onehot, ys[...]).astype(BF16)
            for j in range(block // tok):
                owner = b * (block // tok) + j
                sent[part, owner] = back[j * tok : (j + 1) * tok, :]

                @pl.when(owner != me)
                def _():
                    out_copy(part, owner).start()

        every(rows // block, scatter)
        tile(out_ref, part, me)[...] = sent[part, me]

    def finish(k):
        source = lax.rem(me + k, n)
        for part in range(parts):
            slot = tile(out_ref, part, source)
            remote(slot, slot, gate_send.at[0], out_recv.at[part, source], source).wait_recv()
            out_copy(part, source).wait_send()
            x_copy(part, k).wait_send()

    every(n, finish, 1)

    def finish_aux(k):
        for hop in range(3):
            relay(k, hop).wait_send()

    every(n // plane, finish_aux)
    every(n // plane, lambda k: far(k).wait_send(), 1)


def per_device(
    x_rows, bc_rows, step, route, doc_lengths, conv_weight, conv_bias, rate, skip, clip_level
):
    seq_count = lax.axis_size("seq")
    tok_rows, hp_width = x_rows.shape
    heads = step.shape[1]
    owned = heads // seq_count
    width = hp_width // seq_count
    state2 = bc_rows.shape[1]
    rows = tok_rows * seq_count

    spare = jnp.zeros((tok_rows, LANES - heads - 1), BF16)
    aux = jnp.concatenate([bc_rows, step, route.astype(BF16), spare], axis=1)
    parts = 2 if width % (2 * LANES) == 0 and owned % 2 == 0 else 1
    plane = 4
    size = width // parts
    keep = rows if rows <= 2048 else 16
    flat = size % LANES == 0
    x_send = x_rows if flat else jnp.swapaxes(x_rows.reshape(tok_rows, seq_count, width), 0, 1)

    vmem = pl.BlockSpec(memory_space=pltpu.VMEM)
    dma = pltpu.SemaphoreType.DMA
    out = pl.pallas_call(
        functools.partial(kernel, owned, heads, parts, plane),
        out_shape=jax.ShapeDtypeStruct(x_send.shape, BF16),
        in_specs=[pl.BlockSpec(memory_space=pltpu.SMEM)] * 4 + [vmem] * 4,
        out_specs=vmem,
        scratch_shapes=[
            pltpu.VMEM((8, width), F32),
            pltpu.VMEM((8, state2), F32),
            pltpu.VMEM((1, LANES), F32),
            pltpu.VMEM((LANES, LANES), BF16),
            pltpu.VMEM((seq_count, tok_rows, aux.shape[1]), BF16),
            pltpu.VMEM((parts, seq_count, tok_rows, size), BF16),
            pltpu.VMEM((parts, seq_count, tok_rows, size), BF16),
            pltpu.VMEM((rows, LANES), F32),
            pltpu.VMEM((8, rows), F32),
            pltpu.VMEM((rows, LANES), F32),
            pltpu.VMEM((PAD + rows, state2), F32),
            pltpu.VMEM((PAD + rows, size), F32),
            pltpu.VMEM((rows, LANES), F32),
            pltpu.VMEM((rows, state2), BF16),
            pltpu.VMEM((owned, rows, CHUNK), BF16),
            pltpu.VMEM((rows, width), F32),
            pltpu.VMEM((rows, width), F32),
            pltpu.VMEM((rows // CHUNK, 8, width), F32),
            pltpu.VMEM((rows, size), BF16),
            pltpu.VMEM((state2 // 2, size), F32),
            pltpu.VMEM((keep, keep), BF16),
            pltpu.VMEM((keep, keep), BF16),
            dma((seq_count // plane,)),
            dma((seq_count,)),
            dma((seq_count // plane, 3)),
            dma((parts, seq_count)),
            dma((parts, seq_count)),
            dma((parts, seq_count)),
            dma((parts, seq_count)),
        ],
        compiler_params=pltpu.CompilerParams(
            vmem_limit_bytes=60 * 1024 * 1024, collective_id=0, has_side_effects=True
        ),
    )(doc_lengths, rate, skip, clip_level, x_send, aux, conv_weight, conv_bias[None, :])
    return out if flat else jnp.swapaxes(out, 0, 1).reshape(tok_rows, hp_width)


SUB = 256
SMALL = 16


def fast_conv(rows, taps, bias, off):
    size = off.shape[0]
    acc = bias + taps[0:1, :] * rows[PAD : PAD + size, :]
    for j in range(1, 4):
        back = rows[PAD - j : PAD - j + size, :]
        acc = acc + taps[j : j + 1, :] * jnp.where(off >= j, back, 0.0)
    half = 0.5 * acc
    return (half + half * jnp.tanh(half)).astype(BF16)


def fast_kernel(
    owned, parts, plane, docs_ref, rates, skips, clips, x_ref, bc_ref, step_ref, route_ref, weight_ref, bias_ref, out_ref,
    step_v, route_v, x_taps, bc_taps, bias_v, small_out, small_all, bc_all, x_all, sent, off_ref,
    sorter, unsorter, columns, dt_left, dt_right, places, ub, ux, lhs, b_flip, rise, fall, by_chunk, ys, state,
    load_sem, small_send, small_recv, gate_send, gate_recv, plane_send, x_send, x_recv, own_sem, out_send, out_recv,
):
    n, tok, state2 = bc_all.shape
    rows, size = ys.shape
    heads = step_v.shape[0]
    chunks = rows // CHUNK
    width = size * parts
    local = owned // parts
    me = lax.axis_index("seq")
    inside = lax.rem(me, plane)
    iota = functools.partial(lax.broadcasted_iota, jnp.int32)

    def remote(source, target, send, recv, peer):
        return pltpu.make_async_remote_copy(
            src_ref=source, dst_ref=target, send_sem=send, recv_sem=recv,
            device_id={"seq": peer}, device_id_type=pl.DeviceIdType.MESH,
        )

    def every(count, do, first=0):
        def turn(k, _):
            do(k)
            return 0

        lax.fori_loop(first, count, turn, 0)

    def tile(ref, part, owner):
        return ref.at[:, pl.ds(pl.multiple_of((owner * parts + part) * size, size), size)]

    barrier = pltpu.get_barrier_semaphore()

    def greet(k):
        pl.semaphore_signal(
            barrier, inc=1, device_id={"seq": lax.rem(me + k, n)}, device_id_type=pl.DeviceIdType.MESH
        )

    own = pl.ds(pl.multiple_of(me * width, width), width)
    shared_at = weight_ref.shape[1] - state2
    loads = [
        pltpu.make_async_copy(bc_ref, bc_all.at[me], load_sem.at[0]),
        pltpu.make_async_copy(step_ref, step_v, load_sem.at[1]),
        pltpu.make_async_copy(route_ref, route_v, load_sem.at[2]),
        pltpu.make_async_copy(weight_ref.at[:, own], x_taps, load_sem.at[3]),
        pltpu.make_async_copy(weight_ref.at[:, shared_at:], bc_taps, load_sem.at[4]),
        pltpu.make_async_copy(bias_ref, bias_v, load_sem.at[5]),
    ]
    for load in loads[:3]:
        load.start()
    every(n, greet, 1)
    for load in loads[3:]:
        load.start()

    loads[1].wait()
    loads[2].wait()
    wide_step = step_v[...].astype(F32)
    wide_route = jnp.broadcast_to(route_v[...].astype(F32), (8, tok))
    for p in range(n):
        mine = wide_step[p * owned : (p + 1) * owned, :]
        block = jnp.concatenate([mine, jnp.zeros((8 - owned, tok), F32), wide_route], axis=0)
        small_out[p] = block.astype(BF16)
    small_all[me] = small_out[me]
    loads[0].wait()

    pl.semaphore_wait(barrier, n - 1)

    low_plane = lax.rem(me // plane, 2)
    mate_turn, last_turn = 1 + 2 * low_plane, 3 - 2 * low_plane

    def far(step):
        owner = lax.rem(me + 2 * plane, n) if step == 2 else me
        peer = lax.rem(me + (2 if step == 0 else mate_turn) * plane, n)
        return remote(bc_all.at[owner], bc_all.at[owner], gate_send.at[step], gate_recv.at[owner], peer)

    def small_copy(k):
        peer = lax.rem(me + k, n)
        return remote(small_out.at[peer], small_all.at[me], small_send.at[k], small_recv.at[me], peer)

    def landed(ref, sems, slot):
        return remote(ref.at[slot], ref.at[slot], gate_send.at[0], sems.at[slot], slot)

    across = me - inside + lax.rem(inside + 2, plane)
    sibling = me + 1 - 2 * lax.rem(me, 2)

    def relay(k, hop):
        owner = lax.rem((across if hop == 2 else me) + k * plane, n)
        peer = across if hop == 0 else sibling
        return remote(bc_all.at[owner], bc_all.at[owner], plane_send.at[k, hop], gate_recv.at[owner], peer)

    def x_copy(part, peer):
        return remote(tile(x_ref, part, peer), x_all.at[part, me], x_send.at[part, peer], x_recv.at[part, me], peer)

    planes = n // plane
    half = planes // 2
    mine = me // plane

    def plane_at(i):
        turn = lax.rem(i, half)
        side = lax.rem(mine // half + 1 + i // half, 2)
        return side * half + lax.rem(lax.rem(mine, half) + turn + i // half, half)

    def own_copy(part):
        return pltpu.make_async_copy(tile(x_ref, part, me), x_all.at[part, me], own_sem.at[part])

    def start_at(moment):
        for part, turn, *span in SCHEDULE.get(moment, ()):
            begin, end = span or (0, plane)
            first = plane_at(jnp.int32(turn)) * plane

            def to_peer(j, part=part, first=first):
                peer = first + lax.rem(inside + 1 + j, plane)

                @pl.when(peer != me)
                def _():
                    x_copy(part, peer).start()

            every(end, to_peer, begin)

    every(n, lambda k: small_copy(k).start(), 1)
    far(0).start()
    far(1).start()
    relay(0, 0).start()
    relay(0, 1).start()
    start_at(0)
    for part in range(parts):
        own_copy(part).start()

    starts, total = [], jnp.int32(0)
    for k in range(docs_ref.shape[0]):
        starts.append(total)
        total = total + docs_ref[k]

    def begins(at):
        begin = jnp.zeros(at.shape, jnp.int32)
        for start in starts:
            begin = jnp.where(at >= start, start, begin)
        return begin

    low, high = iota((CHUNK, CHUNK), 0), iota((CHUNK, CHUNK), 1)

    def make_off(c):
        base = pl.multiple_of(c * CHUNK, CHUNK)
        at = low + base
        off_ref[pl.ds(base, CHUNK), :] = (at - begins(at)).astype(F32)

    every(chunks, make_off)

    def small_landed(k):
        landed(small_all, small_recv, lax.rem(me + k, n)).wait_recv()

    every(n, small_landed, 1)

    def find_places():
        number = iota((n, tok), 0).astype(F32)
        named = []
        for i in range(n):
            target = jnp.concatenate([small_all[i].astype(F32)[8:, :]] * (n // 8), axis=0)
            named.append(jnp.where(target == number, 1.0, 0.0))
        earlier = jnp.where(low < high, 1.0, 0.0).astype(BF16)
        right = jnp.concatenate([earlier, jnp.ones((tok, tok), BF16)], axis=1)
        found = dot(jnp.concatenate(named, axis=0).astype(BF16), right)
        before = jnp.zeros((n, tok), F32)
        ranks = []
        for i in range(n):
            here = found[i * n : (i + 1) * n, :]
            ranks.append(here[:, :tok] + before)
            before = before + here[:, tok:]
        base = jnp.zeros((n, tok), F32)
        for d in range(n - 1):
            base = base + jnp.where(number > d, before[d : d + 1, :], 0.0)
        all_places = []
        for i in range(n):
            place = jnp.sum(named[i] * (ranks[i] + base), axis=0, keepdims=True)
            places[i : i + 1, :] = place
            all_places.append(place)
            coarse = jnp.floor(place * (1.0 / CHUNK))
            fine = place - coarse * CHUNK
            lanes = slice(i * tok, (i + 1) * tok)
            steps = small_all[i].astype(F32)[0:8, :]
            split = [jnp.where(coarse == c, steps, 0.0) for c in range(chunks)]
            dt_left[:, lanes] = jnp.concatenate(split, axis=0).astype(BF16)
            dt_right[:, lanes] = jnp.where(low.astype(F32) == fine, 1.0, 0.0).astype(BF16)

    find_places()

    start_at(6)
    row16 = iota((SUB, tok), 0).astype(F32).astype(BF16)
    one, none = jnp.ones((), BF16), jnp.zeros((), BF16)

    def make_sorter(b):
        first = lax.convert_element_type(b * SUB, F32)
        for i in range(n):
            rel = places[i : i + 1, :] - first
            rel = jnp.where((rel >= 0.0) & (rel < SUB), rel, -1.0)
            rel = jnp.broadcast_to(rel, (SUB, tok)).astype(BF16)
            hit = jnp.where(row16 == rel, one, none)
            sorter[pl.ds(pl.multiple_of(b * SUB, SUB), SUB), i * tok : (i + 1) * tok] = hit

    every(rows // SUB, make_sorter)

    start_at(8)
    def forward(k):
        landed(bc_all, gate_recv, lax.rem(me + k * plane, n)).wait_recv()
        if isinstance(k, int):
            far(2).start()
        relay(k, 0).start()
        relay(k, 1).start()

    forward(2)
    forward(mate_turn)
    start_at(7)
    forward(last_turn)
    start_at(1)

    def decays():
        dts = dot_nt(dt_left[...], dt_right[...])
        lane = iota((8, CHUNK), 1)
        slot = iota((8, CHUNK), 0)
        rate = jnp.zeros((8, CHUNK), F32)
        for h in range(owned):
            rate = jnp.where(slot == h, rates[me * owned + h], rate)
        rate = jnp.concatenate([rate] * chunks, axis=0)
        upto = jnp.where(low <= high, 1.0, 0.0).astype(BF16)
        cum = -dot(dts.astype(BF16), upto) * rate
        last = jnp.broadcast_to(cum[:, CHUNK - 1 :], cum.shape)
        middle = 0.5 * last
        up = jnp.exp(cum - middle)
        down = jnp.exp(middle - cum) * dts
        gain = jnp.exp(middle)
        number = iota((8 * chunks, CHUNK), 0) // 8
        ends = number * CHUNK + CHUNK - 1
        goes_on = jnp.where(begins(ends) < number * CHUNK, 1.0, 0.0)
        carry = jnp.exp(last) * goes_on
        by_chunk[0] = up
        by_chunk[1] = down
        by_chunk[2] = gain
        by_chunk[3] = carry

    decays()

    head = iota((1, size), 1) // (size // local)

    def spread(columns, part):
        out = jnp.broadcast_to(columns[:, part * local : part * local + 1], (CHUNK, size))
        for h in range(1, local):
            at = part * local + h
            out = jnp.where(head == h, jnp.broadcast_to(columns[:, at : at + 1], (CHUNK, size)), out)
        return out

    def expand(part):
        pair = by_chunk[0].reshape(chunks, 8, CHUNK)[:, :4], by_chunk[1].reshape(chunks, 8, CHUNK)[:, :4]
        turned = jnp.concatenate(pair, axis=1).reshape(8 * chunks, CHUNK).T
        for c in range(chunks):
            at = slice(c * CHUNK, (c + 1) * CHUNK)
            rise[part, at, :] = spread(turned[:, 8 * c :], part)
            fall[part, at, :] = spread(turned[:, 8 * c + 4 :], part)

    expand(0)

    def crossed(k):
        landed(bc_all, gate_recv, lax.rem(across + k * plane, n)).wait_recv()
        relay(k, 2).start()

    for k in (0, 2, mate_turn, last_turn):
        crossed(k)

    start_at(2)

    block = plane * tok
    core = lax.rem(me, 2)
    ub[0:PAD, :] = jnp.zeros((PAD, state2), F32)

    def gather(b, side):
        first = pl.multiple_of(b * block, block)
        owners = [2 * i + side for i in range(n // 2)]
        lefts = [sorter[pl.ds(first, block), pl.ds(pl.multiple_of(o * tok, tok), tok)] for o in owners]
        here = dot(jnp.concatenate(lefts, axis=1), jnp.concatenate([bc_all[o] for o in owners], axis=0))
        at = pl.ds(pl.multiple_of(first + PAD, PAD), block)
        ub[at, :] = here if side is core else ub[at, :] + here

    every(rows // block, lambda b: gather(b, core))

    lane16 = [(iota((tok, LANES), 1) + j * LANES).astype(F32).astype(BF16) for j in range(SUB // LANES)]
    flipped = jnp.concatenate([places[...], jnp.zeros((tok - n, tok), F32)], axis=0).T
    flipped_coarse = jnp.floor(flipped * (1.0 / SUB))
    flipped_fine = flipped - flipped_coarse * SUB

    def make_columns():
        for i in range(n):
            at = slice(i * tok, (i + 1) * tok)
            columns[0, at, :] = jnp.broadcast_to(flipped_coarse[:, i : i + 1], (tok, LANES)).astype(BF16)
            columns[1, at, :] = jnp.broadcast_to(flipped_fine[:, i : i + 1], (tok, LANES)).astype(BF16)

    def make_unsorter(i):
        at = pl.ds(pl.multiple_of(i * tok, tok), tok)
        coarse, fine = columns[0, at, :], columns[1, at, :]
        for b in range(rows // SUB):
            rel = jnp.where(coarse == jnp.full((), b, BF16), fine, -one)
            for j in range(SUB // LANES):
                unsorter[at, b * SUB + j * LANES : b * SUB + (j + 1) * LANES] = jnp.where(lane16[j] == rel, one, none)

    start_at(9)
    make_columns()

    def rest(k):
        for hop in (0, 2):
            owner = sibling - lax.rem(sibling, plane) + lax.rem(lax.rem(sibling, plane) + hop, plane)
            landed(bc_all, gate_recv, lax.rem(owner + k * plane, n)).wait_recv()

    every(n // plane, rest)

    start_at(3)

    for load in loads[3:]:
        load.wait()
    ux[0:PAD, :] = jnp.zeros((PAD, size), F32)
    every(rows // block, lambda b: gather(b, 1 - core))
    start_at(4)

    gap = low - high

    def wide_bias(first, count):
        return jnp.concatenate([bias_v[pl.ds(first + i, 1), :] for i in range(count)], axis=1)

    def shared(c):
        base = pl.multiple_of(c * CHUNK, CHUNK)
        off = off_ref[pl.ds(base, CHUNK), :]
        off2 = jnp.concatenate([off] * (state2 // LANES), axis=1)
        bias = wide_bias(shared_at // LANES, state2 // LANES)
        act = fast_conv(ub[pl.ds(base, CHUNK + PAD), :], bc_taps[...], bias, off2)
        b_mat, c_mat = act[:, : state2 // 2], act[:, state2 // 2 :]
        scores = dot_nt(c_mat, b_mat)
        keep = (gap >= 0) & (gap.astype(F32) <= off)
        lhs[pl.ds(base, CHUNK), :CHUNK] = jnp.where(keep, scores, 0.0).astype(BF16)
        runs_in = jnp.where(off > low.astype(F32), c_mat.astype(F32), 0.0)
        lhs[pl.ds(base, CHUNK), CHUNK:] = runs_in.astype(BF16)
        runs_out = high[0:1, :].astype(F32) + off[CHUNK - 1 :, :] >= CHUNK - 1
        b_flip[pl.ds(base, CHUNK), :] = jnp.where(runs_out, b_mat.astype(F32).T, 0.0).astype(BF16)

    every(chunks // 4, lambda c: [shared(4 * c + i) for i in range(4)])
    start_at(5)

    def out_copy(part, owner):
        return remote(
            sent.at[part, owner], tile(out_ref, part, me), out_send.at[part, owner], out_recv.at[part, me], owner
        )

    def own_out(part):
        return pltpu.make_async_copy(sent.at[part, me], tile(out_ref, part, me), own_sem.at[parts + part])

    lane_head = iota((1, size), 1) // (size // local)

    def by_head(values):
        out = jnp.full((1, size), values[0], F32)
        for h in range(1, local):
            out = jnp.where(lane_head == h, values[h], out)
        return out

    def finish_aux():
        every(n, lambda k: small_copy(k).wait_send(), 1)
        for step in range(3):
            far(step).wait_send()
        for k in range(n // plane):
            for hop in range(3):
                relay(k, hop).wait_send()

    for part in range(parts):

        def x_landed(k):
            source = lax.rem(me + k, n)
            slot = x_all.at[part, source]
            remote(slot, slot, gate_send.at[0], x_recv.at[part, source], source).wait_recv()

        if part > 0:
            expand(part)
        if part == 1:
            finish_aux()
        if part > 0:
            every(n, lambda k: x_copy(part - 1, lax.rem(me + k, n)).wait_send(), 1)
        own_copy(part).wait()
        every(n, x_landed, 1)

        def gather_x(b):
            first = pl.multiple_of(b * block, block)
            here = dot(sorter[pl.ds(first, block), :], x_all[part].reshape(rows, size))
            ux[pl.ds(pl.multiple_of(first + PAD, PAD), block), :] = here

        every(rows // block, gather_x)
        state[...] = jnp.zeros_like(state)
        skip = by_head([skips[me * owned + part * local + h] for h in range(local)])
        level = by_head([clips[me * owned + part * local + h] for h in range(local)])

        def chunk(c):
            base = pl.multiple_of(c * CHUNK, CHUNK)
            at = pl.ds(base, CHUNK)
            bias = bias_v[pl.ds(me * parts + part, 1), :]
            taps = x_taps[:, part * size : (part + 1) * size]
            wide = fast_conv(ux[pl.ds(base, CHUNK + PAD), :], taps, bias, off_ref[at, :]).astype(F32)
            scaled = (wide * fall[part, at, :]).astype(BF16)
            at8 = pl.ds(pl.multiple_of(c * 8, 8), 8)
            gains, carries = by_chunk[2, at8, :], by_chunk[3, at8, :]
            gain = by_head([gains[part * local + h : part * local + h + 1, :] for h in range(local)])
            carry = by_head([carries[part * local + h : part * local + h + 1, :] for h in range(local)])
            old = state[...]
            right = jnp.concatenate([scaled, (gain * old).astype(BF16)], axis=0)
            y = skip * wide + rise[part, at, :] * dot(lhs[at, :], right)
            ys[at, :] = jnp.clip(y, -level, level).astype(BF16)
            state[...] = carry * old + gain * dot(b_flip[at, :], scaled)

        every(chunks // 4, lambda c: [chunk(4 * c + i) for i in range(4)])

        def scatter(i):
            b = plane_at(i)
            first = pl.multiple_of(b * block, block)
            if part == 0:
                every(plane, lambda j: make_unsorter(b * plane + j))
            back = dot(unsorter[pl.ds(first, block), :], ys[...]).astype(BF16)
            for j in range(block // tok):
                owner = b * (block // tok) + j
                sent[part, owner] = back[j * tok : (j + 1) * tok, :]

                @pl.when(owner != me)
                def _():
                    out_copy(part, owner).start()

        every(rows // block, scatter)
        own_out(part).start()

    def x_sent(part):
        every(n, lambda k: x_copy(part, lax.rem(me + k, n)).wait_send(), 1)

    def finish(part):
        def from_plane(i):
            for j in range(plane):
                source = plane_at(i) * plane + lax.rem(inside + 1 + j, plane)

                @pl.when(source != me)
                def _():
                    slot = tile(out_ref, part, source)
                    out_copy(part, source).wait_send()
                    remote(slot, slot, gate_send.at[0], out_recv.at[part, source], source).wait_recv()

        every(planes, from_plane)

    x_sent(parts - 1)
    for part in range(parts):
        own_out(part).wait()
        finish(part)


def fast_device(
    x_rows, bc_rows, step, route, doc_lengths, conv_weight, conv_bias, rate, skip, clip_level
):
    n = lax.axis_size("seq")
    tok, hp_width = x_rows.shape
    heads = step.shape[1]
    owned = heads // n
    width = hp_width // n
    state2 = bc_rows.shape[1]
    rows = tok * n
    parts = width // LANES
    size = LANES
    plane = 4
    chunks = rows // CHUNK
    bias = conv_bias.reshape(conv_bias.shape[0] // LANES, LANES)

    hbm = pl.BlockSpec(memory_space=pl.ANY)
    dma = pltpu.SemaphoreType.DMA
    return pl.pallas_call(
        functools.partial(fast_kernel, owned, parts, plane),
        out_shape=jax.ShapeDtypeStruct(x_rows.shape, BF16),
        in_specs=[pl.BlockSpec(memory_space=pltpu.SMEM)] * 4 + [hbm] * 6,
        out_specs=OUT_SPEC,
        scratch_shapes=[
            pltpu.VMEM((heads, tok), BF16),
            pltpu.VMEM((1, tok), jnp.int32),
            pltpu.VMEM((4, width), F32),
            pltpu.VMEM((4, state2), F32),
            pltpu.VMEM(bias.shape, F32),
            pltpu.VMEM((n, SMALL, tok), BF16),
            pltpu.VMEM((n, SMALL, tok), BF16),
            pltpu.VMEM((n, tok, state2), BF16),
            pltpu.VMEM((parts, n, tok, size), BF16),
            pltpu.VMEM((parts, n, tok, size), BF16),
            pltpu.VMEM((rows, LANES), F32),
            pltpu.VMEM((rows, rows), BF16),
            pltpu.VMEM((rows, rows), BF16),
            pltpu.VMEM((2, rows, LANES), BF16),
            pltpu.VMEM((8 * chunks, rows), BF16),
            pltpu.VMEM((CHUNK, rows), BF16),
            pltpu.VMEM((n, tok), F32),
            pltpu.VMEM((PAD + rows, state2), F32),
            pltpu.VMEM((PAD + rows, size), F32),
            pltpu.VMEM((rows, 2 * CHUNK), BF16),
            pltpu.VMEM((rows, CHUNK), BF16),
            pltpu.VMEM((parts, rows, size), F32),
            pltpu.VMEM((parts, rows, size), F32),
            pltpu.VMEM((4, 8 * chunks, CHUNK), F32),
            pltpu.VMEM((rows, size), BF16),
            pltpu.VMEM((state2 // 2, size), F32),
            dma((6,)),
            dma((n,)),
            dma((n,)),
            dma((n // plane,)),
            dma((n,)),
            dma((n // plane, 3)),
            dma((parts, n)),
            dma((parts, n)),
            dma((2 * parts,)),
            dma((parts, n)),
            dma((parts, n)),
        ],
        compiler_params=pltpu.CompilerParams(
            vmem_limit_bytes=48 * 1024 * 1024, collective_id=1, has_side_effects=True
        ),
    )(*[pltpu.with_memory_space_constraint(a, pltpu.HBM) for a in (
        doc_lengths, rate, skip, clip_level, x_rows, bc_rows, step.T, route.T, conv_weight, bias
    )])


def fits_fast(n, x_shape, heads, state2):
    width = x_shape[1] // n
    owned = heads // n
    return (
        n == 16 and n * x_shape[0] <= 2048 and x_shape[0] == LANES and width % LANES == 0 and state2 == 2 * CHUNK
        and owned == 4 and width // LANES == 2 and 8 * n * LANES // CHUNK <= CHUNK
    )


def solution(mesh):
    placed = (
        P(("groups", "seq"), None),
        P(("groups", "seq"), None),
        P(("groups", "seq"), None),
        P(("groups", "seq"), None),
        P("groups"),
        P(),
        P(),
        P(),
        P(),
        P(),
    )

    def run(*arrays):
        x_rows, bc_rows, step = arrays[:3]
        fast = fits_fast(lax.axis_size("seq"), x_rows.shape, step.shape[1], bc_rows.shape[1])
        return (fast_device if fast else per_device)(*arrays)

    return jax.shard_map(
        run,
        mesh=mesh,
        in_specs=placed,
        out_specs=P(("groups", "seq"), None),
        check_vma=False,
    )
```

```python
import functools

import jax
import jax.numpy as jnp
from jax import lax
from jax.experimental import pallas as pl
from jax.experimental.pallas import tpu as pltpu
from jax.sharding import PartitionSpec as P

F32 = jnp.float32
BF16 = jnp.bfloat16
CHUNK = 128
LANES = 128
PAD = 8
SCHEDULE = {
    0: ((0, 0, 0, 2),),
    7: ((0, 0, 2, 4),),
    1: ((0, 1),),
    2: ((0, 2), (0, 3)),
    3: ((1, 0), (1, 1), (1, 2), (1, 3)),
}
OUT_SPEC = pl.BlockSpec(memory_space=pl.ANY)


def dot(a, b):
    return jnp.dot(a, b, preferred_element_type=F32)


def dot_nt(a, b):
    return lax.dot_general(a, b, (((1,), (1,)), ((), ())), preferred_element_type=F32)


def dot_tn(a, b):
    return lax.dot_general(a, b, (((0,), (0,)), ((), ())), preferred_element_type=F32)


def find_places(aux_ref, ranks, place_row, place_col, heads):
    rows = ranks.shape[0]
    state2 = aux_ref.shape[2] - LANES
    low = lax.broadcasted_iota(jnp.int32, (LANES, LANES), 0)
    high = lax.broadcasted_iota(jnp.int32, (LANES, LANES), 1)
    earlier = jnp.where(low > high, 1.0, 0.0).astype(BF16)
    before = jnp.where(low < high, 1.0, 0.0).astype(BF16)
    shard = high.astype(F32)
    step = 4

    def named(b):
        target = aux_ref[b, :, state2 : state2 + LANES].astype(F32)[:, heads : heads + 1]
        return jnp.where(target == shard, 1.0, 0.0)

    def count(i, total):
        for j in range(step):
            b = i * step + j
            onehot = named(b)
            ranks[pl.ds(pl.multiple_of(b * LANES, LANES), LANES), :] = dot(earlier, onehot.astype(BF16)) + total
            total = total + jnp.sum(onehot, axis=0, keepdims=True)
        return total

    total = lax.fori_loop(0, rows // LANES // step, count, jnp.zeros((1, LANES), F32))
    total = jnp.broadcast_to(total, (8, LANES))
    coarse = jnp.floor(total * (1.0 / 64.0))
    fine = total - coarse * 64.0
    start = (dot(coarse.astype(BF16), before) * 64.0 + dot(fine.astype(BF16), before))[0:1, :]

    def rank(i, _):
        for j in range(step):
            b = i * step + j
            at = pl.multiple_of(b * LANES, LANES)
            found = named(b) * (ranks[pl.ds(at, LANES), :] + start)
            place = jnp.broadcast_to(jnp.sum(found, axis=1, keepdims=True), (LANES, LANES))
            place_col[pl.ds(at, LANES), :] = place
            place_row[:, pl.ds(at, LANES)] = place.T[0:8, :]
        return 0

    lax.fori_loop(0, rows // LANES // step, rank, 0)


def one_hot_sort(place_row, first, size):
    rows = place_row.shape[1]
    number = lax.broadcasted_iota(jnp.int32, (size, rows), 0).astype(F32)
    hit = place_row[0:1, :] - lax.convert_element_type(first, F32) == number
    return jnp.where(hit, 1.0, 0.0).astype(BF16)


def one_hot_unsort(place_col, first, size):
    rows = place_col.shape[0]
    number = lax.broadcasted_iota(jnp.int32, (size, rows), 1).astype(F32)
    place = place_col[pl.ds(first, size), :]
    hit = jnp.concatenate([place] * (rows // LANES), axis=1) == number
    return jnp.where(hit, 1.0, 0.0).astype(BF16)


def doc_begins(at, starts):
    begin = jnp.zeros((CHUNK, 1), jnp.int32)
    for start in starts:
        begin = jnp.where(at >= start, start, begin)
    return begin


def conv_silu(v, par, at, begin):
    acc = par[4:5, :] + par[0:1, :] * v[PAD:, :]
    for j in range(1, 4):
        keep = jnp.where(at - j >= begin, 1.0, 0.0)
        acc = acc + par[j : j + 1, :] * (v[PAD - j : PAD - j + CHUNK, :] * keep)
    return (acc / (1.0 + jnp.exp(-acc))).astype(BF16)


def shared_chunk(c, starts, ub, ds, bcpar_ref, rate_ref, bcs, ws, ent, tails, carries, owned):
    width = ent.shape[1]
    state_width = bcs.shape[1] // 2
    base = pl.multiple_of(c * CHUNK, CHUNK)
    at = lax.broadcasted_iota(jnp.int32, (CHUNK, 1), 0) + base
    begin = doc_begins(at, starts)
    begin_last = begin[CHUNK - 1 :, :]
    act = conv_silu(ub[pl.ds(base, CHUNK + PAD), :], bcpar_ref[...], at, begin)
    bcs[pl.ds(base, CHUNK), :] = act
    b_mat, c_mat = act[:, :state_width], act[:, state_width:]

    dt = ds[pl.ds(base, CHUNK), :]
    low = lax.broadcasted_iota(jnp.int32, (CHUNK, CHUNK), 0)
    high = lax.broadcasted_iota(jnp.int32, (CHUNK, CHUNK), 1)
    tri = jnp.where(low >= high, 1.0, 0.0).astype(BF16)
    cum = -dot(tri, dt.astype(BF16)) * rate_ref[...]
    shifted = (cum - jnp.log(jnp.maximum(dt, 1e-30))).T
    cum_last = cum[CHUNK - 1 :, :]
    scores = dot_nt(c_mat, b_mat)
    scores = jnp.where((low >= high) & (high + base >= begin), scores, 0.0)
    head = lax.broadcasted_iota(jnp.int32, (1, width), 1) // (width // owned)

    def expand(e):
        out = jnp.broadcast_to(e[:, 0:1], (e.shape[0], width))
        for h in range(1, owned):
            out = jnp.where(head == h, e[:, h : h + 1], out)
        return out

    for h in range(owned):
        decay = jnp.exp(cum[:, h : h + 1] - shifted[h : h + 1, :])
        ws[h, pl.ds(base, CHUNK), :] = (scores * decay).astype(BF16)
    ent[pl.ds(base, CHUNK), :] = expand(jnp.exp(cum) * jnp.where(begin < base, 1.0, 0.0))
    tail = jnp.exp(cum_last - cum) * dt * jnp.where(at >= begin_last, 1.0, 0.0)
    tails[pl.ds(base, CHUNK), :] = expand(tail)
    carry = expand(jnp.exp(cum_last) * jnp.where(begin_last < base, 1.0, 0.0))
    carries[c] = jnp.broadcast_to(carry, (8, width))


def scan_chunk(c, part, parts, starts, ux, xpar_ref, bcs, ws, ent, tails, carries, state, ys, owned):
    size = ux.shape[1]
    lanes = slice(part * size, (part + 1) * size)
    state_width = bcs.shape[1] // 2
    base = pl.multiple_of(c * CHUNK, CHUNK)
    at = lax.broadcasted_iota(jnp.int32, (CHUNK, 1), 0) + base
    begin = doc_begins(at, starts)
    x_mat = conv_silu(ux[pl.ds(base, CHUNK + PAD), :], xpar_ref[:, lanes], at, begin)
    x_wide = x_mat.astype(F32)
    bc = bcs[pl.ds(base, CHUNK), :]
    b_mat, c_mat = bc[:, :state_width], bc[:, state_width:]
    local = owned // parts
    head = lax.broadcasted_iota(jnp.int32, (1, size), 1) // (size // local)
    y = xpar_ref[5:6, lanes] * x_wide
    for h in range(local):
        mine = jnp.where(head == h, x_wide, 0.0).astype(BF16)
        y = y + dot(ws[part * local + h, pl.ds(base, CHUNK), :], mine)
    y = y + dot(c_mat, state[...].astype(BF16)) * ent[pl.ds(base, CHUNK), lanes]
    limit = xpar_ref[6:7, lanes]
    ys[pl.ds(base, CHUNK), :] = jnp.clip(y, -limit, limit).astype(BF16)
    scaled = (x_wide * tails[pl.ds(base, CHUNK), lanes]).astype(BF16)
    state[...] = carries[c][0:1, lanes] * state[...] + dot_tn(b_mat, scaled)


def kernel(
    owned, heads, parts, plane, docs_ref, rates, skips, clips, x_ref, aux_ref, weight_ref, bias_ref, out_ref,
    xpar_ref, bcpar_ref, rate_ref, pick_ref, aux_all, x_all, sent, keys, place_row, place_col, ub, ux, ds, bcs, ws, ent, tails, carries, ys, state,
    sorter, unsorter, gate_send, gate_recv, plane_send, x_send, x_recv, out_send, out_recv,
):
    n, tok = x_all.shape[1:3]
    rows, size = ys.shape
    state2 = bcs.shape[1]
    flat = len(x_ref.shape) == 2
    block = max(tok, min(512, (1 << 20) // rows))
    keep = sorter.shape[0] == rows
    me = lax.axis_index("seq")
    inside = lax.rem(me, plane)

    def remote(source, target, send, recv, peer):
        return pltpu.make_async_remote_copy(
            src_ref=source, dst_ref=target, send_sem=send, recv_sem=recv,
            device_id={"seq": peer}, device_id_type=pl.DeviceIdType.MESH,
        )

    def every(count, do, first=0):
        def turn(k, _):
            do(k)
            return 0

        lax.fori_loop(first, count, turn, 0)

    def tile(ref, part, owner):
        if flat:
            return ref.at[:, pl.ds(pl.multiple_of((owner * parts + part) * size, size), size)]
        return ref.at[owner]

    def own_lanes(ref):
        width = size * parts
        if width % LANES == 0:
            return ref[:, pl.ds(pl.multiple_of(me * width, LANES), width)]
        per = LANES // width
        wide = ref[:, pl.ds(pl.multiple_of(me // per * LANES, LANES), LANES)]
        picked = wide[:, :width]
        for i in range(1, per):
            picked = jnp.where(lax.rem(me, per) == i, wide[:, i * width : (i + 1) * width], picked)
        return picked

    def load_params():
        width = size * parts
        head = lax.broadcasted_iota(jnp.int32, (1, width), 1) // (width // owned)
        lane = lax.broadcasted_iota(jnp.int32, (1, LANES), 1)
        gain = level = jnp.zeros((1, width), F32)
        decay = jnp.zeros((1, LANES), F32)
        for h in range(owned):
            gain = jnp.where(head == h, skips[me * owned + h], gain)
            level = jnp.where(head == h, clips[me * owned + h], level)
            decay = jnp.where(lane == h, rates[me * owned + h], decay)
        xpar_ref[0:4, :] = own_lanes(weight_ref)
        xpar_ref[4:5, :] = own_lanes(bias_ref)
        xpar_ref[5:6, :] = gain
        xpar_ref[6:7, :] = level
        first = weight_ref.shape[1] - state2
        bcpar_ref[0:4, :] = weight_ref[:, first:]
        bcpar_ref[4:5, :] = bias_ref[:, first:]
        rate_ref[...] = decay
        source = lax.broadcasted_iota(jnp.int32, (LANES, LANES), 0)
        target = lax.broadcasted_iota(jnp.int32, (LANES, LANES), 1)
        hit = (source == target + me * owned) & (target < owned)
        pick_ref[...] = jnp.where(hit, 1.0, 0.0).astype(BF16)

    barrier = pltpu.get_barrier_semaphore()

    def greet(k):
        pl.semaphore_signal(
            barrier, inc=1, device_id={"seq": lax.rem(me + k, n)}, device_id_type=pl.DeviceIdType.MESH
        )

    every(n, greet, 1)
    pl.semaphore_wait(barrier, n - 1)

    def far(k):
        peer = lax.rem(me + k * plane, n)
        return remote(aux_ref, aux_all.at[me], gate_send.at[k], gate_recv.at[me], peer)

    def landed(ref, sems, slot):
        return remote(ref.at[slot], ref.at[slot], gate_send.at[0], sems.at[slot], slot)

    across = me - inside + lax.rem(inside + 2, plane)
    sibling = me + 1 - 2 * lax.rem(me, 2)

    def relay(k, hop):
        owner = lax.rem((across if hop == 2 else me) + k * plane, n)
        peer = across if hop == 0 else sibling
        return remote(aux_all.at[owner], aux_all.at[owner], plane_send.at[k, hop], gate_recv.at[owner], peer)

    def x_copy(part, k):
        peer = lax.rem(me + k, n)
        return remote(tile(x_ref, part, peer), x_all.at[part, me], x_send.at[part, k], x_recv.at[part, me], peer)

    every(n // plane, lambda k: far(k).start(), 1)
    aux_all[me] = aux_ref[...]
    relay(0, 0).start()
    relay(0, 1).start()

    def forward(k):
        landed(aux_all, gate_recv, lax.rem(me + k * plane, n)).wait_recv()
        relay(k, 0).start()
        relay(k, 1).start()

    every(n // plane, forward, 1)
    for part in range(parts):
        x_all[part, me] = tile(x_ref, part, me)[...]

    load_params()

    def crossed(k):
        landed(aux_all, gate_recv, lax.rem(across + k * plane, n)).wait_recv()
        relay(k, 2).start()

    every(n // plane, crossed)
    every(n, lambda k: x_copy(0, k).start(), 1)
    for part in range(1, parts):
        every(n, lambda k: x_copy(part, k).start(), 1)

    def rest(k):
        for hop in (0, 2):
            owner = sibling - lax.rem(sibling, plane) + lax.rem(lax.rem(sibling, plane) + hop, plane)
            landed(aux_all, gate_recv, lax.rem(owner + k * plane, n)).wait_recv()

    every(n // plane, rest)
    aux_rows = aux_all
    find_places(aux_rows, keys, place_row, place_col, heads)
    ub[0:PAD, :] = jnp.zeros((PAD, state2), F32)
    ux[0:PAD, :] = jnp.zeros((PAD, size), F32)

    def gather(b):
        first = pl.multiple_of(b * block, block)
        onehot = one_hot_sort(place_row, first, block)
        if keep:
            sorter[pl.ds(first, block), :] = onehot
        aux_here = dot(onehot, aux_all[...].reshape(rows, aux_all.shape[2]))
        ub[pl.ds(pl.multiple_of(first + PAD, PAD), block), :] = aux_here[:, :state2]
        ds[pl.ds(first, block), :] = dot(aux_here[:, state2:].astype(BF16), pick_ref[...])

    every(rows // block, gather)

    starts, total = [], jnp.int32(0)
    for k in range(docs_ref.shape[0]):
        starts.append(total)
        total = total + docs_ref[k]

    def shared(c):
        for i in range(4):
            shared_chunk(4 * c + i, starts, ub, ds, bcpar_ref, rate_ref, bcs, ws, ent, tails, carries, owned)

    every(rows // CHUNK // 4, shared)
    if keep:

        def prepare(b):
            first = pl.multiple_of(b * block, block)
            unsorter[pl.ds(first, block), :] = one_hot_unsort(place_col, first, block)

        every(rows // block, prepare)

    def out_copy(part, owner):
        return remote(
            sent.at[part, owner], tile(out_ref, part, me), out_send.at[part, owner], out_recv.at[part, me], owner
        )

    for part in range(parts):

        def x_landed(k):
            source = lax.rem(me + k, n)
            slot = x_all.at[part, source]
            remote(slot, slot, gate_send.at[0], x_recv.at[part, source], source).wait_recv()

        every(n, x_landed, 1)

        def gather_x(b):
            first = pl.multiple_of(b * block, block)
            onehot = sorter[pl.ds(first, block), :] if keep else one_hot_sort(place_row, first, block)
            x_here = dot(onehot, x_all[part].reshape(rows, size))
            ux[pl.ds(pl.multiple_of(first + PAD, PAD), block), :] = x_here

        every(rows // block, gather_x)
        state[...] = jnp.zeros_like(state)

        def chunk(c):
            for i in range(4):
                scan_chunk(
                    4 * c + i, part, parts, starts, ux, xpar_ref, bcs, ws, ent, tails, carries, state, ys, owned
                )

        every(rows // CHUNK // 4, chunk)

        def scatter(i):
            b = lax.rem(me * tok // block + 1 + i, rows // block)
            first = pl.multiple_of(b * block, block)
            onehot = unsorter[pl.ds(first, block), :] if keep else one_hot_unsort(place_col, first, block)
            back = dot(onehot, ys[...]).astype(BF16)
            for j in range(block // tok):
                owner = b * (block // tok) + j
                sent[part, owner] = back[j * tok : (j + 1) * tok, :]

                @pl.when(owner != me)
                def _():
                    out_copy(part, owner).start()

        every(rows // block, scatter)
        tile(out_ref, part, me)[...] = sent[part, me]

    def finish(k):
        source = lax.rem(me + k, n)
        for part in range(parts):
            slot = tile(out_ref, part, source)
            remote(slot, slot, gate_send.at[0], out_recv.at[part, source], source).wait_recv()
            out_copy(part, source).wait_send()
            x_copy(part, k).wait_send()

    every(n, finish, 1)

    def finish_aux(k):
        for hop in range(3):
            relay(k, hop).wait_send()

    every(n // plane, finish_aux)
    every(n // plane, lambda k: far(k).wait_send(), 1)


def per_device(
    x_rows, bc_rows, step, route, doc_lengths, conv_weight, conv_bias, rate, skip, clip_level
):
    seq_count = lax.axis_size("seq")
    tok_rows, hp_width = x_rows.shape
    heads = step.shape[1]
    owned = heads // seq_count
    width = hp_width // seq_count
    state2 = bc_rows.shape[1]
    rows = tok_rows * seq_count

    spare = jnp.zeros((tok_rows, LANES - heads - 1), BF16)
    aux = jnp.concatenate([bc_rows, step, route.astype(BF16), spare], axis=1)
    parts = 2 if width % (2 * LANES) == 0 and owned % 2 == 0 else 1
    plane = 4
    size = width // parts
    keep = rows if rows <= 2048 else 16
    flat = size % LANES == 0
    x_send = x_rows if flat else jnp.swapaxes(x_rows.reshape(tok_rows, seq_count, width), 0, 1)

    vmem = pl.BlockSpec(memory_space=pltpu.VMEM)
    dma = pltpu.SemaphoreType.DMA
    out = pl.pallas_call(
        functools.partial(kernel, owned, heads, parts, plane),
        out_shape=jax.ShapeDtypeStruct(x_send.shape, BF16),
        in_specs=[pl.BlockSpec(memory_space=pltpu.SMEM)] * 4 + [vmem] * 4,
        out_specs=vmem,
        scratch_shapes=[
            pltpu.VMEM((8, width), F32),
            pltpu.VMEM((8, state2), F32),
            pltpu.VMEM((1, LANES), F32),
            pltpu.VMEM((LANES, LANES), BF16),
            pltpu.VMEM((seq_count, tok_rows, aux.shape[1]), BF16),
            pltpu.VMEM((parts, seq_count, tok_rows, size), BF16),
            pltpu.VMEM((parts, seq_count, tok_rows, size), BF16),
            pltpu.VMEM((rows, LANES), F32),
            pltpu.VMEM((8, rows), F32),
            pltpu.VMEM((rows, LANES), F32),
            pltpu.VMEM((PAD + rows, state2), F32),
            pltpu.VMEM((PAD + rows, size), F32),
            pltpu.VMEM((rows, LANES), F32),
            pltpu.VMEM((rows, state2), BF16),
            pltpu.VMEM((owned, rows, CHUNK), BF16),
            pltpu.VMEM((rows, width), F32),
            pltpu.VMEM((rows, width), F32),
            pltpu.VMEM((rows // CHUNK, 8, width), F32),
            pltpu.VMEM((rows, size), BF16),
            pltpu.VMEM((state2 // 2, size), F32),
            pltpu.VMEM((keep, keep), BF16),
            pltpu.VMEM((keep, keep), BF16),
            dma((seq_count // plane,)),
            dma((seq_count,)),
            dma((seq_count // plane, 3)),
            dma((parts, seq_count)),
            dma((parts, seq_count)),
            dma((parts, seq_count)),
            dma((parts, seq_count)),
        ],
        compiler_params=pltpu.CompilerParams(
            vmem_limit_bytes=60 * 1024 * 1024, collective_id=0, has_side_effects=True
        ),
    )(doc_lengths, rate, skip, clip_level, x_send, aux, conv_weight, conv_bias[None, :])
    return out if flat else jnp.swapaxes(out, 0, 1).reshape(tok_rows, hp_width)


SUB = 256
SMALL = 16


def fast_conv(rows, taps, bias, off):
    size = off.shape[0]
    acc = bias + taps[0:1, :] * rows[PAD : PAD + size, :]
    for j in range(1, 4):
        back = rows[PAD - j : PAD - j + size, :]
        acc = acc + taps[j : j + 1, :] * jnp.where(off >= j, back, 0.0)
    half = 0.5 * acc
    return (half + half * jnp.tanh(half)).astype(BF16)


def fast_kernel(
    owned, parts, plane, docs_ref, rates, skips, clips, x_ref, bc_ref, step_ref, route_ref, weight_ref, bias_ref, out_ref,
    step_v, route_v, x_taps, bc_taps, bias_v, small_out, small_all, bc_all, x_all, sent, off_ref,
    sorter, unsorter, columns, dt_left, dt_right, places, ub, ux, lhs, b_flip, rise, fall, by_chunk, ys, state,
    load_sem, small_send, small_recv, gate_send, gate_recv, plane_send, x_send, x_recv, own_sem, out_send, out_recv,
):
    n, tok, state2 = bc_all.shape
    rows, size = ys.shape
    heads = step_v.shape[0]
    chunks = rows // CHUNK
    width = size * parts
    local = owned // parts
    me = lax.axis_index("seq")
    inside = lax.rem(me, plane)
    iota = functools.partial(lax.broadcasted_iota, jnp.int32)

    def remote(source, target, send, recv, peer):
        return pltpu.make_async_remote_copy(
            src_ref=source, dst_ref=target, send_sem=send, recv_sem=recv,
            device_id={"seq": peer}, device_id_type=pl.DeviceIdType.MESH,
        )

    def every(count, do, first=0):
        def turn(k, _):
            do(k)
            return 0

        lax.fori_loop(first, count, turn, 0)

    def tile(ref, part, owner):
        return ref.at[:, pl.ds(pl.multiple_of((owner * parts + part) * size, size), size)]

    barrier = pltpu.get_barrier_semaphore()

    def greet(k):
        pl.semaphore_signal(
            barrier, inc=1, device_id={"seq": lax.rem(me + k, n)}, device_id_type=pl.DeviceIdType.MESH
        )

    every(n, greet, 1)

    own = pl.ds(pl.multiple_of(me * width, width), width)
    shared_at = weight_ref.shape[1] - state2
    loads = [
        pltpu.make_async_copy(bc_ref, bc_all.at[me], load_sem.at[0]),
        pltpu.make_async_copy(step_ref, step_v, load_sem.at[1]),
        pltpu.make_async_copy(route_ref, route_v, load_sem.at[2]),
        pltpu.make_async_copy(weight_ref.at[:, own], x_taps, load_sem.at[3]),
        pltpu.make_async_copy(weight_ref.at[:, shared_at:], bc_taps, load_sem.at[4]),
        pltpu.make_async_copy(bias_ref, bias_v, load_sem.at[5]),
    ]
    for load in loads:
        load.start()

    loads[1].wait()
    loads[2].wait()
    wide_step = step_v[...].astype(F32)
    wide_route = jnp.broadcast_to(route_v[...].astype(F32), (8, tok))
    for p in range(n):
        mine = wide_step[p * owned : (p + 1) * owned, :]
        block = jnp.concatenate([mine, jnp.zeros((8 - owned, tok), F32), wide_route], axis=0)
        small_out[p] = block.astype(BF16)
    small_all[me] = small_out[me]
    loads[0].wait()

    pl.semaphore_wait(barrier, n - 1)

    low_plane = lax.rem(me // plane, 2)
    mate_turn, last_turn = 1 + 2 * low_plane, 3 - 2 * low_plane

    def far(step):
        owner = lax.rem(me + 2 * plane, n) if step == 2 else me
        peer = lax.rem(me + (2 if step == 0 else mate_turn) * plane, n)
        return remote(bc_all.at[owner], bc_all.at[owner], gate_send.at[step], gate_recv.at[owner], peer)

    def small_copy(k):
        peer = lax.rem(me + k, n)
        return remote(small_out.at[peer], small_all.at[me], small_send.at[k], small_recv.at[me], peer)

    def landed(ref, sems, slot):
        return remote(ref.at[slot], ref.at[slot], gate_send.at[0], sems.at[slot], slot)

    across = me - inside + lax.rem(inside + 2, plane)
    sibling = me + 1 - 2 * lax.rem(me, 2)

    def relay(k, hop):
        owner = lax.rem((across if hop == 2 else me) + k * plane, n)
        peer = across if hop == 0 else sibling
        return remote(bc_all.at[owner], bc_all.at[owner], plane_send.at[k, hop], gate_recv.at[owner], peer)

    def x_copy(part, peer):
        return remote(tile(x_ref, part, peer), x_all.at[part, me], x_send.at[part, peer], x_recv.at[part, me], peer)

    planes = n // plane
    half = planes // 2
    mine = me // plane

    def plane_at(i):
        turn = lax.rem(i, half)
        side = lax.rem(mine // half + 1 + i // half, 2)
        return side * half + lax.rem(lax.rem(mine, half) + turn + i // half, half)

    def own_copy(part):
        return pltpu.make_async_copy(tile(x_ref, part, me), x_all.at[part, me], own_sem.at[part])

    def start_at(moment):
        for part, turn, *span in SCHEDULE.get(moment, ()):
            begin, end = span or (0, plane)
            first = plane_at(jnp.int32(turn)) * plane

            def to_peer(j, part=part, first=first):
                peer = first + lax.rem(inside + 1 + j, plane)

                @pl.when(peer != me)
                def _():
                    x_copy(part, peer).start()

            every(end, to_peer, begin)

    every(n, lambda k: small_copy(k).start(), 1)
    far(0).start()
    relay(0, 0).start()
    far(1).start()
    relay(0, 1).start()
    start_at(0)
    for part in range(parts):
        own_copy(part).start()

    starts, total = [], jnp.int32(0)
    for k in range(docs_ref.shape[0]):
        starts.append(total)
        total = total + docs_ref[k]

    def begins(at):
        begin = jnp.zeros(at.shape, jnp.int32)
        for start in starts:
            begin = jnp.where(at >= start, start, begin)
        return begin

    low, high = iota((CHUNK, CHUNK), 0), iota((CHUNK, CHUNK), 1)

    def make_off(c):
        base = pl.multiple_of(c * CHUNK, CHUNK)
        at = low + base
        off_ref[pl.ds(base, CHUNK), :] = (at - begins(at)).astype(F32)

    every(chunks, make_off)

    def small_landed(k):
        landed(small_all, small_recv, lax.rem(me + k, n)).wait_recv()

    every(n, small_landed, 1)

    def find_places():
        number = iota((n, tok), 0).astype(F32)
        named = []
        for i in range(n):
            target = jnp.concatenate([small_all[i].astype(F32)[8:, :]] * (n // 8), axis=0)
            named.append(jnp.where(target == number, 1.0, 0.0))
        earlier = jnp.where(low < high, 1.0, 0.0).astype(BF16)
        right = jnp.concatenate([earlier, jnp.ones((tok, tok), BF16)], axis=1)
        found = dot(jnp.concatenate(named, axis=0).astype(BF16), right)
        before = jnp.zeros((n, tok), F32)
        ranks = []
        for i in range(n):
            here = found[i * n : (i + 1) * n, :]
            ranks.append(here[:, :tok] + before)
            before = before + here[:, tok:]
        base = jnp.zeros((n, tok), F32)
        for d in range(n - 1):
            base = base + jnp.where(number > d, before[d : d + 1, :], 0.0)
        all_places = []
        for i in range(n):
            place = jnp.sum(named[i] * (ranks[i] + base), axis=0, keepdims=True)
            places[i : i + 1, :] = place
            all_places.append(place)
            coarse = jnp.floor(place * (1.0 / CHUNK))
            fine = place - coarse * CHUNK
            lanes = slice(i * tok, (i + 1) * tok)
            steps = small_all[i].astype(F32)[0:8, :]
            split = [jnp.where(coarse == c, steps, 0.0) for c in range(chunks)]
            dt_left[:, lanes] = jnp.concatenate(split, axis=0).astype(BF16)
            dt_right[:, lanes] = jnp.where(low.astype(F32) == fine, 1.0, 0.0).astype(BF16)

    find_places()

    start_at(6)
    row16 = iota((SUB, tok), 0).astype(F32).astype(BF16)
    one, none = jnp.ones((), BF16), jnp.zeros((), BF16)

    def make_sorter(b):
        first = lax.convert_element_type(b * SUB, F32)
        for i in range(n):
            rel = places[i : i + 1, :] - first
            rel = jnp.where((rel >= 0.0) & (rel < SUB), rel, -1.0)
            rel = jnp.broadcast_to(rel, (SUB, tok)).astype(BF16)
            hit = jnp.where(row16 == rel, one, none)
            sorter[pl.ds(pl.multiple_of(b * SUB, SUB), SUB), i * tok : (i + 1) * tok] = hit

    every(rows // SUB, make_sorter)

    start_at(8)
    def forward(k):
        landed(bc_all, gate_recv, lax.rem(me + k * plane, n)).wait_recv()
        if isinstance(k, int):
            far(2).start()
        relay(k, 0).start()
        relay(k, 1).start()

    forward(2)
    forward(mate_turn)
    start_at(7)
    forward(last_turn)
    start_at(1)

    def decays():
        dts = dot_nt(dt_left[...], dt_right[...])
        lane = iota((8, CHUNK), 1)
        slot = iota((8, CHUNK), 0)
        rate = jnp.zeros((8, CHUNK), F32)
        for h in range(owned):
            rate = jnp.where(slot == h, rates[me * owned + h], rate)
        rate = jnp.concatenate([rate] * chunks, axis=0)
        upto = jnp.where(low <= high, 1.0, 0.0).astype(BF16)
        cum = -dot(dts.astype(BF16), upto) * rate
        last = jnp.broadcast_to(cum[:, CHUNK - 1 :], cum.shape)
        middle = 0.5 * last
        up = jnp.exp(cum - middle)
        down = jnp.exp(middle - cum) * dts
        gain = jnp.exp(middle)
        number = iota((8 * chunks, CHUNK), 0) // 8
        ends = number * CHUNK + CHUNK - 1
        goes_on = jnp.where(begins(ends) < number * CHUNK, 1.0, 0.0)
        carry = jnp.exp(last) * goes_on
        by_chunk[0] = up
        by_chunk[1] = down
        by_chunk[2] = gain
        by_chunk[3] = carry

    decays()

    head = iota((1, size), 1) // (size // local)

    def spread(columns, part):
        out = jnp.broadcast_to(columns[:, part * local : part * local + 1], (CHUNK, size))
        for h in range(1, local):
            at = part * local + h
            out = jnp.where(head == h, jnp.broadcast_to(columns[:, at : at + 1], (CHUNK, size)), out)
        return out

    def expand(part):
        pair = by_chunk[0].reshape(chunks, 8, CHUNK)[:, :4], by_chunk[1].reshape(chunks, 8, CHUNK)[:, :4]
        turned = jnp.concatenate(pair, axis=1).reshape(8 * chunks, CHUNK).T
        for c in range(chunks):
            at = slice(c * CHUNK, (c + 1) * CHUNK)
            rise[part, at, :] = spread(turned[:, 8 * c :], part)
            fall[part, at, :] = spread(turned[:, 8 * c + 4 :], part)

    expand(0)

    def crossed(k):
        landed(bc_all, gate_recv, lax.rem(across + k * plane, n)).wait_recv()
        relay(k, 2).start()

    for k in (0, 2, mate_turn, last_turn):
        crossed(k)

    start_at(2)

    block = plane * tok
    core = lax.rem(me, 2)
    ub[0:PAD, :] = jnp.zeros((PAD, state2), F32)

    def gather(b, side):
        first = pl.multiple_of(b * block, block)
        owners = [2 * i + side for i in range(n // 2)]
        lefts = [sorter[pl.ds(first, block), pl.ds(pl.multiple_of(o * tok, tok), tok)] for o in owners]
        here = dot(jnp.concatenate(lefts, axis=1), jnp.concatenate([bc_all[o] for o in owners], axis=0))
        at = pl.ds(pl.multiple_of(first + PAD, PAD), block)
        ub[at, :] = here if side is core else ub[at, :] + here

    every(rows // block, lambda b: gather(b, core))

    lane16 = [(iota((tok, LANES), 1) + j * LANES).astype(F32).astype(BF16) for j in range(SUB // LANES)]
    flipped = jnp.concatenate([places[...], jnp.zeros((tok - n, tok), F32)], axis=0).T
    flipped_coarse = jnp.floor(flipped * (1.0 / SUB))
    flipped_fine = flipped - flipped_coarse * SUB

    def make_columns():
        for i in range(n):
            at = slice(i * tok, (i + 1) * tok)
            columns[0, at, :] = jnp.broadcast_to(flipped_coarse[:, i : i + 1], (tok, LANES)).astype(BF16)
            columns[1, at, :] = jnp.broadcast_to(flipped_fine[:, i : i + 1], (tok, LANES)).astype(BF16)

    def make_unsorter(i):
        at = pl.ds(pl.multiple_of(i * tok, tok), tok)
        coarse, fine = columns[0, at, :], columns[1, at, :]
        for b in range(rows // SUB):
            rel = jnp.where(coarse == jnp.full((), b, BF16), fine, -one)
            for j in range(SUB // LANES):
                unsorter[at, b * SUB + j * LANES : b * SUB + (j + 1) * LANES] = jnp.where(lane16[j] == rel, one, none)

    start_at(9)
    make_columns()

    def rest(k):
        for hop in (0, 2):
            owner = sibling - lax.rem(sibling, plane) + lax.rem(lax.rem(sibling, plane) + hop, plane)
            landed(bc_all, gate_recv, lax.rem(owner + k * plane, n)).wait_recv()

    every(n // plane, rest)

    start_at(3)

    for load in loads[3:]:
        load.wait()
    ux[0:PAD, :] = jnp.zeros((PAD, size), F32)
    every(rows // block, lambda b: gather(b, 1 - core))
    start_at(4)

    gap = low - high

    def wide_bias(first, count):
        return jnp.concatenate([bias_v[pl.ds(first + i, 1), :] for i in range(count)], axis=1)

    def shared(c):
        base = pl.multiple_of(c * CHUNK, CHUNK)
        off = off_ref[pl.ds(base, CHUNK), :]
        off2 = jnp.concatenate([off] * (state2 // LANES), axis=1)
        bias = wide_bias(shared_at // LANES, state2 // LANES)
        act = fast_conv(ub[pl.ds(base, CHUNK + PAD), :], bc_taps[...], bias, off2)
        b_mat, c_mat = act[:, : state2 // 2], act[:, state2 // 2 :]
        scores = dot_nt(c_mat, b_mat)
        keep = (gap >= 0) & (gap.astype(F32) <= off)
        lhs[pl.ds(base, CHUNK), :CHUNK] = jnp.where(keep, scores, 0.0).astype(BF16)
        runs_in = jnp.where(off > low.astype(F32), c_mat.astype(F32), 0.0)
        lhs[pl.ds(base, CHUNK), CHUNK:] = runs_in.astype(BF16)
        runs_out = high[0:1, :].astype(F32) + off[CHUNK - 1 :, :] >= CHUNK - 1
        b_flip[pl.ds(base, CHUNK), :] = jnp.where(runs_out, b_mat.astype(F32).T, 0.0).astype(BF16)

    every(chunks // 4, lambda c: [shared(4 * c + i) for i in range(4)])
    start_at(5)

    def out_copy(part, owner):
        return remote(
            sent.at[part, owner], tile(out_ref, part, me), out_send.at[part, owner], out_recv.at[part, me], owner
        )

    def own_out(part):
        return pltpu.make_async_copy(sent.at[part, me], tile(out_ref, part, me), own_sem.at[parts + part])

    lane_head = iota((1, size), 1) // (size // local)

    def by_head(values):
        out = jnp.full((1, size), values[0], F32)
        for h in range(1, local):
            out = jnp.where(lane_head == h, values[h], out)
        return out

    for part in range(parts):

        def x_landed(k):
            source = lax.rem(me + k, n)
            slot = x_all.at[part, source]
            remote(slot, slot, gate_send.at[0], x_recv.at[part, source], source).wait_recv()

        if part > 0:
            expand(part)
        own_copy(part).wait()
        every(n, x_landed, 1)

        def gather_x(b):
            first = pl.multiple_of(b * block, block)
            here = dot(sorter[pl.ds(first, block), :], x_all[part].reshape(rows, size))
            ux[pl.ds(pl.multiple_of(first + PAD, PAD), block), :] = here

        every(rows // block, gather_x)
        state[...] = jnp.zeros_like(state)
        skip = by_head([skips[me * owned + part * local + h] for h in range(local)])
        level = by_head([clips[me * owned + part * local + h] for h in range(local)])

        def chunk(c):
            base = pl.multiple_of(c * CHUNK, CHUNK)
            at = pl.ds(base, CHUNK)
            bias = bias_v[pl.ds(me * parts + part, 1), :]
            taps = x_taps[:, part * size : (part + 1) * size]
            wide = fast_conv(ux[pl.ds(base, CHUNK + PAD), :], taps, bias, off_ref[at, :]).astype(F32)
            scaled = (wide * fall[part, at, :]).astype(BF16)
            at8 = pl.ds(pl.multiple_of(c * 8, 8), 8)
            gains, carries = by_chunk[2, at8, :], by_chunk[3, at8, :]
            gain = by_head([gains[part * local + h : part * local + h + 1, :] for h in range(local)])
            carry = by_head([carries[part * local + h : part * local + h + 1, :] for h in range(local)])
            old = state[...]
            right = jnp.concatenate([scaled, (gain * old).astype(BF16)], axis=0)
            y = skip * wide + rise[part, at, :] * dot(lhs[at, :], right)
            ys[at, :] = jnp.clip(y, -level, level).astype(BF16)
            state[...] = carry * old + gain * dot(b_flip[at, :], scaled)

        every(chunks // 4, lambda c: [chunk(4 * c + i) for i in range(4)])

        def scatter(i):
            b = plane_at(i)
            first = pl.multiple_of(b * block, block)
            if part == 0:
                every(plane, lambda j: make_unsorter(b * plane + j))
            back = dot(unsorter[pl.ds(first, block), :], ys[...]).astype(BF16)
            for j in range(block // tok):
                owner = b * (block // tok) + j
                sent[part, owner] = back[j * tok : (j + 1) * tok, :]

                @pl.when(owner != me)
                def _():
                    out_copy(part, owner).start()

        every(rows // block, scatter)
        own_out(part).start()

    def finish(k):
        source = lax.rem(me + k, n)
        for part in range(parts):
            slot = tile(out_ref, part, source)
            remote(slot, slot, gate_send.at[0], out_recv.at[part, source], source).wait_recv()
            out_copy(part, source).wait_send()
            x_copy(part, source).wait_send()
        small_copy(k).wait_send()

    every(n, finish, 1)
    for part in range(parts):
        own_out(part).wait()

    def finish_aux(k):
        for hop in range(3):
            relay(k, hop).wait_send()

    every(n // plane, finish_aux)
    for step in range(3):
        far(step).wait_send()


def fast_device(
    x_rows, bc_rows, step, route, doc_lengths, conv_weight, conv_bias, rate, skip, clip_level
):
    n = lax.axis_size("seq")
    tok, hp_width = x_rows.shape
    heads = step.shape[1]
    owned = heads // n
    width = hp_width // n
    state2 = bc_rows.shape[1]
    rows = tok * n
    parts = width // LANES
    size = LANES
    plane = 4
    chunks = rows // CHUNK
    bias = conv_bias.reshape(conv_bias.shape[0] // LANES, LANES)

    hbm = pl.BlockSpec(memory_space=pl.ANY)
    dma = pltpu.SemaphoreType.DMA
    return pl.pallas_call(
        functools.partial(fast_kernel, owned, parts, plane),
        out_shape=jax.ShapeDtypeStruct(x_rows.shape, BF16),
        in_specs=[pl.BlockSpec(memory_space=pltpu.SMEM)] * 4 + [hbm] * 6,
        out_specs=OUT_SPEC,
        scratch_shapes=[
            pltpu.VMEM((heads, tok), BF16),
            pltpu.VMEM((1, tok), jnp.int32),
            pltpu.VMEM((4, width), F32),
            pltpu.VMEM((4, state2), F32),
            pltpu.VMEM(bias.shape, F32),
            pltpu.VMEM((n, SMALL, tok), BF16),
            pltpu.VMEM((n, SMALL, tok), BF16),
            pltpu.VMEM((n, tok, state2), BF16),
            pltpu.VMEM((parts, n, tok, size), BF16),
            pltpu.VMEM((parts, n, tok, size), BF16),
            pltpu.VMEM((rows, LANES), F32),
            pltpu.VMEM((rows, rows), BF16),
            pltpu.VMEM((rows, rows), BF16),
            pltpu.VMEM((2, rows, LANES), BF16),
            pltpu.VMEM((8 * chunks, rows), BF16),
            pltpu.VMEM((CHUNK, rows), BF16),
            pltpu.VMEM((n, tok), F32),
            pltpu.VMEM((PAD + rows, state2), F32),
            pltpu.VMEM((PAD + rows, size), F32),
            pltpu.VMEM((rows, 2 * CHUNK), BF16),
            pltpu.VMEM((rows, CHUNK), BF16),
            pltpu.VMEM((parts, rows, size), F32),
            pltpu.VMEM((parts, rows, size), F32),
            pltpu.VMEM((4, 8 * chunks, CHUNK), F32),
            pltpu.VMEM((rows, size), BF16),
            pltpu.VMEM((state2 // 2, size), F32),
            dma((6,)),
            dma((n,)),
            dma((n,)),
            dma((n // plane,)),
            dma((n,)),
            dma((n // plane, 3)),
            dma((parts, n)),
            dma((parts, n)),
            dma((2 * parts,)),
            dma((parts, n)),
            dma((parts, n)),
        ],
        compiler_params=pltpu.CompilerParams(
            vmem_limit_bytes=48 * 1024 * 1024, collective_id=1, has_side_effects=True
        ),
    )(*[pltpu.with_memory_space_constraint(a, pltpu.HBM) for a in (
        doc_lengths, rate, skip, clip_level, x_rows, bc_rows, step.T, route.T, conv_weight, bias
    )])


def fits_fast(n, x_shape, heads, state2):
    width = x_shape[1] // n
    owned = heads // n
    return (
        n == 16 and n * x_shape[0] <= 2048 and x_shape[0] == LANES and width % LANES == 0 and state2 == 2 * CHUNK
        and owned == 4 and owned % (width // LANES) == 0 and 8 * n * LANES // CHUNK <= CHUNK
    )


def solution(mesh):
    placed = (
        P(("groups", "seq"), None),
        P(("groups", "seq"), None),
        P(("groups", "seq"), None),
        P(("groups", "seq"), None),
        P("groups"),
        P(),
        P(),
        P(),
        P(),
        P(),
    )

    def run(*arrays):
        x_rows, bc_rows, step = arrays[:3]
        fast = fits_fast(lax.axis_size("seq"), x_rows.shape, step.shape[1], bc_rows.shape[1])
        return (fast_device if fast else per_device)(*arrays)

    return jax.shard_map(
        run,
        mesh=mesh,
        in_specs=placed,
        out_specs=P(("groups", "seq"), None),
        check_vma=False,
    )
```
